32 devices in a mesh: kind: 2 (over core), dp: 8 (over z, x), inner: 2 (over y).
Axes of the slice: x: 2, y: 2, z: 4, core: 2. Of those that a mesh axis runs over, the one named last changes fastest.
Arguments:
- layer_input: bfloat16 [16, 1024, 512], P('dp', 'inner'), may hold values from -6 to 6
- output_grad: bfloat16 [16, 1024, 512], P('dp'), may hold values from -6 to 6
- document_ids: int32 [16, 1024], P('dp'), may hold values from 0 to 8, as said below
- mamba_gain: float32 [512], replicated, may hold values from 0.1 to 1.9
- in_proj: bfloat16 [512, 2048], replicated, may hold values from -0.25 to 0.25
- conv_weight: float32 [1024, 4], replicated, may hold values from -3 to 3
- conv_bias: float32 [1024], replicated, may hold values from -0.5 to 0.5
- state_proj: bfloat16 [1024, 64], replicated, may hold values from -0.1875 to 0.1875
- step_proj: bfloat16 [32, 1024], replicated, may hold values from -1 to 1
- step_bias: float32 [1024], replicated, may hold values from -7 to -2.3
- decay_log: float32 [1024, 16], replicated, may hold values from -4 to 2.5
- skip_gain: float32 [1024], replicated, may hold values from 0.5 to 1.5
- out_proj: bfloat16 [1024, 512], replicated, may hold values from -0.1875 to 0.1875
- attn_gain: float32 [512], replicated, may hold values from 0.1 to 1.9
- query_proj: bfloat16 [512, 512], replicated, may hold values from -0.25 to 0.25
- key_proj: bfloat16 [512, 512], replicated, may hold values from -0.25 to 0.25
- value_proj: bfloat16 [512, 512], replicated, may hold values from -0.25 to 0.25
- mixed_proj: bfloat16 [512, 512], replicated, may hold values from -0.75 to 0.75
Outputs:
- results: float32 [2, 16, 1024, 512], P('kind', 'dp', 'inner')
- grad_mamba_gain: float32 [512], replicated
- grad_in_proj: float32 [512, 2048], replicated
- grad_conv_weight: float32 [1024, 4], replicated
- grad_conv_bias: float32 [1024], replicated
- grad_state_proj: float32 [1024, 64], replicated
- grad_step_proj: float32 [32, 1024], replicated
- grad_step_bias: float32 [1024], replicated
- grad_decay_log: float32 [1024, 16], replicated
- grad_skip_gain: float32 [1024], replicated
- grad_out_proj: float32 [1024, 512], replicated
- grad_attn_gain: float32 [512], replicated
- grad_query: float32 [512, 512], replicated
- grad_key: float32 [512, 512], replicated
- grad_value: float32 [512, 512], replicated
- grad_mixed: float32 [512, 512], replicated
The draws below stay inside these ranges and needn't reach their ends.
Inputs may be any that keep to these rules, and one draw needn't show every extreme that they name: `document_ids`: in each row the ids start at 0 and rise by one at each document's first token; every row holds exactly 9 documents, 4 of them starting before position 256 and 4 after position 768.
All inputs are finite; a program needn't handle non-finite values.
Results may differ from the reference program's by a relative error of at most 0.013.
Values may be sent and summed in bfloat16 or wider, within the bound.
A program may use at most 384 MiB of HBM per device.

```python
import jax
import jax.numpy as jnp
from jax import lax

D = 512
DI = 1024
DS = 16
DR = 32
CONV = 4
HEADS = 8
HEAD_DIM = 64
ROW_LEN = 1024
SCAN_BLOCK = 64
ATT_BLOCK = 512
ROWS = 16


def draw_document_ids(key, part):
    key = jax.random.fold_in(key, 7)
    quarter = ROW_LEN // 4
    row_keys = jax.random.split(key, ROWS)

    def one_row(row_key):
        early_key, late_key = jax.random.split(row_key)
        early = 1 + jax.random.permutation(early_key, quarter - 1)[:4]
        late = 3 * quarter + 1 + jax.random.permutation(late_key, quarter - 1)[:4]
        starts = jnp.concatenate([early, late]).astype(jnp.int32)
        begins = jnp.zeros((ROW_LEN,), jnp.int32).at[starts].set(1)
        return jnp.cumsum(begins).astype(jnp.int32)
    return jax.vmap(one_row)(row_keys)


def steps_of(rng, shape, cuts, least, high):
    loudness, own = 1.0, jax.random.fold_in(rng, 6)
    for axis_at, shards_of in cuts:
        draws = jnp.exp(jax.random.uniform(jax.random.fold_in(own, axis_at), (shards_of,), jnp.float32, least / len(cuts), high / len(cuts)))
        loudness = loudness * jnp.repeat(draws, shape[axis_at] // shards_of).reshape([-1 if axis == axis_at else 1 for axis in range(len(shape))])
    return loudness


def bell_draw(key, extent, scale, reach, cuts=(), kind=jnp.bfloat16):
    result = scale * jax.random.normal(key, extent, jnp.float32)
    if cuts:
        result = result * steps_of(key, extent, cuts, -0.22, 0.18)
    return jnp.clip(result, -reach, reach).astype(kind)


def setup_inputs(seed: int = 0) -> dict:
    streams_of = jax.random.split(jax.random.key(seed), 19)
    return {
        "layer_input": bell_draw(streams_of[0], (ROWS, ROW_LEN, D), 1.0, 6.0, ((0, 8), (1, 2))),
        "output_grad": bell_draw(streams_of[1], (ROWS, ROW_LEN, D), 1.0, 6.0, ((0, 8),)),
        "document_ids": draw_document_ids(jax.random.fold_in(streams_of[18], 71), 0),
        "mamba_gain": jnp.clip(1.0 + 0.18 * jax.random.normal(streams_of[3], (D,), jnp.float32), 0.1, 1.9),
        "in_proj": bell_draw(streams_of[4], (D, 2 * DI), D ** -0.5, 0.25),
        "conv_weight": bell_draw(streams_of[5], (DI, CONV), CONV ** -0.5, 3.0, (), jnp.float32),
        "conv_bias": jnp.clip(jax.random.uniform(streams_of[6], (DI,), jnp.float32, -0.5, 0.5), -0.5, 0.5),
        "state_proj": bell_draw(streams_of[7], (DI, DR + 2 * DS), DI ** -0.5, 0.1875),
        "step_proj": bell_draw(streams_of[8], (DR, DI), DR ** -0.5, 1.0),
        "step_bias": jnp.clip(jax.random.uniform(streams_of[9], (DI,), jnp.float32, -7.0, -2.3), -7.0, -2.3),
        "decay_log": jnp.clip(jax.random.uniform(streams_of[10], (DI, DS), jnp.float32, -4.0, 2.5), -4.0, 2.5),
        "skip_gain": jnp.clip(jax.random.uniform(streams_of[11], (DI,), jnp.float32, 0.5, 1.5), 0.5, 1.5),
        "out_proj": bell_draw(streams_of[12], (DI, D), DI ** -0.5, 0.1875),
        "attn_gain": jnp.clip(1.0 + 0.18 * jax.random.normal(streams_of[13], (D,), jnp.float32), 0.1, 1.9),
        "query_proj": bell_draw(streams_of[14], (D, D), D ** -0.5, 0.25),
        "key_proj": bell_draw(streams_of[15], (D, D), D ** -0.5, 0.25),
        "value_proj": bell_draw(streams_of[16], (D, D), D ** -0.5, 0.25),
        "mixed_proj": bell_draw(streams_of[17], (D, D), (D // 8) ** -0.5, 0.75),
    }


EPS = 1e-05
NEG = -1e+30
HIGH = lax.Precision.HIGHEST

@jax.custom_vjp
def low(v):
    return lax.optimization_barrier(v.astype(jnp.bfloat16)).astype(jnp.float32)

@jax.custom_vjp
def low_back(v):
    return v

def low_keep(v):
    return (low(v), None)

def low_pass(kept, grad):
    return (grad,)

def back_keep(v):
    return (v, None)

def back_low(kept, grad):
    return (low(grad),)
low.defvjp(low_keep, low_pass)
low_back.defvjp(back_keep, back_low)

def selective(step_size, conv_act, in_coef, out_coef, same_doc, decay_neg):
    group_count = step_size.shape[0]

    def time_major(tensor):
        moved = jnp.swapaxes(tensor, 0, 1)
        return moved.reshape((ROW_LEN // SCAN_BLOCK, SCAN_BLOCK) + moved.shape[1:])

    def advance(carried, inputs):
        step_now, act_now, in_now, out_now, same_now = inputs
        decay_now = jnp.exp(step_now[:, None, :] * decay_neg) * same_now[:, None, None]
        carried = decay_now * carried + (step_now * act_now)[:, None, :] * in_now[:, :, None]
        return (carried, lax.optimization_barrier(jnp.sum(out_now[:, :, None] * carried, axis=1)))

    def block_run(carried, inputs):
        return lax.scan(advance, carried, inputs)
    initial = jnp.zeros((group_count, DS, DI), jnp.float32)
    _, outputs = lax.scan(jax.checkpoint(block_run), initial, (time_major(step_size), time_major(conv_act), time_major(in_coef), time_major(out_coef), time_major(same_doc)))
    outputs = outputs.reshape((ROW_LEN,) + outputs.shape[2:])
    return jnp.swapaxes(outputs, 0, 1)

def mamba_rows(u_rows, ids_rows, mamba_gain, in_proj, conv_weight, conv_bias, state_proj, step_proj, step_bias, decay_log, skip_gain, out_proj):
    group_count = u_rows.shape[0]
    factor = lax.rsqrt(lax.optimization_barrier(jnp.mean(u_rows * u_rows, axis=-1, keepdims=True)) + EPS)
    normed = low(u_rows * factor * mamba_gain)
    mixed_in = low_back(jnp.einsum('gtd,de->gte', normed, in_proj, precision=HIGH))
    conv_in = mixed_in[..., :DI]
    gate_z = mixed_in[..., DI:]
    padded = jnp.pad(conv_in, ((0, 0), (CONV - 1, 0), (0, 0)))
    padded_ids = jnp.concatenate([jnp.full((group_count, CONV - 1), -1, jnp.int32), ids_rows], axis=1)
    conv_pre = conv_bias + jnp.zeros_like(conv_in)
    for offset in range(CONV):
        match_doc = (padded_ids[:, offset:offset + ROW_LEN] == ids_rows).astype(jnp.float32)[..., None]
        conv_pre = conv_pre + conv_weight[:, offset] * padded[:, offset:offset + ROW_LEN] * match_doc
    conv_act = jax.nn.silu(conv_pre)
    coef_all = low_back(jnp.einsum('gtc,ce->gte', low(conv_act), state_proj, precision=HIGH))
    step_pre = low_back(jnp.einsum('gtk,kc->gtc', low(coef_all[..., :DR]), step_proj, precision=HIGH)) + step_bias
    step_size = jax.nn.softplus(step_pre)
    in_coef = coef_all[..., DR:DR + DS]
    out_coef = coef_all[..., DR + DS:]
    same_doc = (padded_ids[:, CONV - 2:CONV - 2 + ROW_LEN] == ids_rows).astype(jnp.float32)
    decay_neg = -jnp.exp(decay_log).T
    scan_out = selective(step_size, conv_act, in_coef, out_coef, same_doc, decay_neg) + skip_gain * conv_act
    gated = low(scan_out * jax.nn.silu(gate_z))
    branch = low_back(jnp.einsum('gtc,cd->gtd', gated, out_proj, precision=HIGH))
    return u_rows + branch

def attention_rows(middle, ids_rows, attn_gain, query_proj, key_proj, value_proj, mixed_proj):
    group_count = middle.shape[0]
    factor = lax.rsqrt(lax.optimization_barrier(jnp.mean(middle * middle, axis=-1, keepdims=True)) + EPS)
    normed = low(middle * factor * attn_gain)

    def project(weight):
        projected = low(low_back(jnp.einsum('gtd,de->gte', normed, weight, precision=HIGH)))
        return projected.reshape(group_count, ROW_LEN, HEADS, HEAD_DIM)
    queries = project(query_proj)
    key_rows = project(key_proj)
    values = project(value_proj)
    positions = jnp.arange(ROW_LEN, dtype=jnp.int32)

    def block_at(block_first):
        query_blk = lax.dynamic_slice_in_dim(queries, block_first, ATT_BLOCK, 1)
        ids_blk = lax.dynamic_slice_in_dim(ids_rows, block_first, ATT_BLOCK, 1)
        pos_blk = block_first + jnp.arange(ATT_BLOCK, dtype=jnp.int32)
        allowed = (pos_blk[:, None] >= positions[None, :])[None, None] & (ids_blk[:, None, :, None] == ids_rows[:, None, None, :])
        scores = low_back(jnp.einsum('gqhe,gkhe->ghqk', query_blk, key_rows, precision=HIGH) * HEAD_DIM ** (-0.5))
        scores = jnp.where(allowed, scores, NEG)
        attn_prob = jax.nn.softmax(scores, axis=-1)
        return jnp.einsum('ghqk,gkhe->gqhe', low(attn_prob), values, precision=HIGH)
    firsts = jnp.arange(ROW_LEN // ATT_BLOCK, dtype=jnp.int32) * ATT_BLOCK
    outputs = lax.map(jax.checkpoint(block_at), firsts)
    heads_out = jnp.swapaxes(outputs, 0, 1).reshape(group_count, ROW_LEN, HEADS * HEAD_DIM)
    heads_out = low(low_back(heads_out))
    branch = low_back(jnp.einsum('gte,ed->gtd', heads_out, mixed_proj, precision=HIGH))
    return middle + branch

def reference(layer_input, output_grad, document_ids, mamba_gain, in_proj, conv_weight, conv_bias, state_proj, step_proj, step_bias, decay_log, skip_gain, out_proj, attn_gain, query_proj, key_proj, value_proj, mixed_proj):
    weights_all = tuple((tensor.astype(jnp.float32) for tensor in (mamba_gain, in_proj, conv_weight, conv_bias, state_proj, step_proj, step_bias, decay_log, skip_gain, out_proj, attn_gain, query_proj, key_proj, value_proj, mixed_proj)))
    grouped_ids = document_ids.reshape(-1, 2, ROW_LEN)

    def forward(layer, *weights):

        def group_run(grouped):
            rows_in, ids_in = grouped
            middle = mamba_rows(rows_in, ids_in, *weights[:10])
            return attention_rows(middle, ids_in, *weights[10:])
        outputs = lax.map(jax.checkpoint(group_run), (layer.reshape(-1, 2, ROW_LEN, D), grouped_ids))
        return outputs.reshape(layer.shape)
    layer_out, pullback = jax.vjp(forward, layer_input.astype(jnp.float32), *weights_all)
    gradients = pullback(output_grad.astype(jnp.float32))
    results = jnp.stack([gradients[0], layer_out])
    return (results, gradients[1], gradients[2], gradients[3], gradients[4], gradients[5], gradients[6], gradients[7], gradients[8], gradients[9], gradients[10], gradients[11], gradients[12], gradients[13], gradients[14], gradients[15])
```

```python
import functools

import jax
import jax.numpy as jnp
from jax import lax
from jax.experimental import pallas as pl
from jax.experimental.pallas import tpu as pltpu
from jax.sharding import PartitionSpec as P

HEAD_DIM = 64
EPS = 1e-05
NEG = -1e30
FAR = 1e30
CHUNK = 16
STRETCH = 8
ROWS_STEP = 256
QUERY_BLOCK = 256
KEY_TILE = 128
VMEM_BYTES = 58 * 1024 * 1024
F32 = jnp.float32
BF16 = jnp.bfloat16


def dot_nn(a, b):
    return lax.dot_general(a, b, (((1,), (0,)), ((), ())), preferred_element_type=F32)


def dot_nt(a, b):
    return lax.dot_general(a, b, (((1,), (1,)), ((), ())), preferred_element_type=F32)


def dot_tn(a, b):
    return lax.dot_general(a, b, (((0,), (0,)), ((), ())), preferred_element_type=F32)


def silu_slope(tensor):
    sigma = jax.nn.sigmoid(tensor)
    return sigma * (1.0 + tensor * (1.0 - sigma))


def rms_scale(tensor):
    return lax.rsqrt(jnp.mean(tensor * tensor, axis=-1, keepdims=True) + EPS)


def softplus(tensor):
    return jnp.maximum(tensor, 0.0) + jnp.log1p(jnp.exp(-jnp.abs(tensor)))


def rms_back(tensor, factor, gain_vec, gradient):
    weighted = gradient * gain_vec
    spread = jnp.mean(weighted * tensor, axis=-1, keepdims=True)
    return factor * weighted - tensor * (factor * factor * factor) * spread


def spread(ref, value):
    for c in range(ref.shape[0]):
        ref[c] = value[:, c * 128 : (c + 1) * 128]


def row_of(ref, c, row, states):
    part = ref[c, pl.ds(row, 8, stride=0), :]
    return jnp.concatenate([part] * (states // 8), axis=0)


def column_of(tile, at):
    return jnp.broadcast_to(tile[:, at : at + 1], tile.shape)


def own_token(chunk, states):
    at = lax.broadcasted_iota(jnp.int32, (chunk, chunk * states), 0)
    of = lax.broadcasted_iota(jnp.int32, (chunk, chunk * states), 1) // states
    return at == of


def state_picks(chunk, states):
    at = lax.broadcasted_iota(jnp.int32, (states, chunk * states), 0)
    of = lax.rem(lax.broadcasted_iota(jnp.int32, (states, chunk * states), 1), states)
    return (at == of).astype(F32).astype(BF16)


def remote(src, dst, sems, number, to):
    return pltpu.make_async_remote_copy(
        src_ref=src, dst_ref=dst, send_sem=sems[0].at[number], recv_sem=sems[1].at[number],
        device_id=to, device_id_type=pl.DeviceIdType.MESH,
    )


def call(body, sel, steps, ins, outs, scratch, flops, name):
    bytes_all = sum(a.size * a.dtype.itemsize for a, _, _ in ins)
    return pl.pallas_call(
        body,
        grid_spec=pltpu.PrefetchScalarGridSpec(
            num_scalar_prefetch=1,
            grid=(steps,),
            in_specs=[pl.BlockSpec(block, at) for _, block, at in ins],
            out_specs=[pl.BlockSpec(block, at) for _, _, block, at in outs],
            scratch_shapes=scratch,
        ),
        out_shape=[jax.ShapeDtypeStruct(shape, dtype) for shape, dtype, _, _ in outs],
        compiler_params=pltpu.CompilerParams(
            dimension_semantics=("arbitrary",), vmem_limit_bytes=VMEM_BYTES
        ),
        cost_estimate=pl.CostEstimate(flops=flops, bytes_accessed=bytes_all, transcendentals=0),
        name=name,
    )(sel, *[a for a, _, _ in ins])


def whole(shape):
    zeros = (0,) * len(shape)
    return (shape, lambda i, sel: zeros)


def scan_block(
    coef, pre, gate, flags, step_w, step_b, decay_t, skip, out_w,
    step_o, scan_o, gated_o, starts_o, branch_o, spare,
):
    state, stepd, drive, ys, blocked, h_low = spare
    block, width = pre.shape
    states = decay_t.shape[0]
    rank = step_w.shape[0]
    tiles = width // 128

    step_pre = dot_tn(coef[:rank, :].astype(BF16), step_w[...]) + step_b[...]
    step_o[...] = step_pre
    step = softplus(step_pre)
    act = pre[...] * jax.nn.sigmoid(pre[...])
    spread(drive, step * act)
    spread(stepd, jnp.where(flags[:, 1:2] > 0.0, step, FAR))
    neg = -jnp.exp(decay_t[...])
    neg_of = [neg[:, c * 128 : (c + 1) * 128] for c in range(tiles)]
    own_all = jnp.concatenate([own_token(CHUNK, states)] * (block // CHUNK), axis=0)
    blocked[...] = jnp.where(
        own_all, dot_tn(coef[rank + states :, :].astype(BF16), state_picks(CHUNK, states)), 0.0
    ).astype(BF16)

    def one_chunk(i, h, h_s):
        here = pl.ds(pl.multiple_of(i * CHUNK, CHUNK), CHUNK)
        tile = coef[rank : rank + states, pl.ds(pl.multiple_of((i // 8) * 128, 128), 128)]
        tile = pltpu.roll(tile, lax.rem(128 - lax.rem(i, 8) * CHUNK, 128), 1)
        for c in range(tiles):
            starts_o[here, c * 128 : (c + 1) * 128] = h[c]
        for at in range(CHUNK):
            row = i * CHUNK + at
            write = column_of(tile, at)
            for c in range(tiles):
                decay = jnp.exp(neg_of[c] * row_of(stepd, c, row, states))
                h[c] = decay * h[c] + row_of(drive, c, row, states) * write
                h_s[at * states : (at + 1) * states, c * 128 : (c + 1) * 128] = h[c].astype(BF16)
        return h

    def stretch(number, carried):
        def pair(step_no, carried):
            h = list(carried)
            for sub in range(2):
                at = 2 * step_no + sub
                spot = h_low.at[pl.ds(pl.multiple_of(at * CHUNK * states, CHUNK * states), CHUNK * states)]
                h = one_chunk(number * STRETCH + at, h, spot)
            return tuple(h)

        carried = lax.fori_loop(0, STRETCH // 2, pair, carried)
        for at in range(STRETCH):
            here = pl.ds(pl.multiple_of((number * STRETCH + at) * CHUNK, CHUNK), CHUNK)
            spot = slice(at * CHUNK * states, (at + 1) * CHUNK * states)
            ys[here, :] = dot_nn(blocked[here, :], h_low[spot, :])
        return carried

    begin = tuple(state[:, c * 128 : (c + 1) * 128] for c in range(tiles))
    for c, last in enumerate(lax.fori_loop(0, block // (STRETCH * CHUNK), stretch, begin)):
        state[:, c * 128 : (c + 1) * 128] = last
    scan_out = ys[...] + skip[...] * act
    scan_o[...] = scan_out
    z = gate[...]
    gated = (scan_out * (z * jax.nn.sigmoid(z))).astype(BF16)
    gated_o[...] = gated
    branch_o[...] = dot_nn(gated, out_w[...]).astype(BF16)


def front_kernel(
    flags, gain, layer_all, weights_all,
    x_o, normed_o, conv_o, pre_o, gate_o, coef_o, step_o, scan_o, gated_o, starts_o, branch_o, branch_other_o,
    x, normed, ext, pre, gate, coef, coef_got, coef_sum, step_pre, scan_out, gated, starts, branch,
    branch_got, weights, scan_spare, load_sems, x_sems, coef_sems, branch_sems, store_sems, late_sems,
):
    length, width = x.shape
    blocks = length // ROWS_STEP
    core, row = lax.axis_index("kind"), lax.axis_index("inner")
    other_core, other_row = {"kind": 1 - core}, {"inner": 1 - row}
    w_conv, w_gate, state_w, step_w, decay_t, skip, taps, conv_b, step_b, out_w = weights
    in_all, state_all, step_all, decay_all, skip_all, taps_all, conv_b_all, step_b_all, out_all = weights_all
    channels = w_conv.shape[1]

    def part_of(number):
        return pl.ds(pl.multiple_of(number * channels, 128), channels)

    def rows_at(b):
        return pl.ds(pl.multiple_of(b * ROWS_STEP, ROWS_STEP), ROWS_STEP)

    mine = part_of(core)
    loads = [
        pltpu.make_async_copy(source, target, load_sems.at[i])
        for i, (source, target) in enumerate((
            (layer_all.at[row], x.at[pl.ds(pl.multiple_of(row * (length // 2), 256), length // 2)]),
            (in_all.at[:, mine], w_conv), (in_all.at[:, part_of(2 + core)], w_gate),
            (state_all.at[:, mine], state_w), (step_all.at[:, mine], step_w),
            (decay_all.at[:, mine], decay_t), (skip_all.at[:, mine], skip), (taps_all.at[:, mine], taps),
            (conv_b_all.at[:, mine], conv_b), (step_b_all.at[:, mine], step_b), (out_all.at[mine], out_w),
        ))
    ]
    barrier = pltpu.get_barrier_semaphore()
    for device in (other_core, other_row):
        pl.semaphore_signal(barrier, inc=1, device_id=device, device_id_type=pl.DeviceIdType.MESH)
    pl.semaphore_wait(barrier, 2)
    sent = remote(
        layer_all.at[1 - row, rows_at(core)], x.at[rows_at(row * (blocks // 2) + core)], x_sems, 0, other_row
    )
    sent.start()
    for load in loads:
        load.start()
    for load in loads:
        load.wait()
    ext[0:8, :] = jnp.zeros((8, channels), F32)
    scan_spare[0][...] = jnp.zeros_like(scan_spare[0])

    results = (
        (x, x_o), (normed, normed_o), (gate, gate_o), (pre, pre_o), (step_pre, step_o),
        (scan_out, scan_o), (gated, gated_o), (starts, starts_o), (branch, branch_o),
    )

    def stores(b, numbers=range(len(results))):
        rows = rows_at(b)
        return [
            pltpu.make_async_copy(results[i][0].at[rows], results[i][1].at[rows], store_sems.at[i, b])
            for i in numbers
        ]

    def project(b):
        rows = rows_at(b)
        u = x[rows, :].astype(F32)
        low = (u * rms_scale(u) * gain[...]).astype(BF16)
        normed[rows, :] = low
        ext[pl.ds(pl.multiple_of(b * ROWS_STEP + 8, 8), ROWS_STEP), :] = dot_nn(low, w_conv[...])
        gate[rows, :] = dot_nn(low, w_gate[...])
        for store in stores(b, range(3)):
            store.start()

    first_other = (1 - row) * (blocks // 2)
    project(row * (blocks // 2))
    project(row * (blocks // 2) + 1)
    sent.wait()
    fetched = x.at[rows_at(first_other + core)]
    passed = remote(fetched, fetched, x_sems, 1, other_core)
    passed.start()
    project(first_other + core)
    passed.wait()
    project(first_other + 1 - core)
    store_conv = pltpu.make_async_copy(ext.at[pl.ds(8, length)], conv_o, late_sems.at[0])
    store_conv.start()

    def coef_copy(b):
        return remote(coef.at[b], coef_got.at[b], coef_sems, b, other_core)

    def branch_copy(b):
        rows = rows_at(b)
        return remote(branch.at[rows], branch_got.at[rows], branch_sems, b, other_core)

    for b in range(blocks):
        rows = slice(b * ROWS_STEP, (b + 1) * ROWS_STEP)
        total = conv_b[...] + taps[3:4, :] * ext[8 + b * ROWS_STEP : 8 + (b + 1) * ROWS_STEP, :]
        for j in range(1, 4):
            moved = ext[8 - j + b * ROWS_STEP : 8 - j + (b + 1) * ROWS_STEP, :]
            total = total + taps[3 - j : 4 - j, :] * jnp.where(flags[rows, j : j + 1] > 0.0, moved, 0.0)
        pre[rows, :] = total
        coef[b] = dot_nt(state_w[...], (total * jax.nn.sigmoid(total)).astype(BF16))
        coef_copy(b).start()
        stores(b, [3])[0].start()

    def scan(b, unused):
        rows = rows_at(b)
        coef_copy(b).wait()
        coef_sum[b] = coef[b] + coef_got[b]
        scan_block(
            coef_sum.at[b], pre.at[rows], gate.at[rows], flags.at[rows], step_w, step_b, decay_t, skip, out_w,
            step_pre.at[rows], scan_out.at[rows], gated.at[rows], starts.at[rows], branch.at[rows],
            scan_spare,
        )
        branch_copy(b).start()
        for store in stores(b, range(4, len(results))):
            store.start()
        return unused

    lax.fori_loop(0, blocks, scan, 0)
    store_coef = pltpu.make_async_copy(coef_sum, coef_o, late_sems.at[1])
    store_coef.start()
    for b in range(blocks):
        branch_copy(b).wait()
    store_other = pltpu.make_async_copy(branch_got, branch_other_o, late_sems.at[2])
    store_other.start()
    for copy in (store_conv, store_coef, store_other):
        copy.wait()
    for b in range(blocks):
        for store in stores(b):
            store.wait()


def middle_kernel(
    x, part_a, part_b, first, gain, grads, gated_all, gate_all, scan_all, normed_all, weights_all,
    base_o, scan_grad_o, back_o, pack_o, gain_grad_o,
    grad, gated, gate, scan_out, normed_a, wq, wk, wv, wm, out_w, w_gate,
    normed, q_t, q_n, k_n, v_n, k_t, v_t, g_n, g_t, o_t, dq_n, dk, dv, bias, expo, prob_grad, prob_low,
    score_low,
    dq_low, dk_low, dv_low, branch, branch_got, back, back_got, base, scan_grad, gate_back, gout, ggate,
    pack, load_sems, pass_sems, store_sems,
):
    length, width = x.shape
    core, row = lax.axis_index("kind"), lax.axis_index("inner")
    other_core = {"kind": 1 - core}
    head_cols, channels = wq.shape[1], out_w.shape[0]

    def part_of(size):
        return pl.ds(pl.multiple_of(core * size, 128), size)

    query_all, key_all, value_all, mixed_all, out_all, in_all = weights_all
    gate_cols = pl.ds(pl.multiple_of((2 + core) * channels, 128), channels)
    loads = [
        pltpu.make_async_copy(source, target, load_sems.at[i])
        for i, (source, target) in enumerate((
            (query_all.at[:, part_of(head_cols)], wq), (key_all.at[:, part_of(head_cols)], wk),
            (value_all.at[:, part_of(head_cols)], wv), (grads.at[row], grad),
            (mixed_all.at[part_of(head_cols)], wm), (gated_all, gated), (gate_all, gate),
            (scan_all, scan_out), (normed_all, normed_a), (out_all.at[part_of(channels)], out_w),
            (in_all.at[:, gate_cols], w_gate),
        ))
    ]
    for load in loads:
        load.start()
    barrier = pltpu.get_barrier_semaphore()
    pl.semaphore_signal(barrier, inc=1, device_id=other_core, device_id_type=pl.DeviceIdType.MESH)
    pl.semaphore_wait(barrier, 1)
    for load in loads[:5]:
        load.wait()

    heads = k_n.shape[0]
    scale = HEAD_DIM**-0.5
    for b in range(length // ROWS_STEP):
        rows = slice(b * ROWS_STEP, (b + 1) * ROWS_STEP)
        middle = x[rows, :].astype(F32) + (part_a[rows, :].astype(F32) + part_b[rows, :].astype(F32))
        normed_blk = (middle * rms_scale(middle) * gain[...]).astype(BF16)
        normed[rows, :] = normed_blk
        query = dot_nn(normed_blk, wq[...]).astype(BF16).astype(F32) * scale
        keys = dot_nn(normed_blk, wk[...]).astype(BF16).astype(F32)
        values = dot_nn(normed_blk, wv[...]).astype(BF16).astype(F32)
        out_grad = dot_nt(grad[rows, :], wm[...]).astype(BF16).astype(F32)
        q_t[:, rows] = query.T.astype(BF16)
        k_t[:, rows] = (keys.T * scale).astype(BF16)
        v_t[:, rows] = values.T.astype(BF16)
        g_t[:, rows] = out_grad.T.astype(BF16)
        for h in range(heads):
            cols = slice(h * HEAD_DIM, (h + 1) * HEAD_DIM)
            q_n[h, rows, :] = query[:, cols].astype(BF16)
            k_n[h, rows, :] = keys[:, cols].astype(BF16)
            v_n[h, rows, :] = values[:, cols].astype(BF16)
            g_n[h, rows, :] = out_grad[:, cols].astype(BF16)
    dk[...] = jnp.zeros_like(dk)
    dv[...] = jnp.zeros_like(dv)

    for block in range(length // QUERY_BLOCK):
        cols = slice(block * QUERY_BLOCK, (block + 1) * QUERY_BLOCK)
        reach = (block + 1) * QUERY_BLOCK
        key_at = lax.broadcasted_iota(jnp.int32, (reach, QUERY_BLOCK), 0)
        query_at = lax.broadcasted_iota(jnp.int32, (reach, QUERY_BLOCK), 1) + block * QUERY_BLOCK
        kept = (key_at >= first[:, cols]) & (key_at <= query_at)
        bias[0:reach, :] = jnp.where(kept, 0.0, NEG)

        def one_head(h, unused):
            dims = pl.ds(pl.multiple_of(h * HEAD_DIM, HEAD_DIM), HEAD_DIM)
            tiles = [slice(t * KEY_TILE, (t + 1) * KEY_TILE) for t in range(reach // KEY_TILE)]

            def by_eight(tile):
                return tile.reshape(KEY_TILE // 8, 8, QUERY_BLOCK)

            query, out_grad = q_t[dims, cols], g_t[dims, cols]
            most = jnp.full((8, QUERY_BLOCK), NEG, F32)
            for keys in tiles:
                scores = dot_nn(k_n[h, keys, :], query) + bias[keys, :]
                expo[keys, :] = scores
                most = jnp.maximum(most, jnp.max(by_eight(scores), axis=0))
            most = jnp.max(most, axis=0, keepdims=True)
            total = jnp.zeros((8, QUERY_BLOCK), F32)
            centre = jnp.zeros((8, QUERY_BLOCK), F32)
            for keys in tiles:
                exponent = jnp.exp(expo[keys, :] - most)
                grads = dot_nn(v_n[h, keys, :], out_grad)
                expo[keys, :] = exponent
                prob_grad[keys, :] = grads
                total = total + jnp.sum(by_eight(exponent), axis=0)
                centre = centre + jnp.sum(by_eight(exponent * grads), axis=0)
            scale_by = 1.0 / jnp.sum(total, axis=0, keepdims=True)
            centre = jnp.sum(centre, axis=0, keepdims=True) * scale_by
            for keys in tiles:
                prob = expo[keys, :] * scale_by
                prob_low[keys, :] = prob.astype(BF16)
                score_low[keys, :] = (prob * (prob_grad[keys, :] - centre)).astype(BF16)
            o_t[dims, cols] = dot_nn(v_t[dims, 0:reach], prob_low[0:reach, :]).astype(BF16)
            dq_n[h, cols, :] = dot_nn(k_t[dims, 0:reach], score_low[0:reach, :]).T
            dk[h, 0:reach, :] += dot_nn(score_low[0:reach, :], q_n[h, cols, :])
            dv[h, 0:reach, :] += dot_nn(prob_low[0:reach, :], g_n[h, cols, :])
            return unused

        lax.fori_loop(0, heads, one_head, 0)

    blocks = length // ROWS_STEP

    def rows_at(b):
        return pl.ds(pl.multiple_of(b * ROWS_STEP, ROWS_STEP), ROWS_STEP)

    def back_copy(b):
        return remote(back.at[rows_at(b)], back_got.at[rows_at(b)], pass_sems, b, other_core)

    def branch_copy(b):
        there = branch_got.at[rows_at(b)]
        return remote(branch.at[rows_at(b)], there, pass_sems, blocks + b, other_core)

    def partials(b, unused):
        rows = rows_at(b)
        for target, source in ((dq_low, dq_n), (dk_low, dk), (dv_low, dv)):
            joined = jnp.concatenate([source[h, rows, :] for h in range(heads)], axis=1)
            target[rows, :] = joined.astype(BF16)
        total = dot_nt(dq_low[rows, :], wq[...]) + dot_nt(dk_low[rows, :], wk[...])
        back[rows, :] = (total + dot_nt(dv_low[rows, :], wv[...])).astype(BF16)
        back_copy(b).start()
        branch[rows, :] = dot_tn(o_t[:, rows], wm[...]).astype(BF16)
        branch_copy(b).start()
        return unused

    lax.fori_loop(0, blocks, partials, 0)
    cut = width // 2
    attn_rows = width + cut + head_cols
    pack[0:width, 0:head_cols] = dot_tn(normed[...], dq_low[...]).astype(BF16)
    pack[0:width, head_cols:] = dot_tn(normed[...], dk_low[...]).astype(BF16)
    value_grad = dot_tn(normed[...], dv_low[...]).astype(BF16)
    pack[width : width + cut, 0:head_cols] = value_grad[:cut]
    pack[width : width + cut, head_cols:] = value_grad[cut:]
    pack[width + cut : attn_rows, :] = dot_nn(o_t[...], grad[...]).astype(BF16)
    for load in loads[5:]:
        load.wait()
    gout[...] = jnp.zeros_like(gout)
    ggate[...] = jnp.zeros_like(ggate)
    gain_grad_o[...] = jnp.zeros_like(gain_grad_o)

    def stores(b):
        rows = rows_at(b)
        return [
            pltpu.make_async_copy(source.at[rows], target.at[rows], store_sems.at[i, b])
            for i, (source, target) in enumerate(
                ((base, base_o), (scan_grad, scan_grad_o), (gate_back, back_o))
            )
        ]

    def gating(b, unused):
        rows = rows_at(b)
        back_copy(b).wait()
        branch_copy(b).wait()
        middle = x[rows, :].astype(F32) + (part_a[rows, :].astype(F32) + part_b[rows, :].astype(F32))
        total = back[rows, :].astype(F32) + back_got[rows, :].astype(F32)
        factor = rms_scale(middle)
        middle_grad = grad[rows, :].astype(F32) + rms_back(middle, factor, gain[...], total)
        gain_grad_o[...] += jnp.sum(total * middle * factor, axis=0, keepdims=True)
        layer_out = middle + (branch[rows, :].astype(F32) + branch_got[rows, :].astype(F32))
        chosen = (1 - core).astype(F32)
        base[rows, :] = chosen * middle_grad + (1.0 - chosen) * layer_out
        low = middle_grad.astype(BF16)
        gout[...] += dot_tn(gated[rows, :], low)
        gated_grad = dot_nt(low, out_w[...])
        z = gate[rows, :]
        sigma = jax.nn.sigmoid(z)
        scan_grad[rows, :] = gated_grad * (z * sigma)
        slope = sigma * (1.0 + z * (1.0 - sigma))
        gate_low = (gated_grad * scan_out[rows, :] * slope).astype(BF16)
        ggate[...] += dot_tn(normed_a[rows, :], gate_low)
        gate_back[rows, :] = dot_nt(gate_low, w_gate[...])
        for store in stores(b):
            store.start()
        return unused

    lax.fori_loop(0, blocks, gating, 0)
    pack[attn_rows : attn_rows + channels, :] = gout[...].astype(BF16)
    pack[attn_rows + channels :, :] = ggate[...].astype(BF16)
    last = pltpu.make_async_copy(pack, pack_o, load_sems.at[0])
    last.start()
    for b in range(blocks):
        for store in stores(b):
            store.wait()
    last.wait()


def scan_back_block(
    coef, pre, step_in, scan_grad, flags, starts, step_w, decay_t, skip,
    act_grad, coef_grad, small, spare, between,
):
    (state, steps, stepd, drive, reads, blocked, d_drive, d_expo, in_own, read_own,
     decays, decayed, h_low, sum_low, expo_low) = spare
    block, width = pre.shape
    states = decay_t.shape[0]
    rank = step_w.shape[0]
    tiles = width // 128
    wide = CHUNK * states

    step_pre = step_in[...]
    step = softplus(step_pre)
    act = pre[...] * jax.nn.sigmoid(pre[...])
    spread(steps, step)
    spread(drive, step * act)
    spread(stepd, jnp.where(flags[:, 1:2] > 0.0, step, FAR))
    spread(reads, scan_grad[...])
    neg = -jnp.exp(decay_t[...])
    neg_of = [neg[:, c * 128 : (c + 1) * 128] for c in range(tiles)]
    picks = state_picks(CHUNK, states)
    own = own_token(CHUNK, states)
    own_low = own.astype(F32).astype(BF16)
    own_all = jnp.concatenate([own] * (block // CHUNK), axis=0)
    blocked[...] = jnp.where(
        own_all, dot_tn(coef[rank : rank + states, :].astype(BF16), picks), 0.0
    ).astype(BF16)

    def one_chunk(i, backward, spare):
        decay_s, decayed_s, h_s, sum_s, expo_s = spare
        rows16 = pl.ds(pl.multiple_of(i * CHUNK, CHUNK), CHUNK)
        tile = coef[rank:, pl.ds(pl.multiple_of((i // 8) * 128, 128), 128)]
        tile = pltpu.roll(tile, lax.rem(128 - lax.rem(i, 8) * CHUNK, 128), 1)
        h = [starts[rows16, c * 128 : (c + 1) * 128] for c in range(tiles)]
        for at in range(CHUNK):
            row = i * CHUNK + at
            here = slice(at * states, (at + 1) * states)
            write = column_of(tile[:states], at)
            for c in range(tiles):
                cols = slice(c * 128, (c + 1) * 128)
                decay = jnp.exp(neg_of[c] * row_of(stepd, c, row, states))
                kept = decay * h[c]
                h[c] = kept + row_of(drive, c, row, states) * write
                decay_s[c, here, :] = decay
                decayed_s[c, here, :] = kept
                h_s[here, cols] = h[c].astype(BF16)
        total = [jnp.zeros((states, 128), F32)] * tiles
        for at in reversed(range(CHUNK)):
            row = i * CHUNK + at
            here = slice(at * states, (at + 1) * states)
            read = column_of(tile[states:], at)
            for c in range(tiles):
                cols = slice(c * 128, (c + 1) * 128)
                summed = read * row_of(reads, c, row, states) + backward[c]
                sum_s[here, cols] = summed.astype(BF16)
                expo = summed * decayed_s[c, here, :]
                expo_s[here, cols] = (expo * neg_of[c]).astype(BF16)
                total[c] = total[c] + expo * row_of(steps, c, row, states)
                backward[c] = decay_s[c, here, :] * summed
        for c in range(tiles):
            small[rank : rank + states, c * 128 : (c + 1) * 128] += total[c]

        def flat(ref):
            return jnp.concatenate([ref[c, rows16, :] for c in range(tiles)], axis=1).astype(BF16)

        d_drive[rows16, :] = dot_nn(blocked[rows16, :], sum_s[...])
        d_expo[rows16, :] = dot_nn(own_low, expo_s[...])
        in_own[rows16, :] = jnp.where(own, dot_nt(flat(drive), sum_s[...]), 0.0)
        read_own[rows16, :] = jnp.where(own, dot_nt(flat(reads), h_s[...]), 0.0)
        return backward

    def pair(step_no, carried):
        between(step_no)
        backward = list(carried)
        last = block // CHUNK - 1 - 2 * step_no
        for sub in range(2):
            spare = (decays.at[sub], decayed.at[sub], h_low.at[sub], sum_low.at[sub], expo_low.at[sub])
            backward = one_chunk(last - sub, backward, spare)
        return tuple(backward)

    begin = tuple(state[:, c * 128 : (c + 1) * 128] for c in range(tiles))
    for c, last in enumerate(lax.fori_loop(0, block // (2 * CHUNK), pair, begin)):
        state[:, c * 128 : (c + 1) * 128] = last

    def by_state(ref):
        high = ref[...].astype(BF16)
        rest = (ref[...] - high.astype(F32)).astype(BF16)
        return dot_nt(picks, high) + dot_nt(picks, rest)

    coef_grad[rank : rank + states, :] = by_state(in_own)
    coef_grad[rank + states :, :] = by_state(read_own)

    drive_grad = d_drive[...]
    pre_grad = (d_expo[...] + drive_grad * act) * jax.nn.sigmoid(step_pre)
    tail = rank + states
    small[tail : tail + 1, :] += jnp.sum(pre_grad, axis=0, keepdims=True)
    pre_low = pre_grad.astype(BF16)
    small[:rank, :] += dot_nn(coef[:rank, :].astype(BF16), pre_low)
    coef_grad[:rank, :] = dot_nt(step_w[...], pre_low)
    act_grad[...] = drive_grad * step + scan_grad[...] * skip[...]
    small[tail + 1 : tail + 2, :] += jnp.sum(scan_grad[...] * act, axis=0, keepdims=True)


def conv_back_block(
    coef_grad, pre, act_grad, conv_in, normed, x, gate_back, flags, state_w, taps, w_conv,
    ext, gconv, gsmall, taps_at,
):
    block = pre.shape[0]
    coefs = coef_grad.shape[0]
    v = pre[...]
    sigma = jax.nn.sigmoid(v)
    gsmall[0:coefs, :] += dot_nn(coef_grad, (v * sigma).astype(BF16))
    act_all = act_grad[...] + dot_tn(coef_grad, state_w[...])
    conv_grad = act_all * (sigma * (1.0 + v * (1.0 - sigma)))
    ext[0:block, :] = conv_grad
    conv_in_grad = taps[3:4, :] * conv_grad
    sums = [None] * 4
    sums[3] = jnp.sum(conv_grad * conv_in[...], axis=0, keepdims=True)
    for j in range(1, 4):
        moved = jnp.where(flags[:, 4 + j : 5 + j] > 0.0, ext[j : j + block, :], 0.0)
        sums[3 - j] = jnp.sum(moved * conv_in[...], axis=0, keepdims=True)
        conv_in_grad = conv_in_grad + taps[3 - j : 4 - j, :] * moved
    for j in range(4):
        gsmall[taps_at + j : taps_at + j + 1, :] += sums[j]
    gsmall[taps_at + 4 : taps_at + 5, :] += jnp.sum(conv_grad, axis=0, keepdims=True)
    low = conv_in_grad.astype(BF16)
    gconv[...] += dot_tn(normed[...], low)
    back = gate_back[...] + dot_nt(low, w_conv[...])
    u = x[...].astype(F32)
    gsmall[taps_at + 5 : taps_at + 6, :] += jnp.sum(back * u * rms_scale(u), axis=0, keepdims=True)
    ext[block:, :] = ext[0:8, :]
    return back


def sum_plan(rows, counts):
    bits = [(axis, 1 << i) for axis, size in counts for i in range(size.bit_length() - 1)]
    digits = [bits[i : i + 2] for i in range(0, len(bits), 2)]
    most = (rows * 13 // 20 + 128) // 256 * 256
    sizes = [(0, most), (1, rows - most)] if rows > 1024 else [(0, most // 2), (0, most // 2), (1, rows - most)]
    streams, at, land = [], 0, 0
    for number, size in sizes:
        turn = number % len(digits)
        steps, held = [], size
        for digit in digits[turn:] + digits[:turn]:
            radix = 1 << len(digit)
            split = held % (16 * radix) == 0
            held = held // radix if split else held
            steps.append((digit, split, held, land))
            land += held * (radix - 1)
        streams.append((at, size, steps))
        at += size
    return streams, land


class Summing:
    def __init__(self, plan, src, work, land, full, peer, send, recv):
        self.streams, self.src, self.work, self.land = plan, src, work, land
        self.full, self.peer = full, peer
        self.sems = (send, recv)
        self.turns = len(plan[0][2])
        self.phases = 2 * self.turns + 2
        self.start = []
        for first, _, steps in plan:
            at, spots = first, [first]
            for turn, (digit, split, kept, _) in enumerate(steps):
                at = at + self.index(digit, 0) * kept if split else at
                spots.append(at)
            self.start.append(spots)

    def index(self, digit, flipped):
        total = 0
        for i, (axis, weight) in enumerate(digit):
            place = lax.rem(lax.axis_index(axis) // weight, 2)
            total = total + (1 - place if flipped >> i & 1 else place) * (1 << i)
        return total

    def partner(self, digit, flipped):
        device = {}
        for i, (axis, weight) in enumerate(digit):
            if flipped >> i & 1:
                me = lax.axis_index(axis)
                device[axis] = device.get(axis, me) + weight * (1 - 2 * lax.rem(me // weight, 2))
        return device

    def other_core(self):
        return {"kind": 1 - lax.axis_index("kind")}

    def others(self, s, turn):
        return range(1, 1 << len(self.streams[s][2][turn][0]))

    def rows(self, ref, at, size):
        return ref.at[pl.ds(pl.multiple_of(at, 16), size)]

    def number(self, s, kind, turn, flipped):
        return ((s * 3 + kind) * (self.turns + 1) + turn) * 4 + flipped

    def piece(self, s, turn, flipped):
        digit, split, kept, _ = self.streams[s][2][turn]
        at = self.start[s][turn]
        return at + self.index(digit, flipped) * kept if split else at

    def halves(self, s, turn):
        digit, _, kept, land = self.streams[s][2][turn]
        source = self.src if turn == 0 else self.work
        return [
            remote(
                self.rows(source, self.piece(s, turn, q), kept),
                self.land.at[pl.ds(land + (q - 1) * kept, kept)],
                self.sems, self.number(s, 0, turn, q), self.partner(digit, q),
            )
            for q in self.others(s, turn)
        ]

    def add(self, s, turn):
        _, _, kept, land = self.streams[s][2][turn]
        at = self.start[s][turn + 1]
        source = self.src if turn == 0 else self.work
        target = self.full if turn == self.turns - 1 else self.work

        def step(i, unused):
            here = pl.ds(pl.multiple_of(at + i * 16, 16), 16)
            parts = [source[here, :].astype(F32)]
            for q in self.others(s, turn):
                there = pl.ds(pl.multiple_of(land + (q - 1) * kept + i * 16, 16), 16)
                parts.append(self.land[there, :].astype(F32))
            while len(parts) > 1:
                parts = [parts[i] + parts[i + 1] for i in range(0, len(parts), 2)]
            target[here, :] = parts[0].astype(BF16)
            return unused

        lax.fori_loop(0, kept // 16, step, 0)

    def spreads(self, s, turn):
        digit, split, kept, _ = self.streams[s][2][turn]
        if not split:
            return []
        here = self.rows(self.full, self.start[s][turn + 1], kept)
        return [
            remote(here, here, self.sems, self.number(s, 1, turn, q), self.partner(digit, q))
            for q in self.others(s, turn)
        ]

    def shares(self, s, turn):
        if turn == self.turns:
            found = [(0, self.start[s][turn], self.streams[s][2][-1][2])]
        else:
            _, split, kept, _ = self.streams[s][2][turn]
            found = [(q, self.piece(s, turn, q), kept) for q in self.others(s, turn)] if split else []
        return [
            remote(
                self.rows(self.full, at, size), self.rows(self.peer, at, size), self.sems,
                self.number(s, 2, turn, q), self.other_core(),
            )
            for q, at, size in found
        ]

    def slots(self, count):
        lengths = [2.5 + 14.0 * 0.5**turn for turn in range(self.turns)]
        found, at = [0], 0.0
        for length in lengths + lengths[::-1]:
            at += length * count / 42.0
            if at < count - 1:
                found.append(int(at))
        return found

    def greet(self):
        barrier = pltpu.get_barrier_semaphore()
        partners = [self.other_core()]
        for digit, _, _, _ in self.streams[0][2]:
            partners += [self.partner(digit, q) for q in range(1, 1 << len(digit))]
        for device in partners:
            pl.semaphore_signal(
                barrier, inc=1, device_id=device, device_id_type=pl.DeviceIdType.MESH
            )
        pl.semaphore_wait(barrier, len(partners))

    def begin(self, copies):
        for copy in copies:
            copy.start()

    def finish(self, copies):
        for copy in copies:
            copy.wait()

    def phase(self, number):
        for s in range(len(self.streams)):
            if number == 0:
                self.begin(self.halves(s, 0))
            elif number <= self.turns:
                self.finish(self.halves(s, number - 1))
                self.add(s, number - 1)
                if number < self.turns:
                    self.begin(self.halves(s, number))
                else:
                    self.begin(self.spreads(s, self.turns - 1))
                    self.begin(self.shares(s, self.turns))
            elif number <= 2 * self.turns:
                turn = 2 * self.turns - number
                self.finish(self.spreads(s, turn))
                if turn > 0:
                    self.begin(self.spreads(s, turn - 1))
                self.begin(self.shares(s, turn))
            else:
                for turn in range(self.turns + 1):
                    self.finish(self.shares(s, turn))


def sum_scratch(plan, rows, land, width):
    numbers = len(plan) * 3 * (len(plan[0][2]) + 1) * 4
    return [
        pltpu.VMEM((rows, width), BF16),
        pltpu.VMEM((land, width), BF16),
        pltpu.VMEM((rows, width), BF16),
        pltpu.VMEM((rows, width), BF16),
        pltpu.SemaphoreType.DMA((numbers,)),
        pltpu.SemaphoreType.DMA((numbers,)),
    ]


def both_copies(summing, out, sems, number):
    core = lax.axis_index("kind")
    return [
        pltpu.make_async_copy(summing.full, out.at[core], sems.at[number]),
        pltpu.make_async_copy(summing.peer, out.at[1 - core], sems.at[number + 1]),
    ]


def back_kernel(
    plan, plan_last, steps,
    coef, pre, step_in, scan_grad, flags, starts,
    pre_late, conv_in, normed, x, gate_back, flags_late,
    gain, gain_grad, pack, x_all, base_all, weights_all,
    early_o, late_o, kept_o, got_o,
    step_w, decay_t, skip, state_w, taps, w_conv, weight_sems,
    scan_spare, small, act_grads, coef_grads, coef_got, ext, gconv, gsmall, back, low, low_got,
    x_s, base_s, kept, sent, got, pack_last, sum_spare, sum_spare_last,
    coef_sems, low_sems, pass_sems, local_sems,
):
    pid = pl.program_id(0)
    states, rank, coefs = decay_t.shape[0], step_w.shape[0], state_w.shape[0]
    block = pre.shape[0]
    pairs = block // (2 * CHUNK)
    taps_at = coefs + small.shape[0]
    core, row = lax.axis_index("kind"), lax.axis_index("inner")
    other_core = {"kind": 1 - core}
    first_sum = Summing(plan, pack, *sum_spare)
    last_sum = Summing(plan_last, pack_last, *sum_spare_last)
    slots = first_sum.slots(pairs * steps)
    load_x = pltpu.make_async_copy(x_all, x_s, local_sems.at[0])
    load_base = pltpu.make_async_copy(base_all, base_s, local_sems.at[1])
    mine = pl.ds(pl.multiple_of(core * w_conv.shape[1], 128), w_conv.shape[1])
    load_weights = [
        pltpu.make_async_copy(source.at[:, mine], target, weight_sems.at[i])
        for i, (source, target) in enumerate(
            zip(weights_all, (step_w, decay_t, skip, state_w, taps, w_conv), strict=True)
        )
    ]

    def coef_copy(i):
        return remote(coef_grads.at[i], coef_got.at[i], coef_sems, i, other_core)

    def low_copy(i):
        here = pl.ds(pl.multiple_of((steps - 1 - i) * block, block), block)
        return remote(low.at[here], low_got.at[here], low_sems, i, other_core)

    def first_phase(number):
        first_sum.phase(number)

    @pl.when(pid == 0)
    def _():
        scan_spare[0][...] = jnp.zeros_like(scan_spare[0])
        small[...] = jnp.zeros_like(small)
        ext[block:, :] = jnp.zeros((8, ext.shape[1]), F32)
        gconv[...] = jnp.zeros_like(gconv)
        gsmall[...] = jnp.zeros_like(gsmall)
        for copy in load_weights:
            copy.start()
        first_sum.greet()
        load_x.start()
        load_base.start()
        for copy in load_weights:
            copy.wait()

    @pl.when(pid < steps)
    def _():
        def between(step_no):
            slot = pid * pairs + step_no
            for number, at in enumerate(slots):
                pl.when(slot == at)(functools.partial(first_phase, number))

        scan_back_block(
            coef, pre, step_in, scan_grad, flags, starts, step_w, decay_t, skip,
            act_grads.at[lax.rem(pid, 2)], coef_grads.at[pid], small, scan_spare, between,
        )
        coef_copy(pid).start()

    @pl.when(pid > 0)
    def _():
        late = pid - 1
        coef_copy(late).wait()
        coef_low = (coef_grads[late] + coef_got[late]).astype(BF16)
        here = pl.ds(pl.multiple_of((steps - 1 - late) * block, block), block)
        part = conv_back_block(
            coef_low, pre_late, act_grads.at[lax.rem(late, 2)], conv_in, normed, x, gate_back,
            flags_late, state_w, taps, w_conv, ext, gconv, gsmall, taps_at,
        )
        back[here, :] = part
        low[here, :] = part.astype(BF16)
        low_copy(late).start()

    @pl.when(pid == steps)
    def _():
        width = gconv.shape[0]
        small[rank : rank + states, :] = small[rank : rank + states, :] * -jnp.exp(decay_t[...])
        gsmall[coefs:taps_at, :] = small[...]
        gsmall[taps_at + 6 : taps_at + 7, :] = gain_grad[...]
        pack_last[0:width, :] = gconv[...].astype(BF16)
        pack_last[width:, :] = gsmall[...].astype(BF16)
        last_sum.phase(0)
        for i in range(steps):
            low_copy(i).wait()
        load_x.wait()
        load_base.wait()
        chosen = (1 - core).astype(F32)
        half = kept.shape[0]

        def finish(at, target):
            def part(i, unused):
                here = pl.ds(pl.multiple_of(at + i * 64, 64), 64)
                there = pl.ds(pl.multiple_of(i * 64, 64), 64)
                u = x_s[here, :].astype(F32)
                total = back[here, :] + low_got[here, :].astype(F32)
                backward = rms_back(u, rms_scale(u), gain[...], total)
                target[there, :] = (base_s[here, :] + chosen * backward).astype(target.dtype)
                return unused

            lax.fori_loop(0, half // 64, part, 0)

        finish((1 - row) * half, sent)
        pieces = last_sum.phases - 2
        passing = [
            remote(
                sent.at[pl.ds(i * (half // pieces), half // pieces)],
                got.at[pl.ds(i * (half // pieces), half // pieces)], pass_sems, i, {"inner": 1 - row},
            )
            for i in range(pieces)
        ]
        finish(row * half, kept)
        keep = pltpu.make_async_copy(kept, kept_o, local_sems.at[2])
        keep.start()
        for number in range(len(slots), first_sum.phases):
            first_sum.phase(number)
        store_first = both_copies(first_sum, early_o, local_sems, 3)
        for copy in store_first:
            copy.start()
        for number in range(1, last_sum.phases):
            last_sum.phase(number)
            if number <= pieces:
                passing[number - 1].start()
        store_last = both_copies(last_sum, late_o, local_sems, 5)
        for copy in passing:
            copy.wait()
        store_got = pltpu.make_async_copy(got, got_o, local_sems.at[7])
        store_got.start()
        for copy in store_last:
            copy.start()
        for copy in store_first + store_last + [keep, store_got]:
            copy.wait()


def assemble_kernel(
    sizes, sel, kept, got, query_key, value, mixed, out, gate, conv, small,
    results_o, in_o, out_o, query_o, key_o, value_o, mixed_o,
    state_o, step_o, decay_o, step_bias_o, skip_o, taps_o, conv_bias_o, gain_o, attn_gain_o,
):
    first = sel[1] == 0
    mine, other = kept[...], got[...].astype(F32)
    results_o[0, 0] = jnp.where(first, mine, other)
    results_o[0, 1] = jnp.where(first, other, mine)
    half = conv.shape[2]
    cut = query_key.shape[2] // 2
    for part in range(2):
        here = slice(part * cut, (part + 1) * cut)
        in_o[:, part * half : (part + 1) * half] = conv[part].astype(F32)
        in_o[:, (2 + part) * half : (3 + part) * half] = gate[part].astype(F32)
        query_o[:, here] = query_key[part, :, :cut].astype(F32)
        key_o[:, here] = query_key[part, :, cut:].astype(F32)
        value_o[0, :, here] = value[part, :, :cut].astype(F32)
        value_o[1, :, here] = value[part, :, cut:].astype(F32)
    out_o[...] = out[...].astype(F32)
    mixed_o[...] = mixed[...].astype(F32)
    both = jnp.concatenate([small[0].astype(F32), small[1].astype(F32)], axis=1)
    coefs, rank, states = sizes
    at = 0
    for target, size in (
        (state_o, coefs), (step_o, rank), (decay_o, states), (step_bias_o, 1), (skip_o, 1),
        (None, 6), (taps_o, 4), (conv_bias_o, 1),
    ):
        if target is not None:
            target[...] = both[at : at + size]
        at += size
    gain_o[...] = both[at : at + 1, :half] + both[at : at + 1, half:]
    attn_gain_o[...] = both[at + 1 : at + 2, :half]


def local(
    layer_input, output_grad, document_ids, mamba_gain, in_proj, conv_weight, conv_bias, state_proj,
    step_proj, step_bias, decay_log, skip_gain, out_proj, attn_gain, query_proj, key_proj, value_proj,
    mixed_proj,
):
    _, piece_len, width = layer_input.shape
    length = output_grad.shape[1]
    parts = lax.axis_size("kind")
    half = in_proj.shape[1] // (2 * parts)
    states = decay_log.shape[1]
    rank = step_proj.shape[0]
    coefs = state_proj.shape[1]
    head_cols = width // parts
    heads = head_cols // HEAD_DIM
    core = lax.axis_index("kind")
    row = lax.axis_index("inner")
    sel = jnp.stack([core, row]).astype(jnp.int32)
    steps = length // ROWS_STEP

    def swap(value, axis):
        return jax.tree.map(lambda v: lax.ppermute(v, axis, [(0, 1), (1, 0)]), value)

    ids = lax.dynamic_index_in_dim(document_ids, row, 0, keepdims=False)
    first = jnp.sum((ids[None, :] < ids[:, None]).astype(jnp.int32), axis=1)
    since = jnp.arange(length, dtype=jnp.int32) - first
    after = jnp.concatenate([since, jnp.zeros((4,), jnp.int32)])
    flags = jnp.stack(
        [since >= j for j in range(4)] + [after[j : j + length] >= max(j, 1) for j in range(4)],
        axis=1,
    ).astype(F32)
    first = first[None, :]
    taps = conv_weight.T
    state_t = state_proj.T
    decay_t = decay_log.T
    conv_b, step_b, skip = conv_bias[None, :], step_bias[None, :], skip_gain[None, :]
    gain_a, gain_b = mamba_gain[None, :], attn_gain[None, :]

    def rows(array):
        return (array, (ROWS_STEP, array.shape[1]), lambda i, sel: (i, 0))

    def rows_rev(array):
        return (array, (ROWS_STEP, array.shape[1]), lambda i, sel: (steps - 1 - i, 0))

    def cols(array):
        return (array, (array.shape[0], ROWS_STEP), lambda i, sel: (0, i))

    def cols_rev(array):
        return (array, (array.shape[0], ROWS_STEP), lambda i, sel: (0, steps - 1 - i))

    def full(array):
        return (array,) + whole(array.shape)

    def half_cols(array, size, shift=0):
        return (array, (array.shape[0], size), lambda i, sel: (0, sel[0] + shift))

    def half_rows(array, size):
        return (array, (size, array.shape[1]), lambda i, sel: (sel[0], 0))

    def out_rows(size, dtype):
        return ((length, size), dtype, (ROWS_STEP, size), lambda i, sel: (i, 0))

    def out_rows_rev(size, dtype):
        return ((length, size), dtype, (ROWS_STEP, size), lambda i, sel: (steps - 1 - i, 0))

    def out_whole(shape, dtype=F32):
        return (shape, dtype) + whole(shape)

    w_conv = half_cols(in_proj, half)
    w_gate = half_cols(in_proj, half, parts)
    taps_half = half_cols(taps, half)
    state_half = half_cols(state_t, half)
    step_half = half_cols(step_proj, half)
    decay_half = half_cols(decay_t, half)
    skip_half = half_cols(skip, half)
    out_half = half_rows(out_proj, half)

    small_rows = rank + states + 8
    block_f32 = pltpu.VMEM((half // 128, ROWS_STEP, 128), F32)
    plain_f32 = pltpu.VMEM((ROWS_STEP, half), F32)
    wide = CHUNK * states
    blocks = length // ROWS_STEP
    assert length // CHUNK * states == length
    row_outs = [
        (width, BF16), (width, BF16), (half, F32), (half, F32), (half, F32), None, (half, F32), (half, F32),
        (half, BF16), (half, F32), (width, BF16), (width, BF16),
    ]
    row_f32, row_low = pltpu.VMEM((length, half), F32), pltpu.VMEM((length, half), BF16)
    x_low = pltpu.VMEM((length, width), BF16)
    block_coef = (blocks, coefs, ROWS_STEP)
    front_weights = (in_proj, state_t, step_proj, decay_t, skip, taps, conv_b, step_b, out_proj)

    def pair_of_sems(count):
        return [pltpu.SemaphoreType.DMA((count,)), pltpu.SemaphoreType.DMA((count,))]

    (x, normed_a, conv_in, conv_pre, gate_z, coef, step_pre, scan_out, gated, starts, branch,
     branch_other) = pl.pallas_call(
        front_kernel,
        in_specs=[pl.BlockSpec(memory_space=pltpu.VMEM)] * 2 + [pl.BlockSpec(memory_space=pl.ANY)]
        + [(pl.BlockSpec(memory_space=pl.ANY),) * len(front_weights)],
        out_specs=[pl.BlockSpec(memory_space=pl.ANY)] * len(row_outs),
        out_shape=[
            jax.ShapeDtypeStruct(block_coef, F32) if out is None
            else jax.ShapeDtypeStruct((length, out[0]), out[1])
            for out in row_outs
        ],
        scratch_shapes=[
            x_low, x_low, pltpu.VMEM((length + 8, half), F32), row_f32, row_f32,
            pltpu.VMEM(block_coef, F32), pltpu.VMEM(block_coef, F32), pltpu.VMEM(block_coef, F32),
            row_f32, row_f32, row_low, row_f32, x_low, x_low,
            [pltpu.VMEM((width, half), BF16), pltpu.VMEM((width, half), BF16)]
            + [pltpu.VMEM((array.shape[0], half), array.dtype)
               for array in (state_t, step_proj, decay_t, skip, taps, conv_b, step_b)]
            + [pltpu.VMEM((half, width), BF16)],
            [pltpu.VMEM((states, half), F32), block_f32, block_f32, plain_f32,
             pltpu.VMEM((ROWS_STEP, wide), BF16), pltpu.VMEM((STRETCH * wide, half), BF16)],
            pltpu.SemaphoreType.DMA((11,)), pair_of_sems(2), pair_of_sems(blocks), pair_of_sems(blocks),
            pltpu.SemaphoreType.DMA((9, blocks)), pltpu.SemaphoreType.DMA((3,)),
        ],
        compiler_params=pltpu.CompilerParams(
            vmem_limit_bytes=VMEM_BYTES, collective_id=2, has_side_effects=True
        ),
        cost_estimate=pl.CostEstimate(
            flops=2 * length * states * half * 1000, bytes_accessed=1 << 24, transcendentals=0
        ),
        name="front",
    )(flags, gain_a, layer_input, front_weights)

    vmem_spec = pl.BlockSpec(memory_space=pltpu.VMEM)
    any_spec = pl.BlockSpec(memory_space=pl.ANY)
    token_head = pltpu.VMEM((heads, length, HEAD_DIM), BF16)
    token_head_f32 = pltpu.VMEM((heads, length, HEAD_DIM), F32)
    head_token = pltpu.VMEM((head_cols, length), BF16)
    scores_f32 = pltpu.VMEM((length, QUERY_BLOCK), F32)
    scores_low = pltpu.VMEM((length, QUERY_BLOCK), BF16)
    tokens_low = pltpu.VMEM((length, width), BF16)
    tokens_f32 = pltpu.VMEM((length, width), F32)
    head_low = pltpu.VMEM((length, head_cols), BF16)
    square = pltpu.VMEM((width, head_cols), BF16)
    pack_rows = width + width // 2 + head_cols + half + width
    base, scan_grad, gate_back, pack_early, g_attn_gain = pl.pallas_call(
        middle_kernel,
        in_specs=[vmem_spec] * 5 + [any_spec] * 5 + [(any_spec,) * 6],
        out_specs=[any_spec] * 4 + [vmem_spec],
        out_shape=[
            jax.ShapeDtypeStruct((length, width), F32),
            jax.ShapeDtypeStruct((length, half), F32),
            jax.ShapeDtypeStruct((length, width), F32),
            jax.ShapeDtypeStruct((pack_rows, width), BF16),
            jax.ShapeDtypeStruct((1, width), F32),
        ],
        scratch_shapes=[
            tokens_low, pltpu.VMEM((length, half), BF16), pltpu.VMEM((length, half), F32),
            pltpu.VMEM((length, half), F32), tokens_low, square, square, square,
            pltpu.VMEM((head_cols, width), BF16), pltpu.VMEM((half, width), BF16),
            pltpu.VMEM((width, half), BF16),
            tokens_low, head_token, token_head, token_head, token_head, head_token, head_token,
            token_head, head_token, head_token, token_head_f32, token_head_f32, token_head_f32,
            scores_f32, scores_f32, scores_f32, scores_low, scores_low,
            head_low, head_low, head_low, tokens_low, tokens_low, tokens_low, tokens_low, tokens_f32,
            pltpu.VMEM((length, half), F32), tokens_f32, pltpu.VMEM((half, width), F32),
            pltpu.VMEM((width, half), F32), pltpu.VMEM((pack_rows, width), BF16),
            pltpu.SemaphoreType.DMA((11,)),
            [pltpu.SemaphoreType.DMA((2 * blocks,)), pltpu.SemaphoreType.DMA((2 * blocks,))],
            pltpu.SemaphoreType.DMA((3, blocks)),
        ],
        compiler_params=pltpu.CompilerParams(
            vmem_limit_bytes=VMEM_BYTES, collective_id=3, has_side_effects=True
        ),
        cost_estimate=pl.CostEstimate(
            flops=2 * length * length * width * 10, bytes_accessed=1 << 24, transcendentals=0
        ),
        name="middle",
    )(x, branch, branch_other, first, gain_b, output_grad, gated, gate_z, scan_out, normed_a,
      (query_proj, key_proj, value_proj, mixed_proj, out_proj, in_proj))

    counts = [("inner", lax.axis_size("inner")), ("dp", lax.axis_size("dp"))]
    plan, land = sum_plan(pack_early.shape[0], counts)
    last_rows = width + 128
    plan_last, land_last = sum_plan(last_rows, counts)
    tile_f32 = pltpu.VMEM((2, half // 128, wide, 128), F32)
    tile_low = pltpu.VMEM((2, wide, half), BF16)
    own_f32 = pltpu.VMEM((ROWS_STEP, wide), F32)

    def now(i):
        return jnp.maximum(steps - 1 - i, 0)

    def late_at(i):
        return jnp.minimum(steps - i, steps - 1)

    def back_rows(array, at):
        return (array, (ROWS_STEP, array.shape[1]), lambda i: (at(i), 0))

    def fixed(array):
        return (array, array.shape, None)

    ins = [
        (coef, (None, coefs, ROWS_STEP), lambda i: (now(i), 0, 0)), back_rows(conv_pre, now), back_rows(step_pre, now),
        back_rows(scan_grad, now), back_rows(flags, now),
        (starts, (ROWS_STEP // CHUNK * states, half), lambda i: (now(i), 0)),
        back_rows(conv_pre, late_at), back_rows(conv_in, late_at), back_rows(normed_a, late_at),
        back_rows(x, late_at), back_rows(gate_back, late_at), back_rows(flags, late_at),
        fixed(gain_a), fixed(g_attn_gain), fixed(pack_early),
    ]
    weights_all = (step_proj, decay_t, skip, state_t, taps, in_proj)
    specs = [
        pl.BlockSpec(block, lambda i: (0, 0), pipeline_mode=pl.Buffered(1)) if at is None
        else pl.BlockSpec(block, at)
        for _, block, at in ins
    ]
    early, late, kept, got = pl.pallas_call(
        functools.partial(back_kernel, plan, plan_last, steps),
        grid=(steps + 1,),
        in_specs=specs + [any_spec] * 2 + [(any_spec,) * len(weights_all)],
        out_specs=[any_spec] * 4,
        out_shape=[
            jax.ShapeDtypeStruct((parts,) + pack_early.shape, BF16),
            jax.ShapeDtypeStruct((parts, last_rows, width), BF16),
            jax.ShapeDtypeStruct((piece_len, width), F32),
            jax.ShapeDtypeStruct((piece_len, width), BF16),
        ],
        scratch_shapes=[pltpu.VMEM((array.shape[0], half), array.dtype) for array in weights_all] + [
            pltpu.SemaphoreType.DMA((len(weights_all),)),
            [pltpu.VMEM((states, half), F32), block_f32,
             block_f32, block_f32, block_f32, pltpu.VMEM((ROWS_STEP, wide), BF16), plain_f32,
             plain_f32, own_f32, own_f32, tile_f32, tile_f32, tile_low, tile_low, tile_low],
            pltpu.VMEM((small_rows, half), F32),
            pltpu.VMEM((2, ROWS_STEP, half), F32),
            pltpu.VMEM((steps, coefs, ROWS_STEP), F32),
            pltpu.VMEM((steps, coefs, ROWS_STEP), F32),
            pltpu.VMEM((ROWS_STEP + 8, half), F32),
            pltpu.VMEM((width, half), F32),
            pltpu.VMEM((128, half), F32),
            pltpu.VMEM((length, width), F32),
            pltpu.VMEM((length, width), BF16),
            pltpu.VMEM((length, width), BF16),
            pltpu.VMEM((length, width), BF16),
            pltpu.VMEM((length, width), F32),
            pltpu.VMEM((piece_len, width), F32),
            pltpu.VMEM((piece_len, width), BF16),
            pltpu.VMEM((piece_len, width), BF16),
            pltpu.VMEM((last_rows, width), BF16),
            sum_scratch(plan, pack_early.shape[0], land, width),
            sum_scratch(plan_last, last_rows, land_last, width),
            [pltpu.SemaphoreType.DMA((steps,)), pltpu.SemaphoreType.DMA((steps,))],
            [pltpu.SemaphoreType.DMA((steps,)), pltpu.SemaphoreType.DMA((steps,))],
            [pltpu.SemaphoreType.DMA((16,)), pltpu.SemaphoreType.DMA((16,))],
            pltpu.SemaphoreType.DMA((8,)),
        ],
        compiler_params=pltpu.CompilerParams(
            dimension_semantics=("arbitrary",), vmem_limit_bytes=VMEM_BYTES, collective_id=1,
            has_side_effects=True,
        ),
        cost_estimate=pl.CostEstimate(
            flops=2 * length * states * half * 3000, bytes_accessed=1 << 25, transcendentals=0
        ),
        name="back",
    )(*[a for a, _, _ in ins], x, base, weights_all)
    quarter = width // 4
    eighth = width // 8

    def from_sum(total, size, first_row):
        return (total, (parts, size, width), lambda i, sel: (0, first_row // size + i, 0))

    def out_parts(size):
        return ((parts, 4 * size, width), F32, (parts, size, width), lambda i, sel: (0, i, 0))

    attn_rows = width + width // 2 + head_cols
    results, t_in, t_out, t_query, t_key, t_value, t_mixed, *smalls = call(
        functools.partial(assemble_kernel, (coefs, rank, states)), sel, 4,
        [(kept, (piece_len // 4, width), lambda i, sel: (i, 0)),
         (got, (piece_len // 4, width), lambda i, sel: (i, 0)),
         from_sum(early, quarter, 0), from_sum(early, eighth, width),
         from_sum(early, eighth, width + width // 2), from_sum(early, quarter, attn_rows),
         from_sum(early, quarter, attn_rows + half), from_sum(late, quarter, 0),
         (late, (parts, 128, width), lambda i, sel: (0, width // 128, 0))],
        [((1, 2, piece_len, width), F32, (1, 2, piece_len // 4, width), lambda i, sel: (0, 0, i, 0)),
         ((width, 4 * half), F32, (quarter, 4 * half), lambda i, sel: (i, 0)),
         out_parts(quarter), ((width, width), F32, (quarter, width), lambda i, sel: (i, 0)),
         ((width, width), F32, (quarter, width), lambda i, sel: (i, 0)), out_parts(eighth),
         out_parts(eighth)]
        + [out_whole((size, parts * half)) for size in (coefs, rank, states, 1, 1, 4, 1)]
        + [out_whole((1, width))] * 2,
        [], 0, "assemble",
    )
    t_state, t_step, t_decay, t_step_bias, t_skip, t_taps, t_conv_bias, t_gain, t_attn_gain = smalls
    return (
        results, t_gain[0], t_in, t_taps.T, t_conv_bias[0], t_state.T, t_step, t_step_bias[0],
        t_decay.T, t_skip[0], t_out.reshape(out_proj.shape), t_attn_gain[0], t_query, t_key,
        t_value.reshape(width, width), t_mixed.reshape(width, width),
    )


def solution(mesh):
    in_specs = (P("dp", "inner", None), P("dp", None, None), P("dp", None)) + (P(),) * 15
    out_specs = (P("kind", "dp", "inner", None),) + (P(),) * 15
    return jax.shard_map(local, mesh=mesh, in_specs=in_specs, out_specs=out_specs, check_vma=False)
```

```python
import functools

import jax
import jax.numpy as jnp
from jax import lax
from jax.experimental import pallas as pl
from jax.experimental.pallas import tpu as pltpu
from jax.sharding import PartitionSpec as P

HEAD_DIM = 64
EPS = 1e-05
NEG = -1e30
FAR = 1e30
CHUNK = 16
STRETCH = 8
ROWS_STEP = 256
QUERY_BLOCK = 256
KEY_TILE = 128
VMEM_BYTES = 58 * 1024 * 1024
F32 = jnp.float32
BF16 = jnp.bfloat16


def dot_nn(a, b):
    return lax.dot_general(a, b, (((1,), (0,)), ((), ())), preferred_element_type=F32)


def dot_nt(a, b):
    return lax.dot_general(a, b, (((1,), (1,)), ((), ())), preferred_element_type=F32)


def dot_tn(a, b):
    return lax.dot_general(a, b, (((0,), (0,)), ((), ())), preferred_element_type=F32)


def silu_slope(tensor):
    sigma = jax.nn.sigmoid(tensor)
    return sigma * (1.0 + tensor * (1.0 - sigma))


def rms_scale(tensor):
    return lax.rsqrt(jnp.mean(tensor * tensor, axis=-1, keepdims=True) + EPS)


def softplus(tensor):
    return jnp.maximum(tensor, 0.0) + jnp.log1p(jnp.exp(-jnp.abs(tensor)))


def rms_back(tensor, factor, gain_vec, gradient):
    weighted = gradient * gain_vec
    spread = jnp.mean(weighted * tensor, axis=-1, keepdims=True)
    return factor * weighted - tensor * (factor * factor * factor) * spread


def spread(ref, value):
    for c in range(ref.shape[0]):
        ref[c] = value[:, c * 128 : (c + 1) * 128]


def row_of(ref, c, row, states):
    part = ref[c, pl.ds(row, 8, stride=0), :]
    return jnp.concatenate([part] * (states // 8), axis=0)


def column_of(tile, at):
    return jnp.broadcast_to(tile[:, at : at + 1], tile.shape)


def own_token(chunk, states):
    at = lax.broadcasted_iota(jnp.int32, (chunk, chunk * states), 0)
    of = lax.broadcasted_iota(jnp.int32, (chunk, chunk * states), 1) // states
    return at == of


def state_picks(chunk, states):
    at = lax.broadcasted_iota(jnp.int32, (states, chunk * states), 0)
    of = lax.rem(lax.broadcasted_iota(jnp.int32, (states, chunk * states), 1), states)
    return (at == of).astype(F32).astype(BF16)


def remote(src, dst, sems, number, to):
    return pltpu.make_async_remote_copy(
        src_ref=src, dst_ref=dst, send_sem=sems[0].at[number], recv_sem=sems[1].at[number],
        device_id=to, device_id_type=pl.DeviceIdType.MESH,
    )


def call(body, sel, steps, ins, outs, scratch, flops, name):
    bytes_all = sum(a.size * a.dtype.itemsize for a, _, _ in ins)
    return pl.pallas_call(
        body,
        grid_spec=pltpu.PrefetchScalarGridSpec(
            num_scalar_prefetch=1,
            grid=(steps,),
            in_specs=[pl.BlockSpec(block, at) for _, block, at in ins],
            out_specs=[pl.BlockSpec(block, at) for _, _, block, at in outs],
            scratch_shapes=scratch,
        ),
        out_shape=[jax.ShapeDtypeStruct(shape, dtype) for shape, dtype, _, _ in outs],
        compiler_params=pltpu.CompilerParams(
            dimension_semantics=("arbitrary",), vmem_limit_bytes=VMEM_BYTES
        ),
        cost_estimate=pl.CostEstimate(flops=flops, bytes_accessed=bytes_all, transcendentals=0),
        name=name,
    )(sel, *[a for a, _, _ in ins])


def whole(shape):
    zeros = (0,) * len(shape)
    return (shape, lambda i, sel: zeros)


def scan_block(
    coef, pre, gate, flags, step_w, step_b, decay_t, skip, out_w,
    step_o, scan_o, gated_o, starts_o, branch_o, spare,
):
    state, stepd, drive, ys, blocked, h_low = spare
    block, width = pre.shape
    states = decay_t.shape[0]
    rank = step_w.shape[0]
    tiles = width // 128

    step_pre = dot_tn(coef[:rank, :].astype(BF16), step_w[...]) + step_b[...]
    step_o[...] = step_pre
    step = softplus(step_pre)
    act = pre[...] * jax.nn.sigmoid(pre[...])
    spread(drive, step * act)
    spread(stepd, jnp.where(flags[:, 1:2] > 0.0, step, FAR))
    neg = -jnp.exp(decay_t[...])
    neg_of = [neg[:, c * 128 : (c + 1) * 128] for c in range(tiles)]
    own_all = jnp.concatenate([own_token(CHUNK, states)] * (block // CHUNK), axis=0)
    blocked[...] = jnp.where(
        own_all, dot_tn(coef[rank + states :, :].astype(BF16), state_picks(CHUNK, states)), 0.0
    ).astype(BF16)

    def one_chunk(i, h, h_s):
        here = pl.ds(pl.multiple_of(i * CHUNK, CHUNK), CHUNK)
        tile = coef[rank : rank + states, pl.ds(pl.multiple_of((i // 8) * 128, 128), 128)]
        tile = pltpu.roll(tile, lax.rem(128 - lax.rem(i, 8) * CHUNK, 128), 1)
        for c in range(tiles):
            starts_o[here, c * 128 : (c + 1) * 128] = h[c]
        for at in range(CHUNK):
            row = i * CHUNK + at
            write = column_of(tile, at)
            for c in range(tiles):
                decay = jnp.exp(neg_of[c] * row_of(stepd, c, row, states))
                h[c] = decay * h[c] + row_of(drive, c, row, states) * write
                h_s[at * states : (at + 1) * states, c * 128 : (c + 1) * 128] = h[c].astype(BF16)
        return h

    def stretch(number, carried):
        def pair(step_no, carried):
            h = list(carried)
            for sub in range(2):
                at = 2 * step_no + sub
                spot = h_low.at[pl.ds(pl.multiple_of(at * CHUNK * states, CHUNK * states), CHUNK * states)]
                h = one_chunk(number * STRETCH + at, h, spot)
            return tuple(h)

        carried = lax.fori_loop(0, STRETCH // 2, pair, carried)
        for at in range(STRETCH):
            here = pl.ds(pl.multiple_of((number * STRETCH + at) * CHUNK, CHUNK), CHUNK)
            spot = slice(at * CHUNK * states, (at + 1) * CHUNK * states)
            ys[here, :] = dot_nn(blocked[here, :], h_low[spot, :])
        return carried

    begin = tuple(state[:, c * 128 : (c + 1) * 128] for c in range(tiles))
    for c, last in enumerate(lax.fori_loop(0, block // (STRETCH * CHUNK), stretch, begin)):
        state[:, c * 128 : (c + 1) * 128] = last
    scan_out = ys[...] + skip[...] * act
    scan_o[...] = scan_out
    z = gate[...]
    gated = (scan_out * (z * jax.nn.sigmoid(z))).astype(BF16)
    gated_o[...] = gated
    branch_o[...] = dot_nn(gated, out_w[...]).astype(BF16)


def front_kernel(
    flags, gain, layer_all, weights_all,
    x_o, normed_o, conv_o, pre_o, gate_o, coef_o, step_o, scan_o, gated_o, starts_o, branch_o, branch_other_o,
    x, normed, ext, pre, gate, coef, coef_got, coef_sum, step_pre, scan_out, gated, starts, branch,
    branch_got, weights, scan_spare, load_sems, x_sems, coef_sems, branch_sems, store_sems, late_sems,
):
    length, width = x.shape
    blocks = length // ROWS_STEP
    core, row = lax.axis_index("kind"), lax.axis_index("inner")
    other_core, other_row = {"kind": 1 - core}, {"inner": 1 - row}
    w_conv, w_gate, state_w, step_w, decay_t, skip, taps, conv_b, step_b, out_w = weights
    in_all, state_all, step_all, decay_all, skip_all, taps_all, conv_b_all, step_b_all, out_all = weights_all
    channels = w_conv.shape[1]

    def part_of(number):
        return pl.ds(pl.multiple_of(number * channels, 128), channels)

    def rows_at(b):
        return pl.ds(pl.multiple_of(b * ROWS_STEP, ROWS_STEP), ROWS_STEP)

    mine = part_of(core)
    loads = [
        pltpu.make_async_copy(source, target, load_sems.at[i])
        for i, (source, target) in enumerate((
            (layer_all.at[row], x.at[pl.ds(pl.multiple_of(row * (length // 2), 256), length // 2)]),
            (in_all.at[:, mine], w_conv), (in_all.at[:, part_of(2 + core)], w_gate),
            (state_all.at[:, mine], state_w), (step_all.at[:, mine], step_w),
            (decay_all.at[:, mine], decay_t), (skip_all.at[:, mine], skip), (taps_all.at[:, mine], taps),
            (conv_b_all.at[:, mine], conv_b), (step_b_all.at[:, mine], step_b), (out_all.at[mine], out_w),
        ))
    ]
    barrier = pltpu.get_barrier_semaphore()
    for device in (other_core, other_row):
        pl.semaphore_signal(barrier, inc=1, device_id=device, device_id_type=pl.DeviceIdType.MESH)
    pl.semaphore_wait(barrier, 2)
    sent = remote(
        layer_all.at[1 - row, rows_at(core)], x.at[rows_at(row * (blocks // 2) + core)], x_sems, 0, other_row
    )
    sent.start()
    for load in loads:
        load.start()
    for load in loads:
        load.wait()
    ext[0:8, :] = jnp.zeros((8, channels), F32)
    scan_spare[0][...] = jnp.zeros_like(scan_spare[0])

    results = (
        (x, x_o), (normed, normed_o), (gate, gate_o), (pre, pre_o), (step_pre, step_o),
        (scan_out, scan_o), (gated, gated_o), (starts, starts_o), (branch, branch_o),
    )

    def stores(b, numbers=range(len(results))):
        rows = rows_at(b)
        return [
            pltpu.make_async_copy(results[i][0].at[rows], results[i][1].at[rows], store_sems.at[i, b])
            for i in numbers
        ]

    def project(b):
        rows = rows_at(b)
        u = x[rows, :].astype(F32)
        low = (u * rms_scale(u) * gain[...]).astype(BF16)
        normed[rows, :] = low
        ext[pl.ds(pl.multiple_of(b * ROWS_STEP + 8, 8), ROWS_STEP), :] = dot_nn(low, w_conv[...])
        gate[rows, :] = dot_nn(low, w_gate[...])
        for store in stores(b, range(3)):
            store.start()

    first_other = (1 - row) * (blocks // 2)
    project(row * (blocks // 2))
    project(row * (blocks // 2) + 1)
    sent.wait()
    fetched = x.at[rows_at(first_other + core)]
    passed = remote(fetched, fetched, x_sems, 1, other_core)
    passed.start()
    project(first_other + core)
    passed.wait()
    project(first_other + 1 - core)
    store_conv = pltpu.make_async_copy(ext.at[pl.ds(8, length)], conv_o, late_sems.at[0])
    store_conv.start()

    def coef_copy(b):
        return remote(coef.at[b], coef_got.at[b], coef_sems, b, other_core)

    def branch_copy(b):
        rows = rows_at(b)
        return remote(branch.at[rows], branch_got.at[rows], branch_sems, b, other_core)

    for b in range(blocks):
        rows = slice(b * ROWS_STEP, (b + 1) * ROWS_STEP)
        total = conv_b[...] + taps[3:4, :] * ext[8 + b * ROWS_STEP : 8 + (b + 1) * ROWS_STEP, :]
        for j in range(1, 4):
            moved = ext[8 - j + b * ROWS_STEP : 8 - j + (b + 1) * ROWS_STEP, :]
            total = total + taps[3 - j : 4 - j, :] * jnp.where(flags[rows, j : j + 1] > 0.0, moved, 0.0)
        pre[rows, :] = total
        coef[b] = dot_nt(state_w[...], (total * jax.nn.sigmoid(total)).astype(BF16))
        coef_copy(b).start()
        stores(b, [3])[0].start()

    def scan(b, unused):
        rows = rows_at(b)
        coef_copy(b).wait()
        coef_sum[b] = coef[b] + coef_got[b]
        scan_block(
            coef_sum.at[b], pre.at[rows], gate.at[rows], flags.at[rows], step_w, step_b, decay_t, skip, out_w,
            step_pre.at[rows], scan_out.at[rows], gated.at[rows], starts.at[rows], branch.at[rows],
            scan_spare,
        )
        branch_copy(b).start()
        for store in stores(b, range(4, len(results))):
            store.start()
        return unused

    lax.fori_loop(0, blocks, scan, 0)
    store_coef = pltpu.make_async_copy(coef_sum, coef_o, late_sems.at[1])
    store_coef.start()
    for b in range(blocks):
        branch_copy(b).wait()
    store_other = pltpu.make_async_copy(branch_got, branch_other_o, late_sems.at[2])
    store_other.start()
    for copy in (store_conv, store_coef, store_other):
        copy.wait()
    for b in range(blocks):
        for store in stores(b):
            store.wait()


def middle_kernel(
    plan,
    x, part_a, part_b, first, gain, grads, gated_all, gate_all, scan_all, normed_all, weights_all,
    base_o, scan_grad_o, back_o, pack_o, gain_grad_o, begun_o,
    grad, gated, gate, scan_out, normed_a, wq, wk, wv, wm, out_w, w_gate,
    normed, q_t, q_n, k_n, v_n, k_t, v_t, g_n, g_t, o_t, dq_n, dk, dv, bias, expo, prob_grad, prob_low,
    score_low,
    dq_low, dk_low, dv_low, branch, branch_got, back, back_got, base, scan_grad, gate_back, gout, ggate,
    pack, land, sum_sems, load_sems, pass_sems, store_sems,
):
    length, width = x.shape
    core, row = lax.axis_index("kind"), lax.axis_index("inner")
    other_core = {"kind": 1 - core}
    head_cols, channels = wq.shape[1], out_w.shape[0]

    def part_of(size):
        return pl.ds(pl.multiple_of(core * size, 128), size)

    query_all, key_all, value_all, mixed_all, out_all, in_all = weights_all
    gate_cols = pl.ds(pl.multiple_of((2 + core) * channels, 128), channels)
    loads = [
        pltpu.make_async_copy(source, target, load_sems.at[i])
        for i, (source, target) in enumerate((
            (query_all.at[:, part_of(head_cols)], wq), (key_all.at[:, part_of(head_cols)], wk),
            (value_all.at[:, part_of(head_cols)], wv), (grads.at[row], grad),
            (mixed_all.at[part_of(head_cols)], wm), (gated_all, gated), (gate_all, gate),
            (scan_all, scan_out), (normed_all, normed_a), (out_all.at[part_of(channels)], out_w),
            (in_all.at[:, gate_cols], w_gate),
        ))
    ]
    for load in loads:
        load.start()
    summing = Summing(plan, pack, None, land, None, None, *sum_sems)
    digit, _, begun_rows, _ = plan[0][2][0]
    barrier = pltpu.get_barrier_semaphore()
    partners = [other_core] + [summing.partner(digit, q) for q in range(1, 1 << len(digit))]
    for device in partners:
        pl.semaphore_signal(barrier, inc=1, device_id=device, device_id_type=pl.DeviceIdType.MESH)
    pl.semaphore_wait(barrier, len(partners))
    for load in loads[:5]:
        load.wait()

    heads = k_n.shape[0]
    scale = HEAD_DIM**-0.5
    for b in range(length // ROWS_STEP):
        rows = slice(b * ROWS_STEP, (b + 1) * ROWS_STEP)
        middle = x[rows, :].astype(F32) + (part_a[rows, :].astype(F32) + part_b[rows, :].astype(F32))
        normed_blk = (middle * rms_scale(middle) * gain[...]).astype(BF16)
        normed[rows, :] = normed_blk
        query = dot_nn(normed_blk, wq[...]).astype(BF16).astype(F32) * scale
        keys = dot_nn(normed_blk, wk[...]).astype(BF16).astype(F32)
        values = dot_nn(normed_blk, wv[...]).astype(BF16).astype(F32)
        out_grad = dot_nt(grad[rows, :], wm[...]).astype(BF16).astype(F32)
        q_t[:, rows] = query.T.astype(BF16)
        k_t[:, rows] = (keys.T * scale).astype(BF16)
        v_t[:, rows] = values.T.astype(BF16)
        g_t[:, rows] = out_grad.T.astype(BF16)
        for h in range(heads):
            cols = slice(h * HEAD_DIM, (h + 1) * HEAD_DIM)
            q_n[h, rows, :] = query[:, cols].astype(BF16)
            k_n[h, rows, :] = keys[:, cols].astype(BF16)
            v_n[h, rows, :] = values[:, cols].astype(BF16)
            g_n[h, rows, :] = out_grad[:, cols].astype(BF16)
    dk[...] = jnp.zeros_like(dk)
    dv[...] = jnp.zeros_like(dv)

    for block in range(length // QUERY_BLOCK):
        cols = slice(block * QUERY_BLOCK, (block + 1) * QUERY_BLOCK)
        reach = (block + 1) * QUERY_BLOCK
        key_at = lax.broadcasted_iota(jnp.int32, (reach, QUERY_BLOCK), 0)
        query_at = lax.broadcasted_iota(jnp.int32, (reach, QUERY_BLOCK), 1) + block * QUERY_BLOCK
        kept = (key_at >= first[:, cols]) & (key_at <= query_at)
        bias[0:reach, :] = jnp.where(kept, 0.0, NEG)

        def one_head(h, unused):
            dims = pl.ds(pl.multiple_of(h * HEAD_DIM, HEAD_DIM), HEAD_DIM)
            tiles = [slice(t * KEY_TILE, (t + 1) * KEY_TILE) for t in range(reach // KEY_TILE)]

            def by_eight(tile):
                return tile.reshape(KEY_TILE // 8, 8, QUERY_BLOCK)

            query, out_grad = q_t[dims, cols], g_t[dims, cols]
            most = jnp.full((8, QUERY_BLOCK), NEG, F32)
            for keys in tiles:
                scores = dot_nn(k_n[h, keys, :], query) + bias[keys, :]
                expo[keys, :] = scores
                most = jnp.maximum(most, jnp.max(by_eight(scores), axis=0))
            most = jnp.max(most, axis=0, keepdims=True)
            total = jnp.zeros((8, QUERY_BLOCK), F32)
            centre = jnp.zeros((8, QUERY_BLOCK), F32)
            for keys in tiles:
                exponent = jnp.exp(expo[keys, :] - most)
                grads = dot_nn(v_n[h, keys, :], out_grad)
                expo[keys, :] = exponent
                prob_grad[keys, :] = grads
                total = total + jnp.sum(by_eight(exponent), axis=0)
                centre = centre + jnp.sum(by_eight(exponent * grads), axis=0)
            scale_by = 1.0 / jnp.sum(total, axis=0, keepdims=True)
            centre = jnp.sum(centre, axis=0, keepdims=True) * scale_by
            for keys in tiles:
                prob = expo[keys, :] * scale_by
                prob_low[keys, :] = prob.astype(BF16)
                score_low[keys, :] = (prob * (prob_grad[keys, :] - centre)).astype(BF16)
            o_t[dims, cols] = dot_nn(v_t[dims, 0:reach], prob_low[0:reach, :]).astype(BF16)
            dq_n[h, cols, :] = dot_nn(k_t[dims, 0:reach], score_low[0:reach, :]).T
            dk[h, 0:reach, :] += dot_nn(score_low[0:reach, :], q_n[h, cols, :])
            dv[h, 0:reach, :] += dot_nn(prob_low[0:reach, :], g_n[h, cols, :])
            return unused

        lax.fori_loop(0, heads, one_head, 0)

    blocks = length // ROWS_STEP

    def rows_at(b):
        return pl.ds(pl.multiple_of(b * ROWS_STEP, ROWS_STEP), ROWS_STEP)

    def back_copy(b):
        return remote(back.at[rows_at(b)], back_got.at[rows_at(b)], pass_sems, b, other_core)

    def branch_copy(b):
        there = branch_got.at[rows_at(b)]
        return remote(branch.at[rows_at(b)], there, pass_sems, blocks + b, other_core)

    def partials(b, unused):
        rows = rows_at(b)
        for target, source in ((dq_low, dq_n), (dk_low, dk), (dv_low, dv)):
            joined = jnp.concatenate([source[h, rows, :] for h in range(heads)], axis=1)
            target[rows, :] = joined.astype(BF16)
        total = dot_nt(dq_low[rows, :], wq[...]) + dot_nt(dk_low[rows, :], wk[...])
        back[rows, :] = (total + dot_nt(dv_low[rows, :], wv[...])).astype(BF16)
        back_copy(b).start()
        branch[rows, :] = dot_tn(o_t[:, rows], wm[...]).astype(BF16)
        branch_copy(b).start()
        return unused

    lax.fori_loop(0, blocks, partials, 0)
    cut = width // 2
    attn_rows = width + cut + head_cols
    pack[0:width, 0:head_cols] = dot_tn(normed[...], dq_low[...]).astype(BF16)
    pack[0:width, head_cols:] = dot_tn(normed[...], dk_low[...]).astype(BF16)
    value_grad = dot_tn(normed[...], dv_low[...]).astype(BF16)
    pack[width : width + cut, 0:head_cols] = value_grad[:cut]
    pack[width : width + cut, head_cols:] = value_grad[cut:]
    pack[width + cut : attn_rows, :] = dot_nn(o_t[...], grad[...]).astype(BF16)
    summing.begin(summing.halves(0, 0))
    for load in loads[5:]:
        load.wait()
    gout[...] = jnp.zeros_like(gout)
    ggate[...] = jnp.zeros_like(ggate)
    gain_grad_o[...] = jnp.zeros_like(gain_grad_o)

    def stores(b):
        rows = rows_at(b)
        return [
            pltpu.make_async_copy(source.at[rows], target.at[rows], store_sems.at[i, b])
            for i, (source, target) in enumerate(
                ((base, base_o), (scan_grad, scan_grad_o), (gate_back, back_o))
            )
        ]

    def gating(b, unused):
        rows = rows_at(b)
        back_copy(b).wait()
        branch_copy(b).wait()
        middle = x[rows, :].astype(F32) + (part_a[rows, :].astype(F32) + part_b[rows, :].astype(F32))
        total = back[rows, :].astype(F32) + back_got[rows, :].astype(F32)
        factor = rms_scale(middle)
        middle_grad = grad[rows, :].astype(F32) + rms_back(middle, factor, gain[...], total)
        gain_grad_o[...] += jnp.sum(total * middle * factor, axis=0, keepdims=True)
        layer_out = middle + (branch[rows, :].astype(F32) + branch_got[rows, :].astype(F32))
        chosen = (1 - core).astype(F32)
        base[rows, :] = chosen * middle_grad + (1.0 - chosen) * layer_out
        low = middle_grad.astype(BF16)
        gout[...] += dot_tn(gated[rows, :], low)
        gated_grad = dot_nt(low, out_w[...])
        z = gate[rows, :]
        sigma = jax.nn.sigmoid(z)
        scan_grad[rows, :] = gated_grad * (z * sigma)
        slope = sigma * (1.0 + z * (1.0 - sigma))
        gate_low = (gated_grad * scan_out[rows, :] * slope).astype(BF16)
        ggate[...] += dot_tn(normed_a[rows, :], gate_low)
        gate_back[rows, :] = dot_nt(gate_low, w_gate[...])
        for store in stores(b):
            store.start()
        return unused

    lax.fori_loop(0, blocks, gating, 0)
    pack[attn_rows : attn_rows + channels, :] = gout[...].astype(BF16)
    pack[attn_rows + channels :, :] = ggate[...].astype(BF16)
    last = pltpu.make_async_copy(pack, pack_o, load_sems.at[0])
    last.start()
    summing.finish(summing.halves(0, 0))
    summing.add_to(begun_o, 0, 0, 0)
    for b in range(blocks):
        for store in stores(b):
            store.wait()
    last.wait()


def scan_back_block(
    coef, pre, step_in, scan_grad, flags, starts, step_w, decay_t, skip,
    act_grad, coef_grad, small, spare, between,
):
    (state, steps, stepd, drive, reads, blocked, d_drive, d_expo, in_own, read_own,
     decays, decayed, h_low, sum_low, expo_low) = spare
    block, width = pre.shape
    states = decay_t.shape[0]
    rank = step_w.shape[0]
    tiles = width // 128
    wide = CHUNK * states

    step_pre = step_in[...]
    step = softplus(step_pre)
    act = pre[...] * jax.nn.sigmoid(pre[...])
    spread(steps, step)
    spread(drive, step * act)
    spread(stepd, jnp.where(flags[:, 1:2] > 0.0, step, FAR))
    spread(reads, scan_grad[...])
    neg = -jnp.exp(decay_t[...])
    neg_of = [neg[:, c * 128 : (c + 1) * 128] for c in range(tiles)]
    picks = state_picks(CHUNK, states)
    own = own_token(CHUNK, states)
    own_low = own.astype(F32).astype(BF16)
    own_all = jnp.concatenate([own] * (block // CHUNK), axis=0)
    blocked[...] = jnp.where(
        own_all, dot_tn(coef[rank : rank + states, :].astype(BF16), picks), 0.0
    ).astype(BF16)

    def one_chunk(i, backward, spare):
        decay_s, decayed_s, h_s, sum_s, expo_s = spare
        rows16 = pl.ds(pl.multiple_of(i * CHUNK, CHUNK), CHUNK)
        tile = coef[rank:, pl.ds(pl.multiple_of((i // 8) * 128, 128), 128)]
        tile = pltpu.roll(tile, lax.rem(128 - lax.rem(i, 8) * CHUNK, 128), 1)
        h = [starts[rows16, c * 128 : (c + 1) * 128] for c in range(tiles)]
        for at in range(CHUNK):
            row = i * CHUNK + at
            here = slice(at * states, (at + 1) * states)
            write = column_of(tile[:states], at)
            for c in range(tiles):
                cols = slice(c * 128, (c + 1) * 128)
                decay = jnp.exp(neg_of[c] * row_of(stepd, c, row, states))
                kept = decay * h[c]
                h[c] = kept + row_of(drive, c, row, states) * write
                decay_s[c, here, :] = decay
                decayed_s[c, here, :] = kept
                h_s[here, cols] = h[c].astype(BF16)
        total = [jnp.zeros((states, 128), F32)] * tiles
        for at in reversed(range(CHUNK)):
            row = i * CHUNK + at
            here = slice(at * states, (at + 1) * states)
            read = column_of(tile[states:], at)
            for c in range(tiles):
                cols = slice(c * 128, (c + 1) * 128)
                summed = read * row_of(reads, c, row, states) + backward[c]
                sum_s[here, cols] = summed.astype(BF16)
                expo = summed * decayed_s[c, here, :]
                expo_s[here, cols] = (expo * neg_of[c]).astype(BF16)
                total[c] = total[c] + expo * row_of(steps, c, row, states)
                backward[c] = decay_s[c, here, :] * summed
        for c in range(tiles):
            small[rank : rank + states, c * 128 : (c + 1) * 128] += total[c]

        def flat(ref):
            return jnp.concatenate([ref[c, rows16, :] for c in range(tiles)], axis=1).astype(BF16)

        d_drive[rows16, :] = dot_nn(blocked[rows16, :], sum_s[...])
        d_expo[rows16, :] = dot_nn(own_low, expo_s[...])
        in_own[rows16, :] = jnp.where(own, dot_nt(flat(drive), sum_s[...]), 0.0)
        read_own[rows16, :] = jnp.where(own, dot_nt(flat(reads), h_s[...]), 0.0)
        return backward

    def pair(step_no, carried):
        between(step_no)
        backward = list(carried)
        last = block // CHUNK - 1 - 2 * step_no
        for sub in range(2):
            spare = (decays.at[sub], decayed.at[sub], h_low.at[sub], sum_low.at[sub], expo_low.at[sub])
            backward = one_chunk(last - sub, backward, spare)
        return tuple(backward)

    begin = tuple(state[:, c * 128 : (c + 1) * 128] for c in range(tiles))
    for c, last in enumerate(lax.fori_loop(0, block // (2 * CHUNK), pair, begin)):
        state[:, c * 128 : (c + 1) * 128] = last

    def by_state(ref):
        high = ref[...].astype(BF16)
        rest = (ref[...] - high.astype(F32)).astype(BF16)
        return dot_nt(picks, high) + dot_nt(picks, rest)

    coef_grad[rank : rank + states, :] = by_state(in_own)
    coef_grad[rank + states :, :] = by_state(read_own)

    drive_grad = d_drive[...]
    pre_grad = (d_expo[...] + drive_grad * act) * jax.nn.sigmoid(step_pre)
    tail = rank + states
    small[tail : tail + 1, :] += jnp.sum(pre_grad, axis=0, keepdims=True)
    pre_low = pre_grad.astype(BF16)
    small[:rank, :] += dot_nn(coef[:rank, :].astype(BF16), pre_low)
    coef_grad[:rank, :] = dot_nt(step_w[...], pre_low)
    act_grad[...] = drive_grad * step + scan_grad[...] * skip[...]
    small[tail + 1 : tail + 2, :] += jnp.sum(scan_grad[...] * act, axis=0, keepdims=True)


def conv_back_block(
    coef_grad, pre, act_grad, conv_in, normed, flags, state_w, taps, ext, gconv, gsmall, mix_low, taps_at,
):
    block = pre.shape[0]
    coefs = coef_grad.shape[0]
    v = pre[...]
    sigma = jax.nn.sigmoid(v)
    gsmall[0:coefs, :] += dot_nn(coef_grad, (v * sigma).astype(BF16))
    act_all = act_grad[...] + dot_tn(coef_grad, state_w[...])
    conv_grad = act_all * (sigma * (1.0 + v * (1.0 - sigma)))
    ext[0:block, :] = conv_grad
    conv_in_grad = taps[3:4, :] * conv_grad
    sums = [None] * 4
    sums[3] = jnp.sum(conv_grad * conv_in[...], axis=0, keepdims=True)
    for j in range(1, 4):
        moved = jnp.where(flags[:, 4 + j : 5 + j] > 0.0, ext[j : j + block, :], 0.0)
        sums[3 - j] = jnp.sum(moved * conv_in[...], axis=0, keepdims=True)
        conv_in_grad = conv_in_grad + taps[3 - j : 4 - j, :] * moved
    for j in range(4):
        gsmall[taps_at + j : taps_at + j + 1, :] += sums[j]
    gsmall[taps_at + 4 : taps_at + 5, :] += jnp.sum(conv_grad, axis=0, keepdims=True)
    low = conv_in_grad.astype(BF16)
    gconv[...] += dot_tn(normed[...], low)
    mix_low[...] = low
    ext[block:, :] = ext[0:8, :]


def sum_digits(counts):
    bits = [(axis, 1 << i) for axis, size in counts for i in range(size.bit_length() - 1)]
    return [bits[i : i + 2] for i in range(0, len(bits), 2)]


def sum_plan(counts, parts):
    digits = sum_digits(counts)
    streams, at, land = [], 0, 0
    for number, size, lead in parts:
        turn = number % len(digits)
        steps, held = [], size
        for digit in digits[turn:] + digits[:turn]:
            radix = 1 << len(digit)
            split = held % (16 * radix) == 0
            held = held // radix if split else held
            steps.append((digit, split, held, land))
            land += held * (radix - 1)
        streams.append((at, size, steps, lead))
        at += size
    return streams, land


class Summing:
    def __init__(self, plan, src, work, land, full, peer, send, recv, given=None):
        self.given = given
        self.streams, self.src, self.work, self.land = plan, src, work, land
        self.full, self.peer = full, peer
        self.sems = (send, recv)
        self.turns = len(plan[0][2])
        self.phases = 2 * self.turns + 2 - min(0, *(lead for _, _, _, lead in plan))
        self.start = []
        for first, _, steps, _ in plan:
            at, spots = first, [first]
            for turn, (digit, split, kept, _) in enumerate(steps):
                at = at + self.index(digit, 0) * kept if split else at
                spots.append(at)
            self.start.append(spots)

    def index(self, digit, flipped):
        total = 0
        for i, (axis, weight) in enumerate(digit):
            place = lax.rem(lax.axis_index(axis) // weight, 2)
            total = total + (1 - place if flipped >> i & 1 else place) * (1 << i)
        return total

    def partner(self, digit, flipped):
        device = {}
        for i, (axis, weight) in enumerate(digit):
            if flipped >> i & 1:
                me = lax.axis_index(axis)
                device[axis] = device.get(axis, me) + weight * (1 - 2 * lax.rem(me // weight, 2))
        return device

    def other_core(self):
        return {"kind": 1 - lax.axis_index("kind")}

    def others(self, s, turn):
        return range(1, 1 << len(self.streams[s][2][turn][0]))

    def rows(self, ref, at, size):
        return ref.at[pl.ds(pl.multiple_of(at, 16), size)]

    def number(self, s, kind, turn, flipped):
        return ((s * 3 + kind) * (self.turns + 1) + turn) * 4 + flipped

    def piece(self, s, turn, flipped):
        digit, split, kept, _ = self.streams[s][2][turn]
        at = self.start[s][turn]
        return at + self.index(digit, flipped) * kept if split else at

    def halves(self, s, turn):
        digit, _, kept, land = self.streams[s][2][turn]
        source = self.src if turn == 0 else self.work
        return [
            remote(
                self.rows(source, self.piece(s, turn, q), kept),
                self.land.at[pl.ds(land + (q - 1) * kept, kept)],
                self.sems, self.number(s, 0, turn, q), self.partner(digit, q),
            )
            for q in self.others(s, turn)
        ]

    def add(self, s, turn):
        target = self.full if turn == self.turns - 1 else self.work
        self.add_to(target, self.start[s][turn + 1], s, turn)

    def add_to(self, target, first, s, turn):
        _, _, kept, land = self.streams[s][2][turn]
        at = self.start[s][turn + 1]
        source = self.src if turn == 0 else self.work

        def step(i, unused):
            here = pl.ds(pl.multiple_of(at + i * 16, 16), 16)
            parts = [source[here, :].astype(F32)]
            for q in self.others(s, turn):
                there = pl.ds(pl.multiple_of(land + (q - 1) * kept + i * 16, 16), 16)
                parts.append(self.land[there, :].astype(F32))
            while len(parts) > 1:
                parts = [parts[i] + parts[i + 1] for i in range(0, len(parts), 2)]
            target[pl.ds(pl.multiple_of(first + i * 16, 16), 16), :] = parts[0].astype(BF16)
            return unused

        lax.fori_loop(0, kept // 16, step, 0)

    def spreads(self, s, turn):
        digit, split, kept, _ = self.streams[s][2][turn]
        if not split:
            return []
        here = self.rows(self.full, self.start[s][turn + 1], kept)
        return [
            remote(here, here, self.sems, self.number(s, 1, turn, q), self.partner(digit, q))
            for q in self.others(s, turn)
        ]

    def shares(self, s, turn):
        if turn == self.turns:
            found = [(0, self.start[s][turn], self.streams[s][2][-1][2])]
        else:
            _, split, kept, _ = self.streams[s][2][turn]
            found = [(q, self.piece(s, turn, q), kept) for q in self.others(s, turn)] if split else []
        return [
            remote(
                self.rows(self.full, at, size), self.rows(self.peer, at, size), self.sems,
                self.number(s, 2, turn, q), self.other_core(),
            )
            for q, at, size in found
        ]

    def greet(self):
        barrier = pltpu.get_barrier_semaphore()
        partners = [self.other_core()]
        for digit, _, _, _ in self.streams[0][2]:
            partners += [self.partner(digit, q) for q in range(1, 1 << len(digit))]
        for device in partners:
            pl.semaphore_signal(
                barrier, inc=1, device_id=device, device_id_type=pl.DeviceIdType.MESH
            )
        pl.semaphore_wait(barrier, len(partners))

    def begin(self, copies):
        for copy in copies:
            copy.start()

    def finish(self, copies):
        for copy in copies:
            copy.wait()

    def phase(self, number):
        for s, (_, _, steps, lead) in enumerate(self.streams):
            at = number + lead
            if number == self.phases - 1:
                for turn in range(self.turns + 1):
                    self.finish(self.shares(s, turn))
            elif at == 0:
                self.begin(self.halves(s, 0))
            elif 0 < at <= self.turns:
                if number == 0:
                    kept = steps[at - 1][2]
                    self.work[pl.ds(pl.multiple_of(self.start[s][at], 16), kept), :] = self.given[...]
                else:
                    self.finish(self.halves(s, at - 1))
                    self.add(s, at - 1)
                if at < self.turns:
                    self.begin(self.halves(s, at))
                else:
                    self.begin(self.spreads(s, self.turns - 1))
                    self.begin(self.shares(s, self.turns))
            elif self.turns < at <= 2 * self.turns:
                turn = 2 * self.turns - at
                self.finish(self.spreads(s, turn))
                if turn > 0:
                    self.begin(self.spreads(s, turn - 1))
                self.begin(self.shares(s, turn))


def sum_scratch(plan, rows, land, width):
    numbers = len(plan) * 3 * (len(plan[0][2]) + 1) * 4
    return [
        pltpu.VMEM((rows, width), BF16),
        pltpu.VMEM((land, width), BF16),
        pltpu.VMEM((rows, width), BF16),
        pltpu.VMEM((rows, width), BF16),
        pltpu.SemaphoreType.DMA((numbers,)),
        pltpu.SemaphoreType.DMA((numbers,)),
    ]


def both_copies(summing, out, sems, number):
    core = lax.axis_index("kind")
    return [
        pltpu.make_async_copy(summing.full, out.at[core], sems.at[number]),
        pltpu.make_async_copy(summing.peer, out.at[1 - core], sems.at[number + 1]),
    ]


def back_kernel(
    plan, plan_last, steps,
    coef, pre, step_in, scan_grad, flags, starts,
    pre_late, conv_in, normed, flags_late,
    gain, gain_grad, pack, begun, x_all, base_all, gate_back_all, weights_all,
    early_o, late_o, kept_o, got_o,
    step_w, decay_t, skip, state_w, taps, w_conv, weight_sems,
    scan_spare, small, act_grads, coef_grads, coef_got, ext, gconv, gsmall, mix_low, back, low, low_got,
    x_s, base_s, kept, sent, got, pack_last, sum_spare, sum_spare_last,
    coef_sems, low_sems, pass_sems, local_sems,
):
    pid = pl.program_id(0)
    states, rank, coefs = decay_t.shape[0], step_w.shape[0], state_w.shape[0]
    block = pre.shape[0]
    pairs = block // (2 * CHUNK)
    taps_at = coefs + small.shape[0]
    core, row = lax.axis_index("kind"), lax.axis_index("inner")
    other_core = {"kind": 1 - core}
    first_sum = Summing(plan, pack, *sum_spare, given=begun)
    last_sum = Summing(plan_last, pack_last, *sum_spare_last)
    slots = [share * pairs * steps // 32 for share in (0, 9, 15, 22, 30)]
    load_x = pltpu.make_async_copy(x_all, x_s, local_sems.at[0])
    load_base = pltpu.make_async_copy(base_all, base_s, local_sems.at[1])
    load_back = pltpu.make_async_copy(gate_back_all, back, local_sems.at[8])
    mine = pl.ds(pl.multiple_of(core * w_conv.shape[1], 128), w_conv.shape[1])
    load_weights = [
        pltpu.make_async_copy(source.at[:, mine], target, weight_sems.at[i])
        for i, (source, target) in enumerate(
            zip(weights_all, (step_w, decay_t, skip, state_w, taps, w_conv), strict=True)
        )
    ]

    def coef_copy(i):
        return remote(coef_grads.at[i], coef_got.at[i], coef_sems, i, other_core)

    def low_copy(i):
        here = pl.ds(pl.multiple_of((steps - 1 - i) * block, block), block)
        return remote(low.at[here], low_got.at[here], low_sems, i, other_core)

    def first_phase(number):
        first_sum.phase(number)

    @pl.when(pid == 0)
    def _():
        scan_spare[0][...] = jnp.zeros_like(scan_spare[0])
        small[...] = jnp.zeros_like(small)
        ext[block:, :] = jnp.zeros((8, ext.shape[1]), F32)
        gconv[...] = jnp.zeros_like(gconv)
        gsmall[...] = jnp.zeros_like(gsmall)
        for copy in load_weights:
            copy.start()
        first_sum.greet()
        load_x.start()
        load_base.start()
        load_back.start()
        for copy in load_weights:
            copy.wait()

    @pl.when(pid < steps)
    def _():
        def between(step_no):
            slot = pid * pairs + step_no
            for number, at in enumerate(slots):
                pl.when(slot == at)(functools.partial(first_phase, number))

        scan_back_block(
            coef, pre, step_in, scan_grad, flags, starts, step_w, decay_t, skip,
            act_grads.at[lax.rem(pid, 2)], coef_grads.at[pid], small, scan_spare, between,
        )
        coef_copy(pid).start()

    @pl.when(pid > 0)
    def _():
        late = pid - 1
        coef_copy(late).wait()
        coef_low = (coef_grads[late] + coef_got[late]).astype(BF16)
        here = pl.ds(pl.multiple_of((steps - 1 - late) * block, block), block)
        conv_back_block(
            coef_low, pre_late, act_grads.at[lax.rem(late, 2)], conv_in, normed, flags_late, state_w,
            taps, ext, gconv, gsmall, mix_low.at[here], taps_at,
        )

    @pl.when(pid == steps)
    def _():
        width = gconv.shape[0]
        small[rank : rank + states, :] = small[rank : rank + states, :] * -jnp.exp(decay_t[...])
        gsmall[coefs:taps_at, :] = small[...]
        gsmall[taps_at + 6 : taps_at + 7, :] = gain_grad[...]
        pack_last[0:width, :] = gconv[...].astype(BF16)
        pack_last[width : width + 128, :] = gsmall[...].astype(BF16)
        last_sum.phase(0)
        load_x.wait()
        load_back.wait()
        gain_sum = jnp.zeros((1, width), F32)
        for i in range(steps):
            here = slice((steps - 1 - i) * block, (steps - i) * block)
            total = back[here, :] + dot_nt(mix_low[here, :], w_conv[...])
            back[here, :] = total
            low[here, :] = total.astype(BF16)
            low_copy(i).start()
            u = x_s[here, :].astype(F32)
            gain_sum += jnp.sum(total * u * rms_scale(u), axis=0, keepdims=True)
        pack_last[width + 128 :, :] = jnp.concatenate(
            [gain_sum, jnp.zeros((15, width), F32)], axis=0
        ).astype(BF16)
        for number in range(len(slots), first_sum.phases - 1):
            first_sum.phase(number)
        last_sum.phase(1)
        for i in range(steps):
            low_copy(i).wait()
        load_base.wait()
        chosen = (1 - core).astype(F32)
        half = kept.shape[0]

        def finish(at, target):
            def part(i, unused):
                here = pl.ds(pl.multiple_of(at + i * 64, 64), 64)
                there = pl.ds(pl.multiple_of(i * 64, 64), 64)
                u = x_s[here, :].astype(F32)
                total = back[here, :] + low_got[here, :].astype(F32)
                backward = rms_back(u, rms_scale(u), gain[...], total)
                target[there, :] = (base_s[here, :] + chosen * backward).astype(target.dtype)
                return unused

            lax.fori_loop(0, half // 64, part, 0)

        finish((1 - row) * half, sent)
        pieces = 4
        passing = [
            remote(
                sent.at[pl.ds(i * (half // pieces), half // pieces)],
                got.at[pl.ds(i * (half // pieces), half // pieces)], pass_sems, i, {"inner": 1 - row},
            )
            for i in range(pieces)
        ]
        finish(row * half, kept)
        keep = pltpu.make_async_copy(kept, kept_o, local_sems.at[2])
        keep.start()
        first_sum.phase(first_sum.phases - 1)
        store_first = both_copies(first_sum, early_o, local_sems, 3)
        for copy in store_first:
            copy.start()
        for number in range(2, last_sum.phases):
            last_sum.phase(number)
            if number - 2 < pieces:
                passing[number - 2].start()
        store_last = both_copies(last_sum, late_o, local_sems, 5)
        for copy in passing:
            copy.wait()
        store_got = pltpu.make_async_copy(got, got_o, local_sems.at[7])
        store_got.start()
        for copy in store_last:
            copy.start()
        for copy in store_first + store_last + [keep, store_got]:
            copy.wait()


def assemble_kernel(
    sizes, sel, kept, got, query_key, value, mixed, out, gate, conv, small, gains,
    results_o, in_o, out_o, query_o, key_o, value_o, mixed_o,
    state_o, step_o, decay_o, step_bias_o, skip_o, taps_o, conv_bias_o, gain_o, attn_gain_o,
):
    first = sel[1] == 0
    mine, other = kept[...], got[...].astype(F32)
    results_o[0, 0] = jnp.where(first, mine, other)
    results_o[0, 1] = jnp.where(first, other, mine)
    half = conv.shape[2]
    cut = query_key.shape[2] // 2
    for part in range(2):
        here = slice(part * cut, (part + 1) * cut)
        in_o[:, part * half : (part + 1) * half] = conv[part].astype(F32)
        in_o[:, (2 + part) * half : (3 + part) * half] = gate[part].astype(F32)
        query_o[:, here] = query_key[part, :, :cut].astype(F32)
        key_o[:, here] = query_key[part, :, cut:].astype(F32)
        value_o[0, :, here] = value[part, :, :cut].astype(F32)
        value_o[1, :, here] = value[part, :, cut:].astype(F32)
    out_o[...] = out[...].astype(F32)
    mixed_o[...] = mixed[...].astype(F32)
    both = jnp.concatenate([small[0].astype(F32), small[1].astype(F32)], axis=1)
    coefs, rank, states = sizes
    at = 0
    for target, size in (
        (state_o, coefs), (step_o, rank), (decay_o, states), (step_bias_o, 1), (skip_o, 1),
        (None, 6), (taps_o, 4), (conv_bias_o, 1),
    ):
        if target is not None:
            target[...] = both[at : at + size]
        at += size
    gain_o[...] = gains[0, 0:1].astype(F32) + gains[1, 0:1].astype(F32)
    attn_gain_o[...] = both[at + 1 : at + 2, :half]


def local(
    layer_input, output_grad, document_ids, mamba_gain, in_proj, conv_weight, conv_bias, state_proj,
    step_proj, step_bias, decay_log, skip_gain, out_proj, attn_gain, query_proj, key_proj, value_proj,
    mixed_proj,
):
    _, piece_len, width = layer_input.shape
    length = output_grad.shape[1]
    parts = lax.axis_size("kind")
    half = in_proj.shape[1] // (2 * parts)
    states = decay_log.shape[1]
    rank = step_proj.shape[0]
    coefs = state_proj.shape[1]
    head_cols = width // parts
    heads = head_cols // HEAD_DIM
    core = lax.axis_index("kind")
    row = lax.axis_index("inner")
    sel = jnp.stack([core, row]).astype(jnp.int32)
    steps = length // ROWS_STEP

    def swap(value, axis):
        return jax.tree.map(lambda v: lax.ppermute(v, axis, [(0, 1), (1, 0)]), value)

    ids = lax.dynamic_index_in_dim(document_ids, row, 0, keepdims=False)
    first = jnp.sum((ids[None, :] < ids[:, None]).astype(jnp.int32), axis=1)
    since = jnp.arange(length, dtype=jnp.int32) - first
    after = jnp.concatenate([since, jnp.zeros((4,), jnp.int32)])
    flags = jnp.stack(
        [since >= j for j in range(4)] + [after[j : j + length] >= max(j, 1) for j in range(4)],
        axis=1,
    ).astype(F32)
    first = first[None, :]
    taps = conv_weight.T
    state_t = state_proj.T
    decay_t = decay_log.T
    conv_b, step_b, skip = conv_bias[None, :], step_bias[None, :], skip_gain[None, :]
    gain_a, gain_b = mamba_gain[None, :], attn_gain[None, :]

    def rows(array):
        return (array, (ROWS_STEP, array.shape[1]), lambda i, sel: (i, 0))

    def rows_rev(array):
        return (array, (ROWS_STEP, array.shape[1]), lambda i, sel: (steps - 1 - i, 0))

    def cols(array):
        return (array, (array.shape[0], ROWS_STEP), lambda i, sel: (0, i))

    def cols_rev(array):
        return (array, (array.shape[0], ROWS_STEP), lambda i, sel: (0, steps - 1 - i))

    def full(array):
        return (array,) + whole(array.shape)

    def half_cols(array, size, shift=0):
        return (array, (array.shape[0], size), lambda i, sel: (0, sel[0] + shift))

    def half_rows(array, size):
        return (array, (size, array.shape[1]), lambda i, sel: (sel[0], 0))

    def out_rows(size, dtype):
        return ((length, size), dtype, (ROWS_STEP, size), lambda i, sel: (i, 0))

    def out_rows_rev(size, dtype):
        return ((length, size), dtype, (ROWS_STEP, size), lambda i, sel: (steps - 1 - i, 0))

    def out_whole(shape, dtype=F32):
        return (shape, dtype) + whole(shape)

    w_conv = half_cols(in_proj, half)
    w_gate = half_cols(in_proj, half, parts)
    taps_half = half_cols(taps, half)
    state_half = half_cols(state_t, half)
    step_half = half_cols(step_proj, half)
    decay_half = half_cols(decay_t, half)
    skip_half = half_cols(skip, half)
    out_half = half_rows(out_proj, half)

    small_rows = rank + states + 8
    block_f32 = pltpu.VMEM((half // 128, ROWS_STEP, 128), F32)
    plain_f32 = pltpu.VMEM((ROWS_STEP, half), F32)
    wide = CHUNK * states
    blocks = length // ROWS_STEP
    assert length // CHUNK * states == length
    row_outs = [
        (width, BF16), (width, BF16), (half, F32), (half, F32), (half, F32), None, (half, F32), (half, F32),
        (half, BF16), (half, F32), (width, BF16), (width, BF16),
    ]
    row_f32, row_low = pltpu.VMEM((length, half), F32), pltpu.VMEM((length, half), BF16)
    x_low = pltpu.VMEM((length, width), BF16)
    block_coef = (blocks, coefs, ROWS_STEP)
    front_weights = (in_proj, state_t, step_proj, decay_t, skip, taps, conv_b, step_b, out_proj)

    def pair_of_sems(count):
        return [pltpu.SemaphoreType.DMA((count,)), pltpu.SemaphoreType.DMA((count,))]

    (x, normed_a, conv_in, conv_pre, gate_z, coef, step_pre, scan_out, gated, starts, branch,
     branch_other) = pl.pallas_call(
        front_kernel,
        in_specs=[pl.BlockSpec(memory_space=pltpu.VMEM)] * 2 + [pl.BlockSpec(memory_space=pl.ANY)]
        + [(pl.BlockSpec(memory_space=pl.ANY),) * len(front_weights)],
        out_specs=[pl.BlockSpec(memory_space=pl.ANY)] * len(row_outs),
        out_shape=[
            jax.ShapeDtypeStruct(block_coef, F32) if out is None
            else jax.ShapeDtypeStruct((length, out[0]), out[1])
            for out in row_outs
        ],
        scratch_shapes=[
            x_low, x_low, pltpu.VMEM((length + 8, half), F32), row_f32, row_f32,
            pltpu.VMEM(block_coef, F32), pltpu.VMEM(block_coef, F32), pltpu.VMEM(block_coef, F32),
            row_f32, row_f32, row_low, row_f32, x_low, x_low,
            [pltpu.VMEM((width, half), BF16), pltpu.VMEM((width, half), BF16)]
            + [pltpu.VMEM((array.shape[0], half), array.dtype)
               for array in (state_t, step_proj, decay_t, skip, taps, conv_b, step_b)]
            + [pltpu.VMEM((half, width), BF16)],
            [pltpu.VMEM((states, half), F32), block_f32, block_f32, plain_f32,
             pltpu.VMEM((ROWS_STEP, wide), BF16), pltpu.VMEM((STRETCH * wide, half), BF16)],
            pltpu.SemaphoreType.DMA((11,)), pair_of_sems(2), pair_of_sems(blocks), pair_of_sems(blocks),
            pltpu.SemaphoreType.DMA((9, blocks)), pltpu.SemaphoreType.DMA((3,)),
        ],
        compiler_params=pltpu.CompilerParams(
            vmem_limit_bytes=VMEM_BYTES, collective_id=2, has_side_effects=True
        ),
        cost_estimate=pl.CostEstimate(
            flops=2 * length * states * half * 1000, bytes_accessed=1 << 24, transcendentals=0
        ),
        name="front",
    )(flags, gain_a, layer_input, front_weights)

    vmem_spec = pl.BlockSpec(memory_space=pltpu.VMEM)
    any_spec = pl.BlockSpec(memory_space=pl.ANY)
    token_head = pltpu.VMEM((heads, length, HEAD_DIM), BF16)
    token_head_f32 = pltpu.VMEM((heads, length, HEAD_DIM), F32)
    head_token = pltpu.VMEM((head_cols, length), BF16)
    scores_f32 = pltpu.VMEM((length, QUERY_BLOCK), F32)
    scores_low = pltpu.VMEM((length, QUERY_BLOCK), BF16)
    tokens_low = pltpu.VMEM((length, width), BF16)
    tokens_f32 = pltpu.VMEM((length, width), F32)
    head_low = pltpu.VMEM((length, head_cols), BF16)
    square = pltpu.VMEM((width, head_cols), BF16)
    pack_rows = width + width // 2 + head_cols + half + width
    counts = [("inner", lax.axis_size("inner")), ("dp", lax.axis_size("dp"))]
    attn_rows = width + width // 2 + head_cols
    plan, land = sum_plan(counts, [(0, attn_rows, 1), (0, pack_rows - attn_rows, 0)])
    begun_rows = plan[0][2][0][2]
    base, scan_grad, gate_back, pack_early, g_attn_gain, begun = pl.pallas_call(
        functools.partial(middle_kernel, plan[:1]),
        in_specs=[vmem_spec] * 5 + [any_spec] * 5 + [(any_spec,) * 6],
        out_specs=[any_spec] * 4 + [vmem_spec] * 2,
        out_shape=[
            jax.ShapeDtypeStruct((length, width), F32),
            jax.ShapeDtypeStruct((length, half), F32),
            jax.ShapeDtypeStruct((length, width), F32),
            jax.ShapeDtypeStruct((pack_rows, width), BF16),
            jax.ShapeDtypeStruct((1, width), F32),
            jax.ShapeDtypeStruct((begun_rows, width), BF16),
        ],
        scratch_shapes=[
            tokens_low, pltpu.VMEM((length, half), BF16), pltpu.VMEM((length, half), F32),
            pltpu.VMEM((length, half), F32), tokens_low, square, square, square,
            pltpu.VMEM((head_cols, width), BF16), pltpu.VMEM((half, width), BF16),
            pltpu.VMEM((width, half), BF16),
            tokens_low, head_token, token_head, token_head, token_head, head_token, head_token,
            token_head, head_token, head_token, token_head_f32, token_head_f32, token_head_f32,
            scores_f32, scores_f32, scores_f32, scores_low, scores_low,
            head_low, head_low, head_low, tokens_low, tokens_low, tokens_low, tokens_low, tokens_f32,
            pltpu.VMEM((length, half), F32), tokens_f32, pltpu.VMEM((half, width), F32),
            pltpu.VMEM((width, half), F32), pltpu.VMEM((pack_rows, width), BF16),
            pltpu.VMEM((3 * begun_rows, width), BF16), pair_of_sems(16),
            pltpu.SemaphoreType.DMA((11,)),
            [pltpu.SemaphoreType.DMA((2 * blocks,)), pltpu.SemaphoreType.DMA((2 * blocks,))],
            pltpu.SemaphoreType.DMA((3, blocks)),
        ],
        compiler_params=pltpu.CompilerParams(
            vmem_limit_bytes=VMEM_BYTES, collective_id=3, has_side_effects=True
        ),
        cost_estimate=pl.CostEstimate(
            flops=2 * length * length * width * 10, bytes_accessed=1 << 24, transcendentals=0
        ),
        name="middle",
    )(x, branch, branch_other, first, gain_b, output_grad, gated, gate_z, scan_out, normed_a,
      (query_proj, key_proj, value_proj, mixed_proj, out_proj, in_proj))

    last_rows = width + 144
    plan_last, land_last = sum_plan(
        counts, [(0, width // 2, 0), (0, width // 2, 0), (1, 128, 0), (0, 16, -1)]
    )
    tile_f32 = pltpu.VMEM((2, half // 128, wide, 128), F32)
    tile_low = pltpu.VMEM((2, wide, half), BF16)
    own_f32 = pltpu.VMEM((ROWS_STEP, wide), F32)

    def now(i):
        return jnp.maximum(steps - 1 - i, 0)

    def late_at(i):
        return jnp.minimum(steps - i, steps - 1)

    def back_rows(array, at):
        return (array, (ROWS_STEP, array.shape[1]), lambda i: (at(i), 0))

    def fixed(array):
        return (array, array.shape, None)

    ins = [
        (coef, (None, coefs, ROWS_STEP), lambda i: (now(i), 0, 0)), back_rows(conv_pre, now), back_rows(step_pre, now),
        back_rows(scan_grad, now), back_rows(flags, now),
        (starts, (ROWS_STEP // CHUNK * states, half), lambda i: (now(i), 0)),
        back_rows(conv_pre, late_at), back_rows(conv_in, late_at), back_rows(normed_a, late_at),
        back_rows(flags, late_at), fixed(gain_a), fixed(g_attn_gain), fixed(pack_early), fixed(begun),
    ]
    weights_all = (step_proj, decay_t, skip, state_t, taps, in_proj)
    specs = [
        pl.BlockSpec(block, lambda i: (0, 0), pipeline_mode=pl.Buffered(1)) if at is None
        else pl.BlockSpec(block, at)
        for _, block, at in ins
    ]
    early, late, kept, got = pl.pallas_call(
        functools.partial(back_kernel, plan, plan_last, steps),
        grid=(steps + 1,),
        in_specs=specs + [any_spec] * 3 + [(any_spec,) * len(weights_all)],
        out_specs=[any_spec] * 4,
        out_shape=[
            jax.ShapeDtypeStruct((parts,) + pack_early.shape, BF16),
            jax.ShapeDtypeStruct((parts, last_rows, width), BF16),
            jax.ShapeDtypeStruct((piece_len, width), F32),
            jax.ShapeDtypeStruct((piece_len, width), BF16),
        ],
        scratch_shapes=[pltpu.VMEM((array.shape[0], half), array.dtype) for array in weights_all] + [
            pltpu.SemaphoreType.DMA((len(weights_all),)),
            [pltpu.VMEM((states, half), F32), block_f32,
             block_f32, block_f32, block_f32, pltpu.VMEM((ROWS_STEP, wide), BF16), plain_f32,
             plain_f32, own_f32, own_f32, tile_f32, tile_f32, tile_low, tile_low, tile_low],
            pltpu.VMEM((small_rows, half), F32),
            pltpu.VMEM((2, ROWS_STEP, half), F32),
            pltpu.VMEM((steps, coefs, ROWS_STEP), F32),
            pltpu.VMEM((steps, coefs, ROWS_STEP), F32),
            pltpu.VMEM((ROWS_STEP + 8, half), F32),
            pltpu.VMEM((width, half), F32),
            pltpu.VMEM((128, half), F32),
            pltpu.VMEM((length, half), BF16),
            pltpu.VMEM((length, width), F32),
            pltpu.VMEM((length, width), BF16),
            pltpu.VMEM((length, width), BF16),
            pltpu.VMEM((length, width), BF16),
            pltpu.VMEM((length, width), F32),
            pltpu.VMEM((piece_len, width), F32),
            pltpu.VMEM((piece_len, width), BF16),
            pltpu.VMEM((piece_len, width), BF16),
            pltpu.VMEM((last_rows, width), BF16),
            sum_scratch(plan, pack_early.shape[0], land, width),
            sum_scratch(plan_last, last_rows, land_last, width),
            [pltpu.SemaphoreType.DMA((steps,)), pltpu.SemaphoreType.DMA((steps,))],
            [pltpu.SemaphoreType.DMA((steps,)), pltpu.SemaphoreType.DMA((steps,))],
            [pltpu.SemaphoreType.DMA((16,)), pltpu.SemaphoreType.DMA((16,))],
            pltpu.SemaphoreType.DMA((9,)),
        ],
        compiler_params=pltpu.CompilerParams(
            dimension_semantics=("arbitrary",), vmem_limit_bytes=VMEM_BYTES, collective_id=1,
            has_side_effects=True,
        ),
        cost_estimate=pl.CostEstimate(
            flops=2 * length * states * half * 3000, bytes_accessed=1 << 25, transcendentals=0
        ),
        name="back",
    )(*[a for a, _, _ in ins], x, base, gate_back, weights_all)
    quarter = width // 4
    eighth = width // 8

    def from_sum(total, size, first_row):
        return (total, (parts, size, width), lambda i, sel: (0, first_row // size + i, 0))

    def out_parts(size):
        return ((parts, 4 * size, width), F32, (parts, size, width), lambda i, sel: (0, i, 0))

    results, t_in, t_out, t_query, t_key, t_value, t_mixed, *smalls = call(
        functools.partial(assemble_kernel, (coefs, rank, states)), sel, 4,
        [(kept, (piece_len // 4, width), lambda i, sel: (i, 0)),
         (got, (piece_len // 4, width), lambda i, sel: (i, 0)),
         from_sum(early, quarter, 0), from_sum(early, eighth, width),
         from_sum(early, eighth, width + width // 2), from_sum(early, quarter, attn_rows),
         from_sum(early, quarter, attn_rows + half), from_sum(late, quarter, 0),
         (late, (parts, 128, width), lambda i, sel: (0, width // 128, 0)),
         (late, (parts, 16, width), lambda i, sel: (0, (width + 128) // 16, 0))],
        [((1, 2, piece_len, width), F32, (1, 2, piece_len // 4, width), lambda i, sel: (0, 0, i, 0)),
         ((width, 4 * half), F32, (quarter, 4 * half), lambda i, sel: (i, 0)),
         out_parts(quarter), ((width, width), F32, (quarter, width), lambda i, sel: (i, 0)),
         ((width, width), F32, (quarter, width), lambda i, sel: (i, 0)), out_parts(eighth),
         out_parts(eighth)]
        + [out_whole((size, parts * half)) for size in (coefs, rank, states, 1, 1, 4, 1)]
        + [out_whole((1, width))] * 2,
        [], 0, "assemble",
    )
    t_state, t_step, t_decay, t_step_bias, t_skip, t_taps, t_conv_bias, t_gain, t_attn_gain = smalls
    return (
        results, t_gain[0], t_in, t_taps.T, t_conv_bias[0], t_state.T, t_step, t_step_bias[0],
        t_decay.T, t_skip[0], t_out.reshape(out_proj.shape), t_attn_gain[0], t_query, t_key,
        t_value.reshape(width, width), t_mixed.reshape(width, width),
    )


def solution(mesh):
    in_specs = (P("dp", "inner", None), P("dp", None, None), P("dp", None)) + (P(),) * 15
    out_specs = (P("kind", "dp", "inner", None),) + (P(),) * 15
    return jax.shard_map(local, mesh=mesh, in_specs=in_specs, out_specs=out_specs, check_vma=False)
```

```python
import functools

import jax
import jax.numpy as jnp
from jax import lax
from jax.experimental import pallas as pl
from jax.experimental.pallas import tpu as pltpu
from jax.sharding import PartitionSpec as P

HEAD_DIM = 64
EPS = 1e-05
NEG = -1e30
FAR = 1e30
CHUNK = 16
STRETCH = 8
ROWS_STEP = 256
QUERY_BLOCK = 256
KEY_TILE = 128
VMEM_BYTES = 58 * 1024 * 1024
F32 = jnp.float32
BF16 = jnp.bfloat16


def dot_nn(a, b):
    return lax.dot_general(a, b, (((1,), (0,)), ((), ())), preferred_element_type=F32)


def dot_nt(a, b):
    return lax.dot_general(a, b, (((1,), (1,)), ((), ())), preferred_element_type=F32)


def dot_tn(a, b):
    return lax.dot_general(a, b, (((0,), (0,)), ((), ())), preferred_element_type=F32)


def silu_slope(tensor):
    sigma = jax.nn.sigmoid(tensor)
    return sigma * (1.0 + tensor * (1.0 - sigma))


def rms_scale(tensor):
    return lax.rsqrt(jnp.mean(tensor * tensor, axis=-1, keepdims=True) + EPS)


def softplus(tensor):
    return jnp.maximum(tensor, 0.0) + jnp.log1p(jnp.exp(-jnp.abs(tensor)))


def rms_back(tensor, factor, gain_vec, gradient):
    weighted = gradient * gain_vec
    spread = jnp.mean(weighted * tensor, axis=-1, keepdims=True)
    return factor * weighted - tensor * (factor * factor * factor) * spread


def spread(ref, value):
    for c in range(ref.shape[0]):
        ref[c] = value[:, c * 128 : (c + 1) * 128]


def row_of(ref, c, row, states):
    part = ref[c, pl.ds(row, 8, stride=0), :]
    return jnp.concatenate([part] * (states // 8), axis=0)


def column_of(tile, at):
    return jnp.broadcast_to(tile[:, at : at + 1], tile.shape)


def own_token(chunk, states):
    at = lax.broadcasted_iota(jnp.int32, (chunk, chunk * states), 0)
    of = lax.broadcasted_iota(jnp.int32, (chunk, chunk * states), 1) // states
    return at == of


def state_picks(chunk, states):
    at = lax.broadcasted_iota(jnp.int32, (states, chunk * states), 0)
    of = lax.rem(lax.broadcasted_iota(jnp.int32, (states, chunk * states), 1), states)
    return (at == of).astype(F32).astype(BF16)


def remote(src, dst, sems, number, to):
    return pltpu.make_async_remote_copy(
        src_ref=src, dst_ref=dst, send_sem=sems[0].at[number], recv_sem=sems[1].at[number],
        device_id=to, device_id_type=pl.DeviceIdType.MESH,
    )


def call(body, sel, steps, ins, outs, scratch, flops, name):
    bytes_all = sum(a.size * a.dtype.itemsize for a, _, _ in ins)
    return pl.pallas_call(
        body,
        grid_spec=pltpu.PrefetchScalarGridSpec(
            num_scalar_prefetch=1,
            grid=(steps,),
            in_specs=[pl.BlockSpec(block, at) for _, block, at in ins],
            out_specs=[pl.BlockSpec(block, at) for _, _, block, at in outs],
            scratch_shapes=scratch,
        ),
        out_shape=[jax.ShapeDtypeStruct(shape, dtype) for shape, dtype, _, _ in outs],
        compiler_params=pltpu.CompilerParams(
            dimension_semantics=("arbitrary",), vmem_limit_bytes=VMEM_BYTES
        ),
        cost_estimate=pl.CostEstimate(flops=flops, bytes_accessed=bytes_all, transcendentals=0),
        name=name,
    )(sel, *[a for a, _, _ in ins])


def whole(shape):
    zeros = (0,) * len(shape)
    return (shape, lambda i, sel: zeros)


def scan_block(
    coef, pre, gate, flags, step_w, step_b, decay_t, skip, out_w,
    step_o, scan_o, gated_o, starts_o, branch_o, spare,
):
    state, stepd, drive, ys, blocked, h_low = spare
    block, width = pre.shape
    states = decay_t.shape[0]
    rank = step_w.shape[0]
    tiles = width // 128

    step_pre = dot_tn(coef[:rank, :].astype(BF16), step_w[...]) + step_b[...]
    step_o[...] = step_pre
    step = softplus(step_pre)
    act = pre[...] * jax.nn.sigmoid(pre[...])
    spread(drive, step * act)
    spread(stepd, jnp.where(flags[:, 1:2] > 0.0, step, FAR))
    neg = -jnp.exp(decay_t[...])
    neg_of = [neg[:, c * 128 : (c + 1) * 128] for c in range(tiles)]
    own_all = jnp.concatenate([own_token(CHUNK, states)] * (block // CHUNK), axis=0)
    blocked[...] = jnp.where(
        own_all, dot_tn(coef[rank + states :, :].astype(BF16), state_picks(CHUNK, states)), 0.0
    ).astype(BF16)

    def one_chunk(i, h, h_s):
        here = pl.ds(pl.multiple_of(i * CHUNK, CHUNK), CHUNK)
        tile = coef[rank : rank + states, pl.ds(pl.multiple_of((i // 8) * 128, 128), 128)]
        tile = pltpu.roll(tile, lax.rem(128 - lax.rem(i, 8) * CHUNK, 128), 1)
        for c in range(tiles):
            starts_o[here, c * 128 : (c + 1) * 128] = h[c]
        for at in range(CHUNK):
            row = i * CHUNK + at
            write = column_of(tile, at)
            for c in range(tiles):
                decay = jnp.exp(neg_of[c] * row_of(stepd, c, row, states))
                h[c] = decay * h[c] + row_of(drive, c, row, states) * write
                h_s[at * states : (at + 1) * states, c * 128 : (c + 1) * 128] = h[c].astype(BF16)
        return h

    def stretch(number, carried):
        def pair(step_no, carried):
            h = list(carried)
            for sub in range(2):
                at = 2 * step_no + sub
                spot = h_low.at[pl.ds(pl.multiple_of(at * CHUNK * states, CHUNK * states), CHUNK * states)]
                h = one_chunk(number * STRETCH + at, h, spot)
            return tuple(h)

        carried = lax.fori_loop(0, STRETCH // 2, pair, carried)
        for at in range(STRETCH):
            here = pl.ds(pl.multiple_of((number * STRETCH + at) * CHUNK, CHUNK), CHUNK)
            spot = slice(at * CHUNK * states, (at + 1) * CHUNK * states)
            ys[here, :] = dot_nn(blocked[here, :], h_low[spot, :])
        return carried

    begin = tuple(state[:, c * 128 : (c + 1) * 128] for c in range(tiles))
    for c, last in enumerate(lax.fori_loop(0, block // (STRETCH * CHUNK), stretch, begin)):
        state[:, c * 128 : (c + 1) * 128] = last
    scan_out = ys[...] + skip[...] * act
    scan_o[...] = scan_out
    z = gate[...]
    gated = (scan_out * (z * jax.nn.sigmoid(z))).astype(BF16)
    gated_o[...] = gated
    branch_o[...] = dot_nn(gated, out_w[...]).astype(BF16)


def front_kernel(
    flags, gain, layer_all, weights_all,
    x_o, normed_o, conv_o, pre_o, gate_o, coef_o, step_o, scan_o, gated_o, starts_o, branch_o, branch_other_o,
    x, normed, ext, pre, gate, coef, coef_got, coef_sum, step_pre, scan_out, gated, starts, branch,
    branch_got, weights, scan_spare, load_sems, x_sems, coef_sems, branch_sems, store_sems, late_sems,
):
    length, width = x.shape
    blocks = length // ROWS_STEP
    core, row = lax.axis_index("kind"), lax.axis_index("inner")
    other_core, other_row = {"kind": 1 - core}, {"inner": 1 - row}
    w_conv, w_gate, state_w, step_w, decay_t, skip, taps, conv_b, step_b, out_w = weights
    in_all, state_all, step_all, decay_all, skip_all, taps_all, conv_b_all, step_b_all, out_all = weights_all
    channels = w_conv.shape[1]

    def part_of(number):
        return pl.ds(pl.multiple_of(number * channels, 128), channels)

    def rows_at(b):
        return pl.ds(pl.multiple_of(b * ROWS_STEP, ROWS_STEP), ROWS_STEP)

    mine = part_of(core)
    loads = [
        pltpu.make_async_copy(source, target, load_sems.at[i])
        for i, (source, target) in enumerate((
            (layer_all.at[row], x.at[pl.ds(pl.multiple_of(row * (length // 2), 256), length // 2)]),
            (in_all.at[:, mine], w_conv), (in_all.at[:, part_of(2 + core)], w_gate),
            (state_all.at[:, mine], state_w), (step_all.at[:, mine], step_w),
            (decay_all.at[:, mine], decay_t), (skip_all.at[:, mine], skip), (taps_all.at[:, mine], taps),
            (conv_b_all.at[:, mine], conv_b), (step_b_all.at[:, mine], step_b), (out_all.at[mine], out_w),
        ))
    ]
    barrier = pltpu.get_barrier_semaphore()
    for device in (other_core, other_row):
        pl.semaphore_signal(barrier, inc=1, device_id=device, device_id_type=pl.DeviceIdType.MESH)
    pl.semaphore_wait(barrier, 2)
    sent = remote(
        layer_all.at[1 - row, rows_at(core)], x.at[rows_at(row * (blocks // 2) + core)], x_sems, 0, other_row
    )
    sent.start()
    for load in loads:
        load.start()
    for load in loads:
        load.wait()
    ext[0:8, :] = jnp.zeros((8, channels), F32)
    scan_spare[0][...] = jnp.zeros_like(scan_spare[0])

    results = (
        (x, x_o), (normed, normed_o), (gate, gate_o), (pre, pre_o), (step_pre, step_o),
        (scan_out, scan_o), (gated, gated_o), (starts, starts_o), (branch, branch_o),
    )

    def stores(b, numbers=range(len(results))):
        rows = rows_at(b)
        return [
            pltpu.make_async_copy(results[i][0].at[rows], results[i][1].at[rows], store_sems.at[i, b])
            for i in numbers
        ]

    def project(b):
        rows = rows_at(b)
        u = x[rows, :].astype(F32)
        low = (u * rms_scale(u) * gain[...]).astype(BF16)
        normed[rows, :] = low
        ext[pl.ds(pl.multiple_of(b * ROWS_STEP + 8, 8), ROWS_STEP), :] = dot_nn(low, w_conv[...])
        gate[rows, :] = dot_nn(low, w_gate[...])
        for store in stores(b, range(3)):
            store.start()

    first_other = (1 - row) * (blocks // 2)
    project(row * (blocks // 2))
    project(row * (blocks // 2) + 1)
    sent.wait()
    fetched = x.at[rows_at(first_other + core)]
    passed = remote(fetched, fetched, x_sems, 1, other_core)
    passed.start()
    project(first_other + core)
    passed.wait()
    project(first_other + 1 - core)
    store_conv = pltpu.make_async_copy(ext.at[pl.ds(8, length)], conv_o, late_sems.at[0])
    store_conv.start()

    def coef_copy(b):
        return remote(coef.at[b], coef_got.at[b], coef_sems, b, other_core)

    def branch_copy(b):
        rows = rows_at(b)
        return remote(branch.at[rows], branch_got.at[rows], branch_sems, b, other_core)

    for b in range(blocks):
        rows = slice(b * ROWS_STEP, (b + 1) * ROWS_STEP)
        total = conv_b[...] + taps[3:4, :] * ext[8 + b * ROWS_STEP : 8 + (b + 1) * ROWS_STEP, :]
        for j in range(1, 4):
            moved = ext[8 - j + b * ROWS_STEP : 8 - j + (b + 1) * ROWS_STEP, :]
            total = total + taps[3 - j : 4 - j, :] * jnp.where(flags[rows, j : j + 1] > 0.0, moved, 0.0)
        pre[rows, :] = total
        coef[b] = dot_nt(state_w[...], (total * jax.nn.sigmoid(total)).astype(BF16))
        coef_copy(b).start()
        stores(b, [3])[0].start()

    def scan(b, unused):
        rows = rows_at(b)
        coef_copy(b).wait()
        coef_sum[b] = coef[b] + coef_got[b]
        scan_block(
            coef_sum.at[b], pre.at[rows], gate.at[rows], flags.at[rows], step_w, step_b, decay_t, skip, out_w,
            step_pre.at[rows], scan_out.at[rows], gated.at[rows], starts.at[rows], branch.at[rows],
            scan_spare,
        )
        branch_copy(b).start()
        for store in stores(b, range(4, len(results))):
            store.start()
        return unused

    lax.fori_loop(0, blocks, scan, 0)
    store_coef = pltpu.make_async_copy(coef_sum, coef_o, late_sems.at[1])
    store_coef.start()
    for b in range(blocks):
        branch_copy(b).wait()
    store_other = pltpu.make_async_copy(branch_got, branch_other_o, late_sems.at[2])
    store_other.start()
    for copy in (store_conv, store_coef, store_other):
        copy.wait()
    for b in range(blocks):
        for store in stores(b):
            store.wait()


def middle_kernel(
    x, part_a, part_b, first, gain, grads, gated_all, gate_all, scan_all, normed_all, weights_all,
    base_o, scan_grad_o, back_o, pack_o, gain_grad_o,
    grad, gated, gate, scan_out, normed_a, wq, wk, wv, wm, out_w, w_gate,
    normed, q_t, q_n, k_n, v_n, k_t, v_t, g_n, g_t, o_t, dq_n, dk, dv, bias, expo, prob_grad, prob_low,
    score_low,
    dq_low, dk_low, dv_low, branch, branch_got, back, back_got, base, scan_grad, gate_back, gout, ggate,
    pack, load_sems, pass_sems, store_sems,
):
    length, width = x.shape
    core, row = lax.axis_index("kind"), lax.axis_index("inner")
    other_core = {"kind": 1 - core}
    head_cols, channels = wq.shape[1], out_w.shape[0]

    def part_of(size):
        return pl.ds(pl.multiple_of(core * size, 128), size)

    query_all, key_all, value_all, mixed_all, out_all, in_all = weights_all
    gate_cols = pl.ds(pl.multiple_of((2 + core) * channels, 128), channels)
    loads = [
        pltpu.make_async_copy(source, target, load_sems.at[i])
        for i, (source, target) in enumerate((
            (query_all.at[:, part_of(head_cols)], wq), (key_all.at[:, part_of(head_cols)], wk),
            (value_all.at[:, part_of(head_cols)], wv), (grads.at[row], grad),
            (mixed_all.at[part_of(head_cols)], wm), (gated_all, gated), (gate_all, gate),
            (scan_all, scan_out), (normed_all, normed_a), (out_all.at[part_of(channels)], out_w),
            (in_all.at[:, gate_cols], w_gate),
        ))
    ]
    for load in loads:
        load.start()
    barrier = pltpu.get_barrier_semaphore()
    pl.semaphore_signal(barrier, inc=1, device_id=other_core, device_id_type=pl.DeviceIdType.MESH)
    pl.semaphore_wait(barrier, 1)
    for load in loads[:5]:
        load.wait()

    heads = k_n.shape[0]
    scale = HEAD_DIM**-0.5
    for b in range(length // ROWS_STEP):
        rows = slice(b * ROWS_STEP, (b + 1) * ROWS_STEP)
        middle = x[rows, :].astype(F32) + (part_a[rows, :].astype(F32) + part_b[rows, :].astype(F32))
        normed_blk = (middle * rms_scale(middle) * gain[...]).astype(BF16)
        normed[rows, :] = normed_blk
        query = dot_nn(normed_blk, wq[...]).astype(BF16).astype(F32) * scale
        keys = dot_nn(normed_blk, wk[...]).astype(BF16).astype(F32)
        values = dot_nn(normed_blk, wv[...]).astype(BF16).astype(F32)
        out_grad = dot_nt(grad[rows, :], wm[...]).astype(BF16).astype(F32)
        q_t[:, rows] = query.T.astype(BF16)
        k_t[:, rows] = (keys.T * scale).astype(BF16)
        v_t[:, rows] = values.T.astype(BF16)
        g_t[:, rows] = out_grad.T.astype(BF16)
        for h in range(heads):
            cols = slice(h * HEAD_DIM, (h + 1) * HEAD_DIM)
            q_n[h, rows, :] = query[:, cols].astype(BF16)
            k_n[h, rows, :] = keys[:, cols].astype(BF16)
            v_n[h, rows, :] = values[:, cols].astype(BF16)
            g_n[h, rows, :] = out_grad[:, cols].astype(BF16)
    dk[...] = jnp.zeros_like(dk)
    dv[...] = jnp.zeros_like(dv)

    for block in range(length // QUERY_BLOCK):
        cols = slice(block * QUERY_BLOCK, (block + 1) * QUERY_BLOCK)
        reach = (block + 1) * QUERY_BLOCK
        key_at = lax.broadcasted_iota(jnp.int32, (reach, QUERY_BLOCK), 0)
        query_at = lax.broadcasted_iota(jnp.int32, (reach, QUERY_BLOCK), 1) + block * QUERY_BLOCK
        kept = (key_at >= first[:, cols]) & (key_at <= query_at)
        bias[0:reach, :] = jnp.where(kept, 0.0, NEG)

        def one_head(h, unused):
            dims = pl.ds(pl.multiple_of(h * HEAD_DIM, HEAD_DIM), HEAD_DIM)
            tiles = [slice(t * KEY_TILE, (t + 1) * KEY_TILE) for t in range(reach // KEY_TILE)]

            def by_eight(tile):
                return tile.reshape(KEY_TILE // 8, 8, QUERY_BLOCK)

            query, out_grad = q_t[dims, cols], g_t[dims, cols]
            most = jnp.full((8, QUERY_BLOCK), NEG, F32)
            for keys in tiles:
                scores = dot_nn(k_n[h, keys, :], query) + bias[keys, :]
                expo[keys, :] = scores
                most = jnp.maximum(most, jnp.max(by_eight(scores), axis=0))
            most = jnp.max(most, axis=0, keepdims=True)
            total = jnp.zeros((8, QUERY_BLOCK), F32)
            centre = jnp.zeros((8, QUERY_BLOCK), F32)
            for keys in tiles:
                exponent = jnp.exp(expo[keys, :] - most)
                grads = dot_nn(v_n[h, keys, :], out_grad)
                expo[keys, :] = exponent
                prob_grad[keys, :] = grads
                total = total + jnp.sum(by_eight(exponent), axis=0)
                centre = centre + jnp.sum(by_eight(exponent * grads), axis=0)
            scale_by = 1.0 / jnp.sum(total, axis=0, keepdims=True)
            centre = jnp.sum(centre, axis=0, keepdims=True) * scale_by
            for keys in tiles:
                prob = expo[keys, :] * scale_by
                prob_low[keys, :] = prob.astype(BF16)
                score_low[keys, :] = (prob * (prob_grad[keys, :] - centre)).astype(BF16)
            o_t[dims, cols] = dot_nn(v_t[dims, 0:reach], prob_low[0:reach, :]).astype(BF16)
            dq_n[h, cols, :] = dot_nn(k_t[dims, 0:reach], score_low[0:reach, :]).T
            dk[h, 0:reach, :] += dot_nn(score_low[0:reach, :], q_n[h, cols, :])
            dv[h, 0:reach, :] += dot_nn(prob_low[0:reach, :], g_n[h, cols, :])
            return unused

        lax.fori_loop(0, heads, one_head, 0)

    blocks = length // ROWS_STEP

    def rows_at(b):
        return pl.ds(pl.multiple_of(b * ROWS_STEP, ROWS_STEP), ROWS_STEP)

    def back_copy(b):
        return remote(back.at[rows_at(b)], back_got.at[rows_at(b)], pass_sems, b, other_core)

    def branch_copy(b):
        there = branch_got.at[rows_at(b)]
        return remote(branch.at[rows_at(b)], there, pass_sems, blocks + b, other_core)

    def partials(b, unused):
        rows = rows_at(b)
        for target, source in ((dq_low, dq_n), (dk_low, dk), (dv_low, dv)):
            joined = jnp.concatenate([source[h, rows, :] for h in range(heads)], axis=1)
            target[rows, :] = joined.astype(BF16)
        total = dot_nt(dq_low[rows, :], wq[...]) + dot_nt(dk_low[rows, :], wk[...])
        back[rows, :] = (total + dot_nt(dv_low[rows, :], wv[...])).astype(BF16)
        back_copy(b).start()
        branch[rows, :] = dot_tn(o_t[:, rows], wm[...]).astype(BF16)
        branch_copy(b).start()
        return unused

    lax.fori_loop(0, blocks, partials, 0)
    cut = width // 2
    attn_rows = width + cut + head_cols
    pack[0:width, 0:head_cols] = dot_tn(normed[...], dq_low[...]).astype(BF16)
    pack[0:width, head_cols:] = dot_tn(normed[...], dk_low[...]).astype(BF16)
    value_grad = dot_tn(normed[...], dv_low[...]).astype(BF16)
    pack[width : width + cut, 0:head_cols] = value_grad[:cut]
    pack[width : width + cut, head_cols:] = value_grad[cut:]
    pack[width + cut : attn_rows, :] = dot_nn(o_t[...], grad[...]).astype(BF16)
    for load in loads[5:]:
        load.wait()
    gout[...] = jnp.zeros_like(gout)
    ggate[...] = jnp.zeros_like(ggate)
    gain_grad_o[...] = jnp.zeros_like(gain_grad_o)

    def stores(b):
        rows = rows_at(b)
        return [
            pltpu.make_async_copy(source.at[rows], target.at[rows], store_sems.at[i, b])
            for i, (source, target) in enumerate(
                ((base, base_o), (scan_grad, scan_grad_o), (gate_back, back_o))
            )
        ]

    def gating(b, unused):
        rows = rows_at(b)
        back_copy(b).wait()
        branch_copy(b).wait()
        middle = x[rows, :].astype(F32) + (part_a[rows, :].astype(F32) + part_b[rows, :].astype(F32))
        total = back[rows, :].astype(F32) + back_got[rows, :].astype(F32)
        factor = rms_scale(middle)
        middle_grad = grad[rows, :].astype(F32) + rms_back(middle, factor, gain[...], total)
        gain_grad_o[...] += jnp.sum(total * middle * factor, axis=0, keepdims=True)
        layer_out = middle + (branch[rows, :].astype(F32) + branch_got[rows, :].astype(F32))
        chosen = (1 - core).astype(F32)
        base[rows, :] = chosen * middle_grad + (1.0 - chosen) * layer_out
        low = middle_grad.astype(BF16)
        gout[...] += dot_tn(gated[rows, :], low)
        gated_grad = dot_nt(low, out_w[...])
        z = gate[rows, :]
        sigma = jax.nn.sigmoid(z)
        scan_grad[rows, :] = gated_grad * (z * sigma)
        slope = sigma * (1.0 + z * (1.0 - sigma))
        gate_low = (gated_grad * scan_out[rows, :] * slope).astype(BF16)
        ggate[...] += dot_tn(normed_a[rows, :], gate_low)
        gate_back[rows, :] = dot_nt(gate_low, w_gate[...])
        for store in stores(b):
            store.start()
        return unused

    lax.fori_loop(0, blocks, gating, 0)
    pack[attn_rows : attn_rows + channels, :] = gout[...].astype(BF16)
    pack[attn_rows + channels :, :] = ggate[...].astype(BF16)
    last = pltpu.make_async_copy(pack, pack_o, load_sems.at[0])
    last.start()
    for b in range(blocks):
        for store in stores(b):
            store.wait()
    last.wait()


def scan_back_block(
    coef, pre, step_in, scan_grad, flags, starts, step_w, decay_t, skip,
    act_grad, coef_grad, small, spare, between,
):
    state, steps, stepd, drive, reads, blocked, d_drive, d_expo, *pair_spare = spare
    block, width = pre.shape
    states = decay_t.shape[0]
    rank = step_w.shape[0]
    tiles = width // 128
    wide = CHUNK * states

    step_pre = step_in[...]
    step = softplus(step_pre)
    act = pre[...] * jax.nn.sigmoid(pre[...])
    spread(steps, step)
    spread(drive, step * act)
    spread(stepd, jnp.where(flags[:, 1:2] > 0.0, step, FAR))
    spread(reads, scan_grad[...])
    neg = -jnp.exp(decay_t[...])
    neg_of = [neg[:, c * 128 : (c + 1) * 128] for c in range(tiles)]
    picks = state_picks(CHUNK, states)
    own = own_token(CHUNK, states)
    own_low = own.astype(F32).astype(BF16)
    ones = jnp.ones((128, 128), BF16)
    coef_grad[rank:, :] = jnp.zeros((2 * states, block), F32)
    own_all = jnp.concatenate([own] * (block // CHUNK), axis=0)
    blocked[...] = jnp.where(
        own_all, dot_tn(coef[rank : rank + states, :].astype(BF16), picks), 0.0
    ).astype(BF16)

    def one_chunk(i, backward, spare):
        decay_s, decayed_s, sum_s, expo_s, in_s, read_s = spare
        rows16 = pl.ds(pl.multiple_of(i * CHUNK, CHUNK), CHUNK)
        tile = coef[rank:, pl.ds(pl.multiple_of((i // 8) * 128, 128), 128)]
        tile = pltpu.roll(tile, lax.rem(128 - lax.rem(i, 8) * CHUNK, 128), 1)
        h = [starts[rows16, c * 128 : (c + 1) * 128] for c in range(tiles)]
        for at in range(CHUNK):
            row = i * CHUNK + at
            here = slice(at * states, (at + 1) * states)
            write = column_of(tile[:states], at)
            for c in range(tiles):
                cols = slice(c * 128, (c + 1) * 128)
                decay = jnp.exp(neg_of[c] * row_of(stepd, c, row, states))
                kept = decay * h[c]
                decay_s[c, here, :] = decay
                h[c] = kept + row_of(drive, c, row, states) * write
                decayed_s[c, here, :] = kept
                part = h[c] * row_of(reads, c, row, states)
                reading = part if c == 0 else reading + part
            read_s[here, :] = reading.astype(BF16)
        total = [jnp.zeros((states, 128), F32)] * tiles
        for at in reversed(range(CHUNK)):
            row = i * CHUNK + at
            here = slice(at * states, (at + 1) * states)
            read = column_of(tile[states:], at)
            for c in range(tiles):
                cols = slice(c * 128, (c + 1) * 128)
                summed = read * row_of(reads, c, row, states) + backward[c]
                sum_s[here, cols] = summed.astype(BF16)
                expo = summed * decayed_s[c, here, :]
                expo_s[here, cols] = (expo * neg_of[c]).astype(BF16)
                total[c] = total[c] + expo * row_of(steps, c, row, states)
                backward[c] = decay_s[c, here, :] * summed
                part = summed * row_of(drive, c, row, states)
                writing = part if c == 0 else writing + part
            in_s[here, :] = writing.astype(BF16)
        for c in range(tiles):
            small[rank : rank + states, c * 128 : (c + 1) * 128] += total[c]

        d_drive[rows16, :] = dot_nn(blocked[rows16, :], sum_s[...])
        d_expo[rows16, :] = dot_nn(own_low, expo_s[...])
        lanes = pl.ds(pl.multiple_of((i // 8) * 128, 128), 128)
        own_lane = lax.broadcasted_iota(jnp.int32, (states, 128), 1) - lax.rem(i, 8) * CHUNK
        for low_s, at_row in ((in_s, rank), (read_s, rank + states)):
            lane_sums = dot_nn(low_s[...], ones)
            placed = jnp.zeros((states, 128), F32)
            for at in range(CHUNK):
                placed = jnp.where(own_lane == at, lane_sums[at * states : (at + 1) * states, :], placed)
            coef_grad[at_row : at_row + states, lanes] += placed
        return backward

    def pair(step_no, carried):
        between(step_no)
        backward = list(carried)
        last = block // CHUNK - 1 - 2 * step_no
        for sub in range(2):
            backward = one_chunk(last - sub, backward, pair_spare[sub])
        return tuple(backward)

    begin = tuple(state[:, c * 128 : (c + 1) * 128] for c in range(tiles))
    for c, last in enumerate(lax.fori_loop(0, block // (2 * CHUNK), pair, begin)):
        state[:, c * 128 : (c + 1) * 128] = last

    drive_grad = d_drive[...]
    pre_grad = (d_expo[...] + drive_grad * act) * jax.nn.sigmoid(step_pre)
    tail = rank + states
    small[tail : tail + 1, :] += jnp.sum(pre_grad, axis=0, keepdims=True)
    pre_low = pre_grad.astype(BF16)
    small[:rank, :] += dot_nn(coef[:rank, :].astype(BF16), pre_low)
    coef_grad[:rank, :] = dot_nt(step_w[...], pre_low)
    act_grad[...] = drive_grad * step + scan_grad[...] * skip[...]
    small[tail + 1 : tail + 2, :] += jnp.sum(scan_grad[...] * act, axis=0, keepdims=True)


def conv_back_block(
    coef_grad, pre, act_grad, conv_in, normed, flags, state_w, taps, ext, gconv, gsmall, mix_low, taps_at,
):
    block = pre.shape[0]
    coefs = coef_grad.shape[0]
    v = pre[...]
    sigma = jax.nn.sigmoid(v)
    gsmall[0:coefs, :] += dot_nn(coef_grad, (v * sigma).astype(BF16))
    act_all = act_grad[...] + dot_tn(coef_grad, state_w[...])
    conv_grad = act_all * (sigma * (1.0 + v * (1.0 - sigma)))
    ext[0:block, :] = conv_grad
    conv_in_grad = taps[3:4, :] * conv_grad
    sums = [None] * 4
    sums[3] = jnp.sum(conv_grad * conv_in[...], axis=0, keepdims=True)
    for j in range(1, 4):
        moved = jnp.where(flags[:, 4 + j : 5 + j] > 0.0, ext[j : j + block, :], 0.0)
        sums[3 - j] = jnp.sum(moved * conv_in[...], axis=0, keepdims=True)
        conv_in_grad = conv_in_grad + taps[3 - j : 4 - j, :] * moved
    for j in range(4):
        gsmall[taps_at + j : taps_at + j + 1, :] += sums[j]
    gsmall[taps_at + 4 : taps_at + 5, :] += jnp.sum(conv_grad, axis=0, keepdims=True)
    low = conv_in_grad.astype(BF16)
    gconv[...] += dot_tn(normed[...], low)
    mix_low[...] = low
    ext[block:, :] = ext[0:8, :]


def sum_digits(counts):
    bits = [(axis, 1 << i) for axis, size in counts for i in range(size.bit_length() - 1)]
    return [bits[i : i + 2] for i in range(0, len(bits), 2)]


def sum_plan(counts, parts):
    digits = sum_digits(counts)
    streams, at, land = [], 0, 0
    for number, size, lead in parts:
        turn = number % len(digits)
        steps, held = [], size
        for digit in digits[turn:] + digits[:turn]:
            radix = 1 << len(digit)
            split = held % (16 * radix) == 0
            held = held // radix if split else held
            steps.append((digit, split, held, land))
            land += held * (radix - 1)
        streams.append((at, size, steps, lead))
        at += size
    return streams, land


class Summing:
    def __init__(self, plan, src, work, land, full, peer, send, recv):
        self.streams, self.src, self.work, self.land = plan, src, work, land
        self.full, self.peer = full, peer
        self.sems = (send, recv)
        self.turns = len(plan[0][2])
        self.phases = 2 * self.turns + 2 - min(0, *(lead for _, _, _, lead in plan))
        self.start = []
        for first, _, steps, _ in plan:
            at, spots = first, [first]
            for turn, (digit, split, kept, _) in enumerate(steps):
                at = at + self.index(digit, 0) * kept if split else at
                spots.append(at)
            self.start.append(spots)

    def index(self, digit, flipped):
        total = 0
        for i, (axis, weight) in enumerate(digit):
            place = lax.rem(lax.axis_index(axis) // weight, 2)
            total = total + (1 - place if flipped >> i & 1 else place) * (1 << i)
        return total

    def partner(self, digit, flipped):
        device = {}
        for i, (axis, weight) in enumerate(digit):
            if flipped >> i & 1:
                me = lax.axis_index(axis)
                device[axis] = device.get(axis, me) + weight * (1 - 2 * lax.rem(me // weight, 2))
        return device

    def other_core(self):
        return {"kind": 1 - lax.axis_index("kind")}

    def others(self, s, turn):
        return range(1, 1 << len(self.streams[s][2][turn][0]))

    def rows(self, ref, at, size):
        return ref.at[pl.ds(pl.multiple_of(at, 16), size)]

    def number(self, s, kind, turn, flipped):
        return ((s * 3 + kind) * (self.turns + 1) + turn) * 4 + flipped

    def piece(self, s, turn, flipped):
        digit, split, kept, _ = self.streams[s][2][turn]
        at = self.start[s][turn]
        return at + self.index(digit, flipped) * kept if split else at

    def halves(self, s, turn):
        digit, _, kept, land = self.streams[s][2][turn]
        source = self.src if turn == 0 else self.work
        return [
            remote(
                self.rows(source, self.piece(s, turn, q), kept),
                self.land.at[pl.ds(land + (q - 1) * kept, kept)],
                self.sems, self.number(s, 0, turn, q), self.partner(digit, q),
            )
            for q in self.others(s, turn)
        ]

    def add(self, s, turn):
        target = self.full if turn == self.turns - 1 else self.work
        self.add_to(target, self.start[s][turn + 1], s, turn)

    def add_to(self, target, first, s, turn):
        _, _, kept, land = self.streams[s][2][turn]
        at = self.start[s][turn + 1]
        source = self.src if turn == 0 else self.work

        def step(i, unused):
            here = pl.ds(pl.multiple_of(at + i * 16, 16), 16)
            parts = [source[here, :].astype(F32)]
            for q in self.others(s, turn):
                there = pl.ds(pl.multiple_of(land + (q - 1) * kept + i * 16, 16), 16)
                parts.append(self.land[there, :].astype(F32))
            while len(parts) > 1:
                parts = [parts[i] + parts[i + 1] for i in range(0, len(parts), 2)]
            target[pl.ds(pl.multiple_of(first + i * 16, 16), 16), :] = parts[0].astype(BF16)
            return unused

        lax.fori_loop(0, kept // 16, step, 0)

    def spreads(self, s, turn):
        digit, split, kept, _ = self.streams[s][2][turn]
        if not split:
            return []
        here = self.rows(self.full, self.start[s][turn + 1], kept)
        return [
            remote(here, here, self.sems, self.number(s, 1, turn, q), self.partner(digit, q))
            for q in self.others(s, turn)
        ]

    def shares(self, s, turn):
        if turn == self.turns:
            found = [(0, self.start[s][turn], self.streams[s][2][-1][2])]
        else:
            _, split, kept, _ = self.streams[s][2][turn]
            found = [(q, self.piece(s, turn, q), kept) for q in self.others(s, turn)] if split else []
        return [
            remote(
                self.rows(self.full, at, size), self.rows(self.peer, at, size), self.sems,
                self.number(s, 2, turn, q), self.other_core(),
            )
            for q, at, size in found
        ]

    def greet(self):
        barrier = pltpu.get_barrier_semaphore()
        partners = [self.other_core()]
        for digit, _, _, _ in self.streams[0][2]:
            partners += [self.partner(digit, q) for q in range(1, 1 << len(digit))]
        for device in partners:
            pl.semaphore_signal(
                barrier, inc=1, device_id=device, device_id_type=pl.DeviceIdType.MESH
            )
        pl.semaphore_wait(barrier, len(partners))

    def begin(self, copies):
        for copy in copies:
            copy.start()

    def finish(self, copies):
        for copy in copies:
            copy.wait()

    def phase(self, number):
        for s, (_, _, _, lead) in enumerate(self.streams):
            at = number + lead
            if number == self.phases - 1:
                for turn in range(self.turns + 1):
                    self.finish(self.shares(s, turn))
            elif at == 0:
                self.begin(self.halves(s, 0))
            elif 0 < at <= self.turns:
                self.finish(self.halves(s, at - 1))
                self.add(s, at - 1)
                if at < self.turns:
                    self.begin(self.halves(s, at))
                else:
                    self.begin(self.spreads(s, self.turns - 1))
                    self.begin(self.shares(s, self.turns))
            elif self.turns < at <= 2 * self.turns:
                turn = 2 * self.turns - at
                self.finish(self.spreads(s, turn))
                if turn > 0:
                    self.begin(self.spreads(s, turn - 1))
                self.begin(self.shares(s, turn))


def sum_scratch(plan, rows, land, width):
    numbers = len(plan) * 3 * (len(plan[0][2]) + 1) * 4
    return [
        pltpu.VMEM((rows, width), BF16),
        pltpu.VMEM((land, width), BF16),
        pltpu.VMEM((rows, width), BF16),
        pltpu.VMEM((rows, width), BF16),
        pltpu.SemaphoreType.DMA((numbers,)),
        pltpu.SemaphoreType.DMA((numbers,)),
    ]


def both_copies(summing, out, sems, number):
    core = lax.axis_index("kind")
    return [
        pltpu.make_async_copy(summing.full, out.at[core], sems.at[number]),
        pltpu.make_async_copy(summing.peer, out.at[1 - core], sems.at[number + 1]),
    ]


def back_kernel(
    plan, plan_last, steps,
    coef, pre, step_in, scan_grad, flags, starts,
    pre_late, conv_in, normed, flags_late,
    gain, gain_grad, pack, x_all, base_all, gate_back_all, weights_all,
    early_o, late_o, kept_o, got_o,
    step_w, decay_t, skip, state_w, taps, w_conv, weight_sems,
    scan_spare, small, act_grads, coef_grads, coef_got, ext, gconv, gsmall, mix_low, back, low, low_got,
    x_s, base_s, kept, sent, got, pack_last, sum_spare, sum_spare_last,
    coef_sems, low_sems, pass_sems, local_sems,
):
    pid = pl.program_id(0)
    states, rank, coefs = decay_t.shape[0], step_w.shape[0], state_w.shape[0]
    block = pre.shape[0]
    pairs = block // (2 * CHUNK)
    taps_at = coefs + small.shape[0]
    core, row = lax.axis_index("kind"), lax.axis_index("inner")
    other_core = {"kind": 1 - core}
    first_sum = Summing(plan, pack, *sum_spare)
    last_sum = Summing(plan_last, pack_last, *sum_spare_last)
    slots = [share * pairs * steps // 32 for share in (0, 13, 20, 28)]
    load_x = pltpu.make_async_copy(x_all, x_s, local_sems.at[0])
    load_base = pltpu.make_async_copy(base_all, base_s, local_sems.at[1])
    load_back = pltpu.make_async_copy(gate_back_all, back, local_sems.at[8])
    mine = pl.ds(pl.multiple_of(core * w_conv.shape[1], 128), w_conv.shape[1])
    load_weights = [
        pltpu.make_async_copy(source.at[:, mine], target, weight_sems.at[i])
        for i, (source, target) in enumerate(
            zip(weights_all, (step_w, decay_t, skip, state_w, taps, w_conv), strict=True)
        )
    ]

    def coef_copy(i):
        return remote(coef_grads.at[i], coef_got.at[i], coef_sems, i, other_core)

    def low_copy(i):
        here = pl.ds(pl.multiple_of((steps - 1 - i) * block, block), block)
        return remote(low.at[here], low_got.at[here], low_sems, i, other_core)

    def first_phase(number):
        first_sum.phase(number)

    @pl.when(pid == 0)
    def _():
        scan_spare[0][...] = jnp.zeros_like(scan_spare[0])
        small[...] = jnp.zeros_like(small)
        ext[block:, :] = jnp.zeros((8, ext.shape[1]), F32)
        gconv[...] = jnp.zeros_like(gconv)
        gsmall[...] = jnp.zeros_like(gsmall)
        for copy in load_weights:
            copy.start()
        first_sum.greet()
        load_x.start()
        load_base.start()
        load_back.start()
        for copy in load_weights:
            copy.wait()

    @pl.when(pid < steps)
    def _():
        def between(step_no):
            slot = pid * pairs + step_no
            for number, at in enumerate(slots):
                pl.when(slot == at)(functools.partial(first_phase, number))

        scan_back_block(
            coef, pre, step_in, scan_grad, flags, starts, step_w, decay_t, skip,
            act_grads.at[lax.rem(pid, 2)], coef_grads.at[pid], small, scan_spare, between,
        )
        coef_copy(pid).start()

    @pl.when(pid > 0)
    def _():
        late = pid - 1
        coef_copy(late).wait()
        coef_low = (coef_grads[late] + coef_got[late]).astype(BF16)
        here = pl.ds(pl.multiple_of((steps - 1 - late) * block, block), block)
        conv_back_block(
            coef_low, pre_late, act_grads.at[lax.rem(late, 2)], conv_in, normed, flags_late, state_w,
            taps, ext, gconv, gsmall, mix_low.at[here], taps_at,
        )

    @pl.when(pid == steps)
    def _():
        width = gconv.shape[0]
        small[rank : rank + states, :] = small[rank : rank + states, :] * -jnp.exp(decay_t[...])
        gsmall[coefs:taps_at, :] = small[...]
        gsmall[taps_at + 6 : taps_at + 7, :] = gain_grad[...]
        pack_last[0:width, :] = gconv[...].astype(BF16)
        pack_last[width : width + 128, :] = gsmall[...].astype(BF16)
        last_sum.phase(0)
        load_x.wait()
        load_back.wait()
        gain_sum = jnp.zeros((1, width), F32)
        for i in range(steps):
            here = slice((steps - 1 - i) * block, (steps - i) * block)
            total = back[here, :] + dot_nt(mix_low[here, :], w_conv[...])
            back[here, :] = total
            low[here, :] = total.astype(BF16)
            low_copy(i).start()
            u = x_s[here, :].astype(F32)
            gain_sum += jnp.sum(total * u * rms_scale(u), axis=0, keepdims=True)
        pack_last[width + 128 :, :] = jnp.concatenate(
            [gain_sum, jnp.zeros((15, width), F32)], axis=0
        ).astype(BF16)
        for number in range(len(slots), first_sum.phases - 1):
            first_sum.phase(number)
        last_sum.phase(1)
        for i in range(steps):
            low_copy(i).wait()
        load_base.wait()
        chosen = (1 - core).astype(F32)
        half = kept.shape[0]

        def finish(at, target):
            def part(i, unused):
                here = pl.ds(pl.multiple_of(at + i * 64, 64), 64)
                there = pl.ds(pl.multiple_of(i * 64, 64), 64)
                u = x_s[here, :].astype(F32)
                total = back[here, :] + low_got[here, :].astype(F32)
                backward = rms_back(u, rms_scale(u), gain[...], total)
                target[there, :] = (base_s[here, :] + chosen * backward).astype(target.dtype)
                return unused

            lax.fori_loop(0, half // 64, part, 0)

        finish((1 - row) * half, sent)
        pieces = 4
        passing = [
            remote(
                sent.at[pl.ds(i * (half // pieces), half // pieces)],
                got.at[pl.ds(i * (half // pieces), half // pieces)], pass_sems, i, {"inner": 1 - row},
            )
            for i in range(pieces)
        ]
        finish(row * half, kept)
        keep = pltpu.make_async_copy(kept, kept_o, local_sems.at[2])
        keep.start()
        first_sum.phase(first_sum.phases - 1)
        store_first = both_copies(first_sum, early_o, local_sems, 3)
        for copy in store_first:
            copy.start()
        for number in range(2, last_sum.phases):
            last_sum.phase(number)
            if number - 2 < pieces:
                passing[number - 2].start()
        store_last = both_copies(last_sum, late_o, local_sems, 5)
        for copy in passing:
            copy.wait()
        store_got = pltpu.make_async_copy(got, got_o, local_sems.at[7])
        store_got.start()
        for copy in store_last:
            copy.start()
        for copy in store_first + store_last + [keep, store_got]:
            copy.wait()


def assemble_kernel(
    sizes, sel, kept, got, query_key, value, mixed, out, gate, conv, small, gains,
    results_o, in_o, out_o, query_o, key_o, value_o, mixed_o,
    state_o, step_o, decay_o, step_bias_o, skip_o, taps_o, conv_bias_o, gain_o, attn_gain_o,
):
    first = sel[1] == 0
    mine, other = kept[...], got[...].astype(F32)
    results_o[0, 0] = jnp.where(first, mine, other)
    results_o[0, 1] = jnp.where(first, other, mine)
    half = conv.shape[2]
    cut = query_key.shape[2] // 2
    for part in range(2):
        here = slice(part * cut, (part + 1) * cut)
        in_o[:, part * half : (part + 1) * half] = conv[part].astype(F32)
        in_o[:, (2 + part) * half : (3 + part) * half] = gate[part].astype(F32)
        query_o[:, here] = query_key[part, :, :cut].astype(F32)
        key_o[:, here] = query_key[part, :, cut:].astype(F32)
        value_o[0, :, here] = value[part, :, :cut].astype(F32)
        value_o[1, :, here] = value[part, :, cut:].astype(F32)
    out_o[...] = out[...].astype(F32)
    mixed_o[...] = mixed[...].astype(F32)
    both = jnp.concatenate([small[0].astype(F32), small[1].astype(F32)], axis=1)
    coefs, rank, states = sizes
    at = 0
    for target, size in (
        (state_o, coefs), (step_o, rank), (decay_o, states), (step_bias_o, 1), (skip_o, 1),
        (None, 6), (taps_o, 4), (conv_bias_o, 1),
    ):
        if target is not None:
            target[...] = both[at : at + size]
        at += size
    gain_o[...] = gains[0, 0:1].astype(F32) + gains[1, 0:1].astype(F32)
    attn_gain_o[...] = both[at + 1 : at + 2, :half]


def local(
    layer_input, output_grad, document_ids, mamba_gain, in_proj, conv_weight, conv_bias, state_proj,
    step_proj, step_bias, decay_log, skip_gain, out_proj, attn_gain, query_proj, key_proj, value_proj,
    mixed_proj,
):
    _, piece_len, width = layer_input.shape
    length = output_grad.shape[1]
    parts = lax.axis_size("kind")
    half = in_proj.shape[1] // (2 * parts)
    states = decay_log.shape[1]
    rank = step_proj.shape[0]
    coefs = state_proj.shape[1]
    head_cols = width // parts
    heads = head_cols // HEAD_DIM
    core = lax.axis_index("kind")
    row = lax.axis_index("inner")
    sel = jnp.stack([core, row]).astype(jnp.int32)
    steps = length // ROWS_STEP

    def swap(value, axis):
        return jax.tree.map(lambda v: lax.ppermute(v, axis, [(0, 1), (1, 0)]), value)

    ids = lax.dynamic_index_in_dim(document_ids, row, 0, keepdims=False)
    first = jnp.sum((ids[None, :] < ids[:, None]).astype(jnp.int32), axis=1)
    since = jnp.arange(length, dtype=jnp.int32) - first
    after = jnp.concatenate([since, jnp.zeros((4,), jnp.int32)])
    flags = jnp.stack(
        [since >= j for j in range(4)] + [after[j : j + length] >= max(j, 1) for j in range(4)],
        axis=1,
    ).astype(F32)
    first = first[None, :]
    taps = conv_weight.T
    state_t = state_proj.T
    decay_t = decay_log.T
    conv_b, step_b, skip = conv_bias[None, :], step_bias[None, :], skip_gain[None, :]
    gain_a, gain_b = mamba_gain[None, :], attn_gain[None, :]

    def rows(array):
        return (array, (ROWS_STEP, array.shape[1]), lambda i, sel: (i, 0))

    def rows_rev(array):
        return (array, (ROWS_STEP, array.shape[1]), lambda i, sel: (steps - 1 - i, 0))

    def cols(array):
        return (array, (array.shape[0], ROWS_STEP), lambda i, sel: (0, i))

    def cols_rev(array):
        return (array, (array.shape[0], ROWS_STEP), lambda i, sel: (0, steps - 1 - i))

    def full(array):
        return (array,) + whole(array.shape)

    def half_cols(array, size, shift=0):
        return (array, (array.shape[0], size), lambda i, sel: (0, sel[0] + shift))

    def half_rows(array, size):
        return (array, (size, array.shape[1]), lambda i, sel: (sel[0], 0))

    def out_rows(size, dtype):
        return ((length, size), dtype, (ROWS_STEP, size), lambda i, sel: (i, 0))

    def out_rows_rev(size, dtype):
        return ((length, size), dtype, (ROWS_STEP, size), lambda i, sel: (steps - 1 - i, 0))

    def out_whole(shape, dtype=F32):
        return (shape, dtype) + whole(shape)

    w_conv = half_cols(in_proj, half)
    w_gate = half_cols(in_proj, half, parts)
    taps_half = half_cols(taps, half)
    state_half = half_cols(state_t, half)
    step_half = half_cols(step_proj, half)
    decay_half = half_cols(decay_t, half)
    skip_half = half_cols(skip, half)
    out_half = half_rows(out_proj, half)

    small_rows = rank + states + 8
    block_f32 = pltpu.VMEM((half // 128, ROWS_STEP, 128), F32)
    plain_f32 = pltpu.VMEM((ROWS_STEP, half), F32)
    wide = CHUNK * states
    blocks = length // ROWS_STEP
    assert length // CHUNK * states == length
    row_outs = [
        (width, BF16), (width, BF16), (half, F32), (half, F32), (half, F32), None, (half, F32), (half, F32),
        (half, BF16), (half, F32), (width, BF16), (width, BF16),
    ]
    row_f32, row_low = pltpu.VMEM((length, half), F32), pltpu.VMEM((length, half), BF16)
    x_low = pltpu.VMEM((length, width), BF16)
    block_coef = (blocks, coefs, ROWS_STEP)
    front_weights = (in_proj, state_t, step_proj, decay_t, skip, taps, conv_b, step_b, out_proj)

    def pair_of_sems(count):
        return [pltpu.SemaphoreType.DMA((count,)), pltpu.SemaphoreType.DMA((count,))]

    (x, normed_a, conv_in, conv_pre, gate_z, coef, step_pre, scan_out, gated, starts, branch,
     branch_other) = pl.pallas_call(
        front_kernel,
        in_specs=[pl.BlockSpec(memory_space=pltpu.VMEM)] * 2 + [pl.BlockSpec(memory_space=pl.ANY)]
        + [(pl.BlockSpec(memory_space=pl.ANY),) * len(front_weights)],
        out_specs=[pl.BlockSpec(memory_space=pl.ANY)] * len(row_outs),
        out_shape=[
            jax.ShapeDtypeStruct(block_coef, F32) if out is None
            else jax.ShapeDtypeStruct((length, out[0]), out[1])
            for out in row_outs
        ],
        scratch_shapes=[
            x_low, x_low, pltpu.VMEM((length + 8, half), F32), row_f32, row_f32,
            pltpu.VMEM(block_coef, F32), pltpu.VMEM(block_coef, F32), pltpu.VMEM(block_coef, F32),
            row_f32, row_f32, row_low, row_f32, x_low, x_low,
            [pltpu.VMEM((width, half), BF16), pltpu.VMEM((width, half), BF16)]
            + [pltpu.VMEM((array.shape[0], half), array.dtype)
               for array in (state_t, step_proj, decay_t, skip, taps, conv_b, step_b)]
            + [pltpu.VMEM((half, width), BF16)],
            [pltpu.VMEM((states, half), F32), block_f32, block_f32, plain_f32,
             pltpu.VMEM((ROWS_STEP, wide), BF16), pltpu.VMEM((STRETCH * wide, half), BF16)],
            pltpu.SemaphoreType.DMA((11,)), pair_of_sems(2), pair_of_sems(blocks), pair_of_sems(blocks),
            pltpu.SemaphoreType.DMA((9, blocks)), pltpu.SemaphoreType.DMA((3,)),
        ],
        compiler_params=pltpu.CompilerParams(
            vmem_limit_bytes=VMEM_BYTES, collective_id=2, has_side_effects=True
        ),
        cost_estimate=pl.CostEstimate(
            flops=2 * length * states * half * 1000, bytes_accessed=1 << 24, transcendentals=0
        ),
        name="front",
    )(flags, gain_a, layer_input, front_weights)

    vmem_spec = pl.BlockSpec(memory_space=pltpu.VMEM)
    any_spec = pl.BlockSpec(memory_space=pl.ANY)
    token_head = pltpu.VMEM((heads, length, HEAD_DIM), BF16)
    token_head_f32 = pltpu.VMEM((heads, length, HEAD_DIM), F32)
    head_token = pltpu.VMEM((head_cols, length), BF16)
    scores_f32 = pltpu.VMEM((length, QUERY_BLOCK), F32)
    scores_low = pltpu.VMEM((length, QUERY_BLOCK), BF16)
    tokens_low = pltpu.VMEM((length, width), BF16)
    tokens_f32 = pltpu.VMEM((length, width), F32)
    head_low = pltpu.VMEM((length, head_cols), BF16)
    square = pltpu.VMEM((width, head_cols), BF16)
    pack_rows = width + width // 2 + head_cols + half + width
    counts = [("inner", lax.axis_size("inner")), ("dp", lax.axis_size("dp"))]
    attn_rows = width + width // 2 + head_cols
    most = (pack_rows * 13 // 20 + 128) // 256 * 256
    plan, land = sum_plan(counts, [(0, most, 0), (1, pack_rows - most, 0)])
    base, scan_grad, gate_back, pack_early, g_attn_gain = pl.pallas_call(
        middle_kernel,
        in_specs=[vmem_spec] * 5 + [any_spec] * 5 + [(any_spec,) * 6],
        out_specs=[any_spec] * 4 + [vmem_spec],
        out_shape=[
            jax.ShapeDtypeStruct((length, width), F32),
            jax.ShapeDtypeStruct((length, half), F32),
            jax.ShapeDtypeStruct((length, width), F32),
            jax.ShapeDtypeStruct((pack_rows, width), BF16),
            jax.ShapeDtypeStruct((1, width), F32),
        ],
        scratch_shapes=[
            tokens_low, pltpu.VMEM((length, half), BF16), pltpu.VMEM((length, half), F32),
            pltpu.VMEM((length, half), F32), tokens_low, square, square, square,
            pltpu.VMEM((head_cols, width), BF16), pltpu.VMEM((half, width), BF16),
            pltpu.VMEM((width, half), BF16),
            tokens_low, head_token, token_head, token_head, token_head, head_token, head_token,
            token_head, head_token, head_token, token_head_f32, token_head_f32, token_head_f32,
            scores_f32, scores_f32, scores_f32, scores_low, scores_low,
            head_low, head_low, head_low, tokens_low, tokens_low, tokens_low, tokens_low, tokens_f32,
            pltpu.VMEM((length, half), F32), tokens_f32, pltpu.VMEM((half, width), F32),
            pltpu.VMEM((width, half), F32), pltpu.VMEM((pack_rows, width), BF16),
            pltpu.SemaphoreType.DMA((11,)),
            [pltpu.SemaphoreType.DMA((2 * blocks,)), pltpu.SemaphoreType.DMA((2 * blocks,))],
            pltpu.SemaphoreType.DMA((3, blocks)),
        ],
        compiler_params=pltpu.CompilerParams(
            vmem_limit_bytes=VMEM_BYTES, collective_id=3, has_side_effects=True
        ),
        cost_estimate=pl.CostEstimate(
            flops=2 * length * length * width * 10, bytes_accessed=1 << 24, transcendentals=0
        ),
        name="middle",
    )(x, branch, branch_other, first, gain_b, output_grad, gated, gate_z, scan_out, normed_a,
      (query_proj, key_proj, value_proj, mixed_proj, out_proj, in_proj))

    last_rows = width + 144
    plan_last, land_last = sum_plan(
        counts, [(0, width // 2, 0), (0, width // 2, 0), (1, 128, 0), (0, 16, -1)]
    )
    tile_f32 = pltpu.VMEM((half // 128, wide, 128), F32)
    tile_low = pltpu.VMEM((wide, half), BF16)
    fold_low = pltpu.VMEM((wide, 128), BF16)
    chunk_spare = [tile_f32, tile_f32, tile_low, tile_low, fold_low, fold_low]

    def now(i):
        return jnp.maximum(steps - 1 - i, 0)

    def late_at(i):
        return jnp.minimum(steps - i, steps - 1)

    def back_rows(array, at):
        return (array, (ROWS_STEP, array.shape[1]), lambda i: (at(i), 0))

    def fixed(array):
        return (array, array.shape, None)

    ins = [
        (coef, (None, coefs, ROWS_STEP), lambda i: (now(i), 0, 0)), back_rows(conv_pre, now), back_rows(step_pre, now),
        back_rows(scan_grad, now), back_rows(flags, now),
        (starts, (ROWS_STEP // CHUNK * states, half), lambda i: (now(i), 0)),
        back_rows(conv_pre, late_at), back_rows(conv_in, late_at), back_rows(normed_a, late_at),
        back_rows(flags, late_at), fixed(gain_a), fixed(g_attn_gain), fixed(pack_early),
    ]
    weights_all = (step_proj, decay_t, skip, state_t, taps, in_proj)
    specs = [
        pl.BlockSpec(block, lambda i: (0, 0), pipeline_mode=pl.Buffered(1)) if at is None
        else pl.BlockSpec(block, at)
        for _, block, at in ins
    ]
    early, late, kept, got = pl.pallas_call(
        functools.partial(back_kernel, plan, plan_last, steps),
        grid=(steps + 1,),
        in_specs=specs + [any_spec] * 3 + [(any_spec,) * len(weights_all)],
        out_specs=[any_spec] * 4,
        out_shape=[
            jax.ShapeDtypeStruct((parts,) + pack_early.shape, BF16),
            jax.ShapeDtypeStruct((parts, last_rows, width), BF16),
            jax.ShapeDtypeStruct((piece_len, width), F32),
            jax.ShapeDtypeStruct((piece_len, width), BF16),
        ],
        scratch_shapes=[pltpu.VMEM((array.shape[0], half), array.dtype) for array in weights_all] + [
            pltpu.SemaphoreType.DMA((len(weights_all),)),
            [pltpu.VMEM((states, half), F32), block_f32,
             block_f32, block_f32, block_f32, pltpu.VMEM((ROWS_STEP, wide), BF16), plain_f32,
             plain_f32, chunk_spare, chunk_spare],
            pltpu.VMEM((small_rows, half), F32),
            pltpu.VMEM((2, ROWS_STEP, half), F32),
            pltpu.VMEM((steps, coefs, ROWS_STEP), F32),
            pltpu.VMEM((steps, coefs, ROWS_STEP), F32),
            pltpu.VMEM((ROWS_STEP + 8, half), F32),
            pltpu.VMEM((width, half), F32),
            pltpu.VMEM((128, half), F32),
            pltpu.VMEM((length, half), BF16),
            pltpu.VMEM((length, width), F32),
            pltpu.VMEM((length, width), BF16),
            pltpu.VMEM((length, width), BF16),
            pltpu.VMEM((length, width), BF16),
            pltpu.VMEM((length, width), F32),
            pltpu.VMEM((piece_len, width), F32),
            pltpu.VMEM((piece_len, width), BF16),
            pltpu.VMEM((piece_len, width), BF16),
            pltpu.VMEM((last_rows, width), BF16),
            sum_scratch(plan, pack_early.shape[0], land, width),
            sum_scratch(plan_last, last_rows, land_last, width),
            [pltpu.SemaphoreType.DMA((steps,)), pltpu.SemaphoreType.DMA((steps,))],
            [pltpu.SemaphoreType.DMA((steps,)), pltpu.SemaphoreType.DMA((steps,))],
            [pltpu.SemaphoreType.DMA((16,)), pltpu.SemaphoreType.DMA((16,))],
            pltpu.SemaphoreType.DMA((9,)),
        ],
        compiler_params=pltpu.CompilerParams(
            dimension_semantics=("arbitrary",), vmem_limit_bytes=VMEM_BYTES, collective_id=1,
            has_side_effects=True,
        ),
        cost_estimate=pl.CostEstimate(
            flops=2 * length * states * half * 3000, bytes_accessed=1 << 25, transcendentals=0
        ),
        name="back",
    )(*[a for a, _, _ in ins], x, base, gate_back, weights_all)
    quarter = width // 4
    eighth = width // 8

    def from_sum(total, size, first_row):
        return (total, (parts, size, width), lambda i, sel: (0, first_row // size + i, 0))

    def out_parts(size):
        return ((parts, 4 * size, width), F32, (parts, size, width), lambda i, sel: (0, i, 0))

    results, t_in, t_out, t_query, t_key, t_value, t_mixed, *smalls = call(
        functools.partial(assemble_kernel, (coefs, rank, states)), sel, 4,
        [(kept, (piece_len // 4, width), lambda i, sel: (i, 0)),
         (got, (piece_len // 4, width), lambda i, sel: (i, 0)),
         from_sum(early, quarter, 0), from_sum(early, eighth, width),
         from_sum(early, eighth, width + width // 2), from_sum(early, quarter, attn_rows),
         from_sum(early, quarter, attn_rows + half), from_sum(late, quarter, 0),
         (late, (parts, 128, width), lambda i, sel: (0, width // 128, 0)),
         (late, (parts, 16, width), lambda i, sel: (0, (width + 128) // 16, 0))],
        [((1, 2, piece_len, width), F32, (1, 2, piece_len // 4, width), lambda i, sel: (0, 0, i, 0)),
         ((width, 4 * half), F32, (quarter, 4 * half), lambda i, sel: (i, 0)),
         out_parts(quarter), ((width, width), F32, (quarter, width), lambda i, sel: (i, 0)),
         ((width, width), F32, (quarter, width), lambda i, sel: (i, 0)), out_parts(eighth),
         out_parts(eighth)]
        + [out_whole((size, parts * half)) for size in (coefs, rank, states, 1, 1, 4, 1)]
        + [out_whole((1, width))] * 2,
        [], 0, "assemble",
    )
    t_state, t_step, t_decay, t_step_bias, t_skip, t_taps, t_conv_bias, t_gain, t_attn_gain = smalls
    return (
        results, t_gain[0], t_in, t_taps.T, t_conv_bias[0], t_state.T, t_step, t_step_bias[0],
        t_decay.T, t_skip[0], t_out.reshape(out_proj.shape), t_attn_gain[0], t_query, t_key,
        t_value.reshape(width, width), t_mixed.reshape(width, width),
    )


def solution(mesh):
    in_specs = (P("dp", "inner", None), P("dp", None, None), P("dp", None)) + (P(),) * 15
    out_specs = (P("kind", "dp", "inner", None),) + (P(),) * 15
    return jax.shard_map(local, mesh=mesh, in_specs=in_specs, out_specs=out_specs, check_vma=False)
```

```python
import functools

import jax
import jax.numpy as jnp
from jax import lax
from jax.experimental import pallas as pl
from jax.experimental.pallas import tpu as pltpu
from jax.sharding import PartitionSpec as P

HEAD_DIM = 64
EPS = 1e-05
NEG = -1e30
FAR = 1e30
CHUNK = 16
STRETCH = 8
ROWS_STEP = 256
QUERY_BLOCK = 256
KEY_TILE = 128
VMEM_BYTES = 58 * 1024 * 1024
F32 = jnp.float32
BF16 = jnp.bfloat16


def dot_nn(a, b):
    return lax.dot_general(a, b, (((1,), (0,)), ((), ())), preferred_element_type=F32)


def dot_nt(a, b):
    return lax.dot_general(a, b, (((1,), (1,)), ((), ())), preferred_element_type=F32)


def dot_tn(a, b):
    return lax.dot_general(a, b, (((0,), (0,)), ((), ())), preferred_element_type=F32)


def silu_slope(tensor):
    sigma = jax.nn.sigmoid(tensor)
    return sigma * (1.0 + tensor * (1.0 - sigma))


def rms_scale(tensor):
    return lax.rsqrt(jnp.mean(tensor * tensor, axis=-1, keepdims=True) + EPS)


def softplus(tensor):
    return jnp.maximum(tensor, 0.0) + jnp.log1p(jnp.exp(-jnp.abs(tensor)))


def rms_back(tensor, factor, gain_vec, gradient):
    weighted = gradient * gain_vec
    spread = jnp.mean(weighted * tensor, axis=-1, keepdims=True)
    return factor * weighted - tensor * (factor * factor * factor) * spread


def spread(ref, value):
    for c in range(ref.shape[0]):
        ref[c] = value[:, c * 128 : (c + 1) * 128]


def row_of(ref, c, row, states):
    part = ref[c, pl.ds(row, 8, stride=0), :]
    return jnp.concatenate([part] * (states // 8), axis=0)


def column_of(tile, at):
    return jnp.broadcast_to(tile[:, at : at + 1], tile.shape)


def own_token(chunk, states):
    at = lax.broadcasted_iota(jnp.int32, (chunk, chunk * states), 0)
    of = lax.broadcasted_iota(jnp.int32, (chunk, chunk * states), 1) // states
    return at == of


def state_picks(chunk, states):
    at = lax.broadcasted_iota(jnp.int32, (states, chunk * states), 0)
    of = lax.rem(lax.broadcasted_iota(jnp.int32, (states, chunk * states), 1), states)
    return (at == of).astype(F32).astype(BF16)


def remote(src, dst, sems, number, to):
    return pltpu.make_async_remote_copy(
        src_ref=src, dst_ref=dst, send_sem=sems[0].at[number], recv_sem=sems[1].at[number],
        device_id=to, device_id_type=pl.DeviceIdType.MESH,
    )


def call(body, sel, steps, ins, outs, scratch, flops, name):
    bytes_all = sum(a.size * a.dtype.itemsize for a, _, _ in ins)
    return pl.pallas_call(
        body,
        grid_spec=pltpu.PrefetchScalarGridSpec(
            num_scalar_prefetch=1,
            grid=(steps,),
            in_specs=[pl.BlockSpec(block, at) for _, block, at in ins],
            out_specs=[pl.BlockSpec(block, at) for _, _, block, at in outs],
            scratch_shapes=scratch,
        ),
        out_shape=[jax.ShapeDtypeStruct(shape, dtype) for shape, dtype, _, _ in outs],
        compiler_params=pltpu.CompilerParams(
            dimension_semantics=("arbitrary",), vmem_limit_bytes=VMEM_BYTES
        ),
        cost_estimate=pl.CostEstimate(flops=flops, bytes_accessed=bytes_all, transcendentals=0),
        name=name,
    )(sel, *[a for a, _, _ in ins])


def whole(shape):
    zeros = (0,) * len(shape)
    return (shape, lambda i, sel: zeros)


def scan_block(
    coef, pre, gate, flags, step_w, step_b, decay_t, skip, out_w,
    step_o, size_o, act_o, scan_o, gated_o, starts_o, branch_o, spare,
):
    state, stepd, drive, ys, blocked, h_low = spare
    block, width = pre.shape
    states = decay_t.shape[0]
    rank = step_w.shape[0]
    tiles = width // 128

    step_pre = dot_tn(coef[:rank, :].astype(BF16), step_w[...]) + step_b[...]
    step_o[...] = step_pre
    step = softplus(step_pre)
    size_o[...] = step
    act = pre[...] * jax.nn.sigmoid(pre[...])
    act_o[...] = act
    spread(drive, step * act)
    spread(stepd, jnp.where(flags[:, 1:2] > 0.0, step, FAR))
    neg = -jnp.exp(decay_t[...])
    neg_of = [neg[:, c * 128 : (c + 1) * 128] for c in range(tiles)]
    own_all = jnp.concatenate([own_token(CHUNK, states)] * (block // CHUNK), axis=0)
    blocked[...] = jnp.where(
        own_all, dot_tn(coef[rank + states :, :].astype(BF16), state_picks(CHUNK, states)), 0.0
    ).astype(BF16)

    def one_chunk(i, h, h_s):
        here = pl.ds(pl.multiple_of(i * CHUNK, CHUNK), CHUNK)
        tile = coef[rank : rank + states, pl.ds(pl.multiple_of((i // 8) * 128, 128), 128)]
        tile = pltpu.roll(tile, lax.rem(128 - lax.rem(i, 8) * CHUNK, 128), 1)
        for c in range(tiles):
            starts_o[here, c * 128 : (c + 1) * 128] = h[c]
        for at in range(CHUNK):
            row = i * CHUNK + at
            write = column_of(tile, at)
            for c in range(tiles):
                decay = jnp.exp(neg_of[c] * row_of(stepd, c, row, states))
                h[c] = decay * h[c] + row_of(drive, c, row, states) * write
                h_s[at * states : (at + 1) * states, c * 128 : (c + 1) * 128] = h[c].astype(BF16)
        return h

    def stretch(number, carried):
        def pair(step_no, carried):
            h = list(carried)
            for sub in range(2):
                at = 2 * step_no + sub
                spot = h_low.at[pl.ds(pl.multiple_of(at * CHUNK * states, CHUNK * states), CHUNK * states)]
                h = one_chunk(number * STRETCH + at, h, spot)
            return tuple(h)

        carried = lax.fori_loop(0, STRETCH // 2, pair, carried)
        for at in range(STRETCH):
            here = pl.ds(pl.multiple_of((number * STRETCH + at) * CHUNK, CHUNK), CHUNK)
            spot = slice(at * CHUNK * states, (at + 1) * CHUNK * states)
            ys[here, :] = dot_nn(blocked[here, :], h_low[spot, :])
        return carried

    begin = tuple(state[:, c * 128 : (c + 1) * 128] for c in range(tiles))
    for c, last in enumerate(lax.fori_loop(0, block // (STRETCH * CHUNK), stretch, begin)):
        state[:, c * 128 : (c + 1) * 128] = last
    scan_out = ys[...] + skip[...] * act
    scan_o[...] = scan_out
    z = gate[...]
    gated = (scan_out * (z * jax.nn.sigmoid(z))).astype(BF16)
    gated_o[...] = gated
    branch_o[...] = dot_nn(gated, out_w[...]).astype(BF16)


def front_kernel(
    flags, gain, layer_all, weights_all,
    x_o, normed_o, conv_o, pre_o, gate_o, coef_o, step_o, size_o, act_o, scan_o, gated_o, starts_o, branch_o,
    branch_other_o,
    x, normed, ext, pre, gate, coef, coef_got, coef_sum, step_pre, size, act, scan_out, gated, starts,
    branch, branch_got, weights, scan_spare, load_sems, x_sems, coef_sems, branch_sems, store_sems, late_sems,
):
    length, width = x.shape
    blocks = length // ROWS_STEP
    core, row = lax.axis_index("kind"), lax.axis_index("inner")
    other_core, other_row = {"kind": 1 - core}, {"inner": 1 - row}
    w_conv, w_gate, state_w, step_w, decay_t, skip, taps, conv_b, step_b, out_w = weights
    in_all, state_all, step_all, decay_all, skip_all, taps_all, conv_b_all, step_b_all, out_all = weights_all
    channels = w_conv.shape[1]

    def part_of(number):
        return pl.ds(pl.multiple_of(number * channels, 128), channels)

    def rows_at(b):
        return pl.ds(pl.multiple_of(b * ROWS_STEP, ROWS_STEP), ROWS_STEP)

    mine = part_of(core)
    loads = [
        pltpu.make_async_copy(source, target, load_sems.at[i])
        for i, (source, target) in enumerate((
            (layer_all.at[row], x.at[pl.ds(pl.multiple_of(row * (length // 2), 256), length // 2)]),
            (in_all.at[:, mine], w_conv), (in_all.at[:, part_of(2 + core)], w_gate),
            (state_all.at[:, mine], state_w), (step_all.at[:, mine], step_w),
            (decay_all.at[:, mine], decay_t), (skip_all.at[:, mine], skip), (taps_all.at[:, mine], taps),
            (conv_b_all.at[:, mine], conv_b), (step_b_all.at[:, mine], step_b), (out_all.at[mine], out_w),
        ))
    ]
    barrier = pltpu.get_barrier_semaphore()
    for device in (other_core, other_row):
        pl.semaphore_signal(barrier, inc=1, device_id=device, device_id_type=pl.DeviceIdType.MESH)
    pl.semaphore_wait(barrier, 2)
    sent = remote(
        layer_all.at[1 - row, rows_at(core)], x.at[rows_at(row * (blocks // 2) + core)], x_sems, 0, other_row
    )
    sent.start()
    for load in loads:
        load.start()
    for load in loads:
        load.wait()
    ext[0:8, :] = jnp.zeros((8, channels), F32)
    scan_spare[0][...] = jnp.zeros_like(scan_spare[0])

    results = (
        (x, x_o), (normed, normed_o), (gate, gate_o), (pre, pre_o), (step_pre, step_o), (size, size_o),
        (act, act_o), (scan_out, scan_o), (gated, gated_o), (starts, starts_o), (branch, branch_o),
    )

    def stores(b, numbers=range(len(results))):
        rows = rows_at(b)
        return [
            pltpu.make_async_copy(results[i][0].at[rows], results[i][1].at[rows], store_sems.at[i, b])
            for i in numbers
        ]

    def project(b):
        rows = rows_at(b)
        u = x[rows, :].astype(F32)
        low = (u * rms_scale(u) * gain[...]).astype(BF16)
        normed[rows, :] = low
        ext[pl.ds(pl.multiple_of(b * ROWS_STEP + 8, 8), ROWS_STEP), :] = dot_nn(low, w_conv[...])
        gate[rows, :] = dot_nn(low, w_gate[...])
        for store in stores(b, range(3)):
            store.start()

    first_other = (1 - row) * (blocks // 2)
    project(row * (blocks // 2))
    project(row * (blocks // 2) + 1)
    sent.wait()
    fetched = x.at[rows_at(first_other + core)]
    passed = remote(fetched, fetched, x_sems, 1, other_core)
    passed.start()
    project(first_other + core)
    passed.wait()
    project(first_other + 1 - core)
    store_conv = pltpu.make_async_copy(ext.at[pl.ds(8, length)], conv_o, late_sems.at[0])
    store_conv.start()

    def coef_copy(b):
        return remote(coef.at[b], coef_got.at[b], coef_sems, b, other_core)

    def branch_copy(b):
        rows = rows_at(b)
        return remote(branch.at[rows], branch_got.at[rows], branch_sems, b, other_core)

    for b in range(blocks):
        rows = slice(b * ROWS_STEP, (b + 1) * ROWS_STEP)
        total = conv_b[...] + taps[3:4, :] * ext[8 + b * ROWS_STEP : 8 + (b + 1) * ROWS_STEP, :]
        for j in range(1, 4):
            moved = ext[8 - j + b * ROWS_STEP : 8 - j + (b + 1) * ROWS_STEP, :]
            total = total + taps[3 - j : 4 - j, :] * jnp.where(flags[rows, j : j + 1] > 0.0, moved, 0.0)
        pre[rows, :] = total
        coef[b] = dot_nt(state_w[...], (total * jax.nn.sigmoid(total)).astype(BF16))
        coef_copy(b).start()
        stores(b, [3])[0].start()

    def scan(b, unused):
        rows = rows_at(b)
        coef_copy(b).wait()
        coef_sum[b] = coef[b] + coef_got[b]
        scan_block(
            coef_sum.at[b], pre.at[rows], gate.at[rows], flags.at[rows], step_w, step_b, decay_t, skip, out_w,
            step_pre.at[rows], size.at[rows], act.at[rows], scan_out.at[rows], gated.at[rows], starts.at[rows], branch.at[rows],
            scan_spare,
        )
        branch_copy(b).start()
        for store in stores(b, range(4, len(results))):
            store.start()
        return unused

    lax.fori_loop(0, blocks, scan, 0)
    store_coef = pltpu.make_async_copy(coef_sum, coef_o, late_sems.at[1])
    store_coef.start()
    for b in range(blocks):
        branch_copy(b).wait()
    store_other = pltpu.make_async_copy(branch_got, branch_other_o, late_sems.at[2])
    store_other.start()
    for copy in (store_conv, store_coef, store_other):
        copy.wait()
    for b in range(blocks):
        for store in stores(b):
            store.wait()


def middle_kernel(
    x, part_a, part_b, first, gain, grads, gated_all, gate_all, scan_all, normed_all, weights_all,
    base_o, scan_grad_o, back_o, pack_o, gain_grad_o,
    grad, gated, gate, scan_out, normed_a, wq, wk, wv, wm, out_w, w_gate,
    normed, q_t, q_n, k_n, v_n, k_t, v_t, g_n, g_t, o_t, dq_n, dk, dv, bias, expo, prob_grad, prob_low,
    score_low,
    dq_low, dk_low, dv_low, branch, branch_got, back, back_got, base, scan_grad, gate_back, gout, ggate,
    pack, load_sems, pass_sems, store_sems,
):
    length, width = x.shape
    core, row = lax.axis_index("kind"), lax.axis_index("inner")
    other_core = {"kind": 1 - core}
    head_cols, channels = wq.shape[1], out_w.shape[0]

    def part_of(size):
        return pl.ds(pl.multiple_of(core * size, 128), size)

    query_all, key_all, value_all, mixed_all, out_all, in_all = weights_all
    gate_cols = pl.ds(pl.multiple_of((2 + core) * channels, 128), channels)
    loads = [
        pltpu.make_async_copy(source, target, load_sems.at[i])
        for i, (source, target) in enumerate((
            (query_all.at[:, part_of(head_cols)], wq), (key_all.at[:, part_of(head_cols)], wk),
            (value_all.at[:, part_of(head_cols)], wv), (grads.at[row], grad),
            (mixed_all.at[part_of(head_cols)], wm), (gated_all, gated), (gate_all, gate),
            (scan_all, scan_out), (normed_all, normed_a), (out_all.at[part_of(channels)], out_w),
            (in_all.at[:, gate_cols], w_gate),
        ))
    ]
    for load in loads:
        load.start()
    barrier = pltpu.get_barrier_semaphore()
    pl.semaphore_signal(barrier, inc=1, device_id=other_core, device_id_type=pl.DeviceIdType.MESH)
    pl.semaphore_wait(barrier, 1)
    for load in loads[:5]:
        load.wait()

    heads = k_n.shape[0]
    scale = HEAD_DIM**-0.5
    for b in range(length // ROWS_STEP):
        rows = slice(b * ROWS_STEP, (b + 1) * ROWS_STEP)
        middle = x[rows, :].astype(F32) + (part_a[rows, :].astype(F32) + part_b[rows, :].astype(F32))
        normed_blk = (middle * rms_scale(middle) * gain[...]).astype(BF16)
        normed[rows, :] = normed_blk
        query = dot_nn(normed_blk, wq[...]).astype(BF16).astype(F32) * scale
        keys = dot_nn(normed_blk, wk[...]).astype(BF16).astype(F32)
        values = dot_nn(normed_blk, wv[...]).astype(BF16).astype(F32)
        out_grad = dot_nt(grad[rows, :], wm[...]).astype(BF16).astype(F32)
        q_t[:, rows] = query.T.astype(BF16)
        k_t[:, rows] = (keys.T * scale).astype(BF16)
        v_t[:, rows] = values.T.astype(BF16)
        g_t[:, rows] = out_grad.T.astype(BF16)
        for h in range(heads):
            cols = slice(h * HEAD_DIM, (h + 1) * HEAD_DIM)
            q_n[h, rows, :] = query[:, cols].astype(BF16)
            k_n[h, rows, :] = keys[:, cols].astype(BF16)
            v_n[h, rows, :] = values[:, cols].astype(BF16)
            g_n[h, rows, :] = out_grad[:, cols].astype(BF16)
    dk[...] = jnp.zeros_like(dk)
    dv[...] = jnp.zeros_like(dv)

    for block in range(length // QUERY_BLOCK):
        cols = slice(block * QUERY_BLOCK, (block + 1) * QUERY_BLOCK)
        reach = (block + 1) * QUERY_BLOCK
        key_at = lax.broadcasted_iota(jnp.int32, (reach, QUERY_BLOCK), 0)
        query_at = lax.broadcasted_iota(jnp.int32, (reach, QUERY_BLOCK), 1) + block * QUERY_BLOCK
        kept = (key_at >= first[:, cols]) & (key_at <= query_at)
        bias[0:reach, :] = jnp.where(kept, 0.0, NEG)

        def one_head(h, unused):
            dims = pl.ds(pl.multiple_of(h * HEAD_DIM, HEAD_DIM), HEAD_DIM)
            tiles = [slice(t * KEY_TILE, (t + 1) * KEY_TILE) for t in range(reach // KEY_TILE)]

            def by_eight(tile):
                return tile.reshape(KEY_TILE // 8, 8, QUERY_BLOCK)

            query, out_grad = q_t[dims, cols], g_t[dims, cols]
            most = jnp.full((8, QUERY_BLOCK), NEG, F32)
            for keys in tiles:
                scores = dot_nn(k_n[h, keys, :], query) + bias[keys, :]
                expo[keys, :] = scores
                most = jnp.maximum(most, jnp.max(by_eight(scores), axis=0))
            most = jnp.max(most, axis=0, keepdims=True)
            total = jnp.zeros((8, QUERY_BLOCK), F32)
            centre = jnp.zeros((8, QUERY_BLOCK), F32)
            for keys in tiles:
                exponent = jnp.exp(expo[keys, :] - most)
                grads = dot_nn(v_n[h, keys, :], out_grad)
                expo[keys, :] = exponent
                prob_grad[keys, :] = grads
                total = total + jnp.sum(by_eight(exponent), axis=0)
                centre = centre + jnp.sum(by_eight(exponent * grads), axis=0)
            scale_by = 1.0 / jnp.sum(total, axis=0, keepdims=True)
            centre = jnp.sum(centre, axis=0, keepdims=True) * scale_by
            for keys in tiles:
                prob = expo[keys, :] * scale_by
                prob_low[keys, :] = prob.astype(BF16)
                score_low[keys, :] = (prob * (prob_grad[keys, :] - centre)).astype(BF16)
            o_t[dims, cols] = dot_nn(v_t[dims, 0:reach], prob_low[0:reach, :]).astype(BF16)
            dq_n[h, cols, :] = dot_nn(k_t[dims, 0:reach], score_low[0:reach, :]).T
            dk[h, 0:reach, :] += dot_nn(score_low[0:reach, :], q_n[h, cols, :])
            dv[h, 0:reach, :] += dot_nn(prob_low[0:reach, :], g_n[h, cols, :])
            return unused

        lax.fori_loop(0, heads, one_head, 0)

    blocks = length // ROWS_STEP

    def rows_at(b):
        return pl.ds(pl.multiple_of(b * ROWS_STEP, ROWS_STEP), ROWS_STEP)

    def back_copy(b):
        return remote(back.at[rows_at(b)], back_got.at[rows_at(b)], pass_sems, b, other_core)

    def branch_copy(b):
        there = branch_got.at[rows_at(b)]
        return remote(branch.at[rows_at(b)], there, pass_sems, blocks + b, other_core)

    def partials(b, unused):
        rows = rows_at(b)
        for target, source in ((dq_low, dq_n), (dk_low, dk), (dv_low, dv)):
            joined = jnp.concatenate([source[h, rows, :] for h in range(heads)], axis=1)
            target[rows, :] = joined.astype(BF16)
        total = dot_nt(dq_low[rows, :], wq[...]) + dot_nt(dk_low[rows, :], wk[...])
        back[rows, :] = (total + dot_nt(dv_low[rows, :], wv[...])).astype(BF16)
        back_copy(b).start()
        branch[rows, :] = dot_tn(o_t[:, rows], wm[...]).astype(BF16)
        branch_copy(b).start()
        return unused

    lax.fori_loop(0, blocks, partials, 0)
    cut = width // 2
    attn_rows = width + cut + head_cols
    pack[0:width, 0:head_cols] = dot_tn(normed[...], dq_low[...]).astype(BF16)
    pack[0:width, head_cols:] = dot_tn(normed[...], dk_low[...]).astype(BF16)
    value_grad = dot_tn(normed[...], dv_low[...]).astype(BF16)
    pack[width : width + cut, 0:head_cols] = value_grad[:cut]
    pack[width : width + cut, head_cols:] = value_grad[cut:]
    pack[width + cut : attn_rows, :] = dot_nn(o_t[...], grad[...]).astype(BF16)
    for load in loads[5:]:
        load.wait()
    gout[...] = jnp.zeros_like(gout)
    ggate[...] = jnp.zeros_like(ggate)
    gain_grad_o[...] = jnp.zeros_like(gain_grad_o)

    def stores(b):
        rows = rows_at(b)
        return [
            pltpu.make_async_copy(source.at[rows], target.at[rows], store_sems.at[i, b])
            for i, (source, target) in enumerate(
                ((base, base_o), (scan_grad, scan_grad_o), (gate_back, back_o))
            )
        ]

    def gating(b, unused):
        rows = rows_at(b)
        back_copy(b).wait()
        branch_copy(b).wait()
        middle = x[rows, :].astype(F32) + (part_a[rows, :].astype(F32) + part_b[rows, :].astype(F32))
        total = back[rows, :].astype(F32) + back_got[rows, :].astype(F32)
        factor = rms_scale(middle)
        middle_grad = grad[rows, :].astype(F32) + rms_back(middle, factor, gain[...], total)
        gain_grad_o[...] += jnp.sum(total * middle * factor, axis=0, keepdims=True)
        layer_out = middle + (branch[rows, :].astype(F32) + branch_got[rows, :].astype(F32))
        chosen = (1 - core).astype(F32)
        base[rows, :] = chosen * middle_grad + (1.0 - chosen) * layer_out
        low = middle_grad.astype(BF16)
        gout[...] += dot_tn(gated[rows, :], low)
        gated_grad = dot_nt(low, out_w[...])
        z = gate[rows, :]
        sigma = jax.nn.sigmoid(z)
        scan_grad[rows, :] = gated_grad * (z * sigma)
        slope = sigma * (1.0 + z * (1.0 - sigma))
        gate_low = (gated_grad * scan_out[rows, :] * slope).astype(BF16)
        ggate[...] += dot_tn(normed_a[rows, :], gate_low)
        gate_back[rows, :] = dot_nt(gate_low, w_gate[...])
        for store in stores(b):
            store.start()
        return unused

    lax.fori_loop(0, blocks, gating, 0)
    pack[attn_rows : attn_rows + channels, :] = gout[...].astype(BF16)
    pack[attn_rows + channels :, :] = ggate[...].astype(BF16)
    last = pltpu.make_async_copy(pack, pack_o, load_sems.at[0])
    last.start()
    for b in range(blocks):
        for store in stores(b):
            store.wait()
    last.wait()


def scan_back_block(
    coef, act_in, size_in, step_in, scan_grad, flags, starts, step_w, decay_t, skip,
    act_grad, coef_grad, small, spare, between,
):
    (state, steps, stepd, drive, reads, blocked, d_drive, d_expo, in_own, read_own,
     decays, decayed, h_low, sum_low, expo_low) = spare
    block, width = act_in.shape
    states = decay_t.shape[0]
    rank = step_w.shape[0]
    tiles = width // 128
    wide = CHUNK * states

    step, act = size_in[...], act_in[...]
    spread(steps, step)
    spread(drive, step * act)
    spread(stepd, jnp.where(flags[:, 1:2] > 0.0, step, FAR))
    spread(reads, scan_grad[...])
    neg = -jnp.exp(decay_t[...])
    neg_of = [neg[:, c * 128 : (c + 1) * 128] for c in range(tiles)]
    picks = state_picks(CHUNK, states)
    own = own_token(CHUNK, states)
    own_low = own.astype(F32).astype(BF16)
    own_all = jnp.concatenate([own] * (block // CHUNK), axis=0)
    blocked[...] = jnp.where(
        own_all, dot_tn(coef[rank : rank + states, :].astype(BF16), picks), 0.0
    ).astype(BF16)

    def one_chunk(i, backward, spare):
        decay_s, decayed_s, h_s, sum_s, expo_s = spare
        rows16 = pl.ds(pl.multiple_of(i * CHUNK, CHUNK), CHUNK)
        tile = coef[rank:, pl.ds(pl.multiple_of((i // 8) * 128, 128), 128)]
        tile = pltpu.roll(tile, lax.rem(128 - lax.rem(i, 8) * CHUNK, 128), 1)
        h = [starts[rows16, c * 128 : (c + 1) * 128] for c in range(tiles)]
        for at in range(CHUNK):
            row = i * CHUNK + at
            here = slice(at * states, (at + 1) * states)
            write = column_of(tile[:states], at)
            for c in range(tiles):
                cols = slice(c * 128, (c + 1) * 128)
                decay = jnp.exp(neg_of[c] * row_of(stepd, c, row, states))
                kept = decay * h[c]
                h[c] = kept + row_of(drive, c, row, states) * write
                decay_s[c, here, :] = decay
                decayed_s[c, here, :] = kept
                h_s[here, cols] = h[c].astype(BF16)
        total = [jnp.zeros((states, 128), F32)] * tiles
        for at in reversed(range(CHUNK)):
            row = i * CHUNK + at
            here = slice(at * states, (at + 1) * states)
            read = column_of(tile[states:], at)
            for c in range(tiles):
                cols = slice(c * 128, (c + 1) * 128)
                summed = read * row_of(reads, c, row, states) + backward[c]
                sum_s[here, cols] = summed.astype(BF16)
                expo = summed * decayed_s[c, here, :]
                expo_s[here, cols] = (expo * neg_of[c]).astype(BF16)
                total[c] = total[c] + expo * row_of(steps, c, row, states)
                backward[c] = decay_s[c, here, :] * summed
        for c in range(tiles):
            small[rank : rank + states, c * 128 : (c + 1) * 128] += total[c]

        def flat(ref):
            return jnp.concatenate([ref[c, rows16, :] for c in range(tiles)], axis=1).astype(BF16)

        d_drive[rows16, :] = dot_nn(blocked[rows16, :], sum_s[...])
        d_expo[rows16, :] = dot_nn(own_low, expo_s[...])
        in_own[rows16, :] = jnp.where(own, dot_nt(flat(drive), sum_s[...]), 0.0)
        read_own[rows16, :] = jnp.where(own, dot_nt(flat(reads), h_s[...]), 0.0)
        return backward

    def pair(step_no, carried):
        between(step_no)
        backward = list(carried)
        last = block // CHUNK - 1 - 2 * step_no
        for sub in range(2):
            spare = (decays.at[sub], decayed.at[sub], h_low.at[sub], sum_low.at[sub], expo_low.at[sub])
            backward = one_chunk(last - sub, backward, spare)
        return tuple(backward)

    begin = tuple(state[:, c * 128 : (c + 1) * 128] for c in range(tiles))
    for c, last in enumerate(lax.fori_loop(0, block // (2 * CHUNK), pair, begin)):
        state[:, c * 128 : (c + 1) * 128] = last

    def by_state(ref):
        high = ref[...].astype(BF16)
        rest = (ref[...] - high.astype(F32)).astype(BF16)
        return dot_nt(picks, high) + dot_nt(picks, rest)

    coef_grad[rank : rank + states, :] = by_state(in_own)
    coef_grad[rank + states :, :] = by_state(read_own)

    drive_grad = d_drive[...]
    pre_grad = (d_expo[...] + drive_grad * act) * jax.nn.sigmoid(step_in[...])
    tail = rank + states
    small[tail : tail + 1, :] += jnp.sum(pre_grad, axis=0, keepdims=True)
    pre_low = pre_grad.astype(BF16)
    small[:rank, :] += dot_nn(coef[:rank, :].astype(BF16), pre_low)
    coef_grad[:rank, :] = dot_nt(step_w[...], pre_low)
    act_grad[...] = drive_grad * step + scan_grad[...] * skip[...]
    small[tail + 1 : tail + 2, :] += jnp.sum(scan_grad[...] * act, axis=0, keepdims=True)


def conv_back_block(
    coef_grad, pre, act_grad, conv_in, normed, flags, state_w, taps, ext, gconv, gsmall, mix_low, taps_at,
):
    block = pre.shape[0]
    coefs = coef_grad.shape[0]
    v = pre[...]
    sigma = jax.nn.sigmoid(v)
    gsmall[0:coefs, :] += dot_nn(coef_grad, (v * sigma).astype(BF16))
    act_all = act_grad[...] + dot_tn(coef_grad, state_w[...])
    conv_grad = act_all * (sigma * (1.0 + v * (1.0 - sigma)))
    ext[0:block, :] = conv_grad
    conv_in_grad = taps[3:4, :] * conv_grad
    sums = [None] * 4
    sums[3] = jnp.sum(conv_grad * conv_in[...], axis=0, keepdims=True)
    for j in range(1, 4):
        moved = jnp.where(flags[:, 4 + j : 5 + j] > 0.0, ext[j : j + block, :], 0.0)
        sums[3 - j] = jnp.sum(moved * conv_in[...], axis=0, keepdims=True)
        conv_in_grad = conv_in_grad + taps[3 - j : 4 - j, :] * moved
    for j in range(4):
        gsmall[taps_at + j : taps_at + j + 1, :] += sums[j]
    gsmall[taps_at + 4 : taps_at + 5, :] += jnp.sum(conv_grad, axis=0, keepdims=True)
    low = conv_in_grad.astype(BF16)
    gconv[...] += dot_tn(normed[...], low)
    mix_low[...] = low
    ext[block:, :] = ext[0:8, :]


def sum_digits(counts):
    bits = [(axis, 1 << i) for axis, size in counts for i in range(size.bit_length() - 1)]
    return [bits[i : i + 2] for i in range(0, len(bits), 2)]


def sum_plan(counts, parts):
    digits = sum_digits(counts)
    streams, at, land = [], 0, 0
    for number, size, lead in parts:
        turn = number % len(digits)
        steps, held = [], size
        for digit in digits[turn:] + digits[:turn]:
            radix = 1 << len(digit)
            split = held % (16 * radix) == 0
            held = held // radix if split else held
            steps.append((digit, split, held, land))
            land += held * (radix - 1)
        streams.append((at, size, steps, lead))
        at += size
    return streams, land


class Summing:
    def __init__(self, plan, src, work, land, full, peer, send, recv):
        self.streams, self.src, self.work, self.land = plan, src, work, land
        self.full, self.peer = full, peer
        self.sems = (send, recv)
        self.turns = len(plan[0][2])
        self.phases = 2 * self.turns + 2 - min(0, *(lead for _, _, _, lead in plan))
        self.start = []
        for first, _, steps, _ in plan:
            at, spots = first, [first]
            for turn, (digit, split, kept, _) in enumerate(steps):
                at = at + self.index(digit, 0) * kept if split else at
                spots.append(at)
            self.start.append(spots)

    def index(self, digit, flipped):
        total = 0
        for i, (axis, weight) in enumerate(digit):
            place = lax.rem(lax.axis_index(axis) // weight, 2)
            total = total + (1 - place if flipped >> i & 1 else place) * (1 << i)
        return total

    def partner(self, digit, flipped):
        device = {}
        for i, (axis, weight) in enumerate(digit):
            if flipped >> i & 1:
                me = lax.axis_index(axis)
                device[axis] = device.get(axis, me) + weight * (1 - 2 * lax.rem(me // weight, 2))
        return device

    def other_core(self):
        return {"kind": 1 - lax.axis_index("kind")}

    def others(self, s, turn):
        return range(1, 1 << len(self.streams[s][2][turn][0]))

    def rows(self, ref, at, size):
        return ref.at[pl.ds(pl.multiple_of(at, 16), size)]

    def number(self, s, kind, turn, flipped):
        return ((s * 3 + kind) * (self.turns + 1) + turn) * 4 + flipped

    def piece(self, s, turn, flipped):
        digit, split, kept, _ = self.streams[s][2][turn]
        at = self.start[s][turn]
        return at + self.index(digit, flipped) * kept if split else at

    def halves(self, s, turn):
        digit, _, kept, land = self.streams[s][2][turn]
        source = self.src if turn == 0 else self.work
        return [
            remote(
                self.rows(source, self.piece(s, turn, q), kept),
                self.land.at[pl.ds(land + (q - 1) * kept, kept)],
                self.sems, self.number(s, 0, turn, q), self.partner(digit, q),
            )
            for q in self.others(s, turn)
        ]

    def add(self, s, turn):
        target = self.full if turn == self.turns - 1 else self.work
        self.add_to(target, self.start[s][turn + 1], s, turn)

    def add_to(self, target, first, s, turn):
        _, _, kept, land = self.streams[s][2][turn]
        at = self.start[s][turn + 1]
        source = self.src if turn == 0 else self.work

        def step(i, unused):
            here = pl.ds(pl.multiple_of(at + i * 16, 16), 16)
            parts = [source[here, :].astype(F32)]
            for q in self.others(s, turn):
                there = pl.ds(pl.multiple_of(land + (q - 1) * kept + i * 16, 16), 16)
                parts.append(self.land[there, :].astype(F32))
            while len(parts) > 1:
                parts = [parts[i] + parts[i + 1] for i in range(0, len(parts), 2)]
            target[pl.ds(pl.multiple_of(first + i * 16, 16), 16), :] = parts[0].astype(BF16)
            return unused

        lax.fori_loop(0, kept // 16, step, 0)

    def spreads(self, s, turn):
        digit, split, kept, _ = self.streams[s][2][turn]
        if not split:
            return []
        here = self.rows(self.full, self.start[s][turn + 1], kept)
        return [
            remote(here, here, self.sems, self.number(s, 1, turn, q), self.partner(digit, q))
            for q in self.others(s, turn)
        ]

    def shares(self, s, turn):
        if turn == self.turns:
            found = [(0, self.start[s][turn], self.streams[s][2][-1][2])]
        else:
            _, split, kept, _ = self.streams[s][2][turn]
            found = [(q, self.piece(s, turn, q), kept) for q in self.others(s, turn)] if split else []
        return [
            remote(
                self.rows(self.full, at, size), self.rows(self.peer, at, size), self.sems,
                self.number(s, 2, turn, q), self.other_core(),
            )
            for q, at, size in found
        ]

    def greet(self):
        barrier = pltpu.get_barrier_semaphore()
        partners = [self.other_core()]
        for digit, _, _, _ in self.streams[0][2]:
            partners += [self.partner(digit, q) for q in range(1, 1 << len(digit))]
        for device in partners:
            pl.semaphore_signal(
                barrier, inc=1, device_id=device, device_id_type=pl.DeviceIdType.MESH
            )
        pl.semaphore_wait(barrier, len(partners))

    def begin(self, copies):
        for copy in copies:
            copy.start()

    def finish(self, copies):
        for copy in copies:
            copy.wait()

    def phase(self, number):
        for s, (_, _, _, lead) in enumerate(self.streams):
            at = number + lead
            if number == self.phases - 1:
                for turn in range(self.turns + 1):
                    self.finish(self.shares(s, turn))
            elif at == 0:
                self.begin(self.halves(s, 0))
            elif 0 < at <= self.turns:
                self.finish(self.halves(s, at - 1))
                self.add(s, at - 1)
                if at < self.turns:
                    self.begin(self.halves(s, at))
                else:
                    self.begin(self.spreads(s, self.turns - 1))
                    self.begin(self.shares(s, self.turns))
            elif self.turns < at <= 2 * self.turns:
                turn = 2 * self.turns - at
                self.finish(self.spreads(s, turn))
                if turn > 0:
                    self.begin(self.spreads(s, turn - 1))
                self.begin(self.shares(s, turn))


def sum_scratch(plan, rows, land, width):
    numbers = len(plan) * 3 * (len(plan[0][2]) + 1) * 4
    return [
        pltpu.VMEM((rows, width), BF16),
        pltpu.VMEM((land, width), BF16),
        pltpu.VMEM((rows, width), BF16),
        pltpu.VMEM((rows, width), BF16),
        pltpu.SemaphoreType.DMA((numbers,)),
        pltpu.SemaphoreType.DMA((numbers,)),
    ]


def both_copies(summing, out, sems, number):
    core = lax.axis_index("kind")
    return [
        pltpu.make_async_copy(summing.full, out.at[core], sems.at[number]),
        pltpu.make_async_copy(summing.peer, out.at[1 - core], sems.at[number + 1]),
    ]


def back_kernel(
    plan, plan_last, steps,
    coef, act_in, size_in, step_in, scan_grad, flags, starts,
    pre_late, conv_in, normed, flags_late,
    gain, gain_grad, pack, x_all, base_all, gate_back_all, weights_all,
    early_o, late_o, kept_o, got_o,
    step_w, decay_t, skip, state_w, taps, w_conv, weight_sems,
    scan_spare, small, act_grads, coef_grads, coef_got, ext, gconv, gsmall, mix_low, back, low, low_got,
    x_s, base_s, kept, sent, got, pack_last, sum_spare, sum_spare_last,
    coef_sems, low_sems, pass_sems, local_sems,
):
    pid = pl.program_id(0)
    states, rank, coefs = decay_t.shape[0], step_w.shape[0], state_w.shape[0]
    block = act_in.shape[0]
    pairs = block // (2 * CHUNK)
    taps_at = coefs + small.shape[0]
    core, row = lax.axis_index("kind"), lax.axis_index("inner")
    other_core = {"kind": 1 - core}
    first_sum = Summing(plan, pack, *sum_spare)
    last_sum = Summing(plan_last, pack_last, *sum_spare_last)
    slots = [share * pairs * steps // 32 for share in (0, 12, 19, 27)]
    load_x = pltpu.make_async_copy(x_all, x_s, local_sems.at[0])
    load_base = pltpu.make_async_copy(base_all, base_s, local_sems.at[1])
    load_back = pltpu.make_async_copy(gate_back_all, back, local_sems.at[8])
    mine = pl.ds(pl.multiple_of(core * w_conv.shape[1], 128), w_conv.shape[1])
    load_weights = [
        pltpu.make_async_copy(source.at[:, mine], target, weight_sems.at[i])
        for i, (source, target) in enumerate(
            zip(weights_all, (step_w, decay_t, skip, state_w, taps, w_conv), strict=True)
        )
    ]

    def coef_copy(i):
        return remote(coef_grads.at[i], coef_got.at[i], coef_sems, i, other_core)

    def low_copy(i):
        here = pl.ds(pl.multiple_of((steps - 1 - i) * block, block), block)
        return remote(low.at[here], low_got.at[here], low_sems, i, other_core)

    def first_phase(number):
        first_sum.phase(number)

    @pl.when(pid == 0)
    def _():
        scan_spare[0][...] = jnp.zeros_like(scan_spare[0])
        small[...] = jnp.zeros_like(small)
        ext[block:, :] = jnp.zeros((8, ext.shape[1]), F32)
        gconv[...] = jnp.zeros_like(gconv)
        gsmall[...] = jnp.zeros_like(gsmall)
        for copy in load_weights:
            copy.start()
        first_sum.greet()
        load_x.start()
        load_base.start()
        load_back.start()
        for copy in load_weights:
            copy.wait()

    @pl.when(pid < steps)
    def _():
        def between(step_no):
            slot = pid * pairs + step_no
            for number, at in enumerate(slots):
                pl.when(slot == at)(functools.partial(first_phase, number))

        scan_back_block(
            coef, act_in, size_in, step_in, scan_grad, flags, starts, step_w, decay_t, skip,
            act_grads.at[lax.rem(pid, 2)], coef_grads.at[pid], small, scan_spare, between,
        )
        coef_copy(pid).start()

    @pl.when(pid > 0)
    def _():
        late = pid - 1
        coef_copy(late).wait()
        coef_low = (coef_grads[late] + coef_got[late]).astype(BF16)
        here = pl.ds(pl.multiple_of((steps - 1 - late) * block, block), block)
        conv_back_block(
            coef_low, pre_late, act_grads.at[lax.rem(late, 2)], conv_in, normed, flags_late, state_w,
            taps, ext, gconv, gsmall, mix_low.at[here], taps_at,
        )

    @pl.when(pid == steps)
    def _():
        width = gconv.shape[0]
        small[rank : rank + states, :] = small[rank : rank + states, :] * -jnp.exp(decay_t[...])
        gsmall[coefs:taps_at, :] = small[...]
        gsmall[taps_at + 6 : taps_at + 7, :] = gain_grad[...]
        pack_last[0:width, :] = gconv[...].astype(BF16)
        pack_last[width : width + 128, :] = gsmall[...].astype(BF16)
        last_sum.phase(0)
        load_x.wait()
        load_back.wait()
        gain_sum = jnp.zeros((1, width), F32)
        for i in range(steps):
            here = slice((steps - 1 - i) * block, (steps - i) * block)
            total = back[here, :] + dot_nt(mix_low[here, :], w_conv[...])
            back[here, :] = total
            low[here, :] = total.astype(BF16)
            low_copy(i).start()
            u = x_s[here, :].astype(F32)
            gain_sum += jnp.sum(total * u * rms_scale(u), axis=0, keepdims=True)
        pack_last[width + 128 :, :] = jnp.concatenate(
            [gain_sum, jnp.zeros((15, width), F32)], axis=0
        ).astype(BF16)
        for number in range(len(slots), first_sum.phases - 1):
            first_sum.phase(number)
        last_sum.phase(1)
        for i in range(steps):
            low_copy(i).wait()
        load_base.wait()
        chosen = (1 - core).astype(F32)
        half = kept.shape[0]

        def finish(at, target):
            def part(i, unused):
                here = pl.ds(pl.multiple_of(at + i * 64, 64), 64)
                there = pl.ds(pl.multiple_of(i * 64, 64), 64)
                u = x_s[here, :].astype(F32)
                total = back[here, :] + low_got[here, :].astype(F32)
                backward = rms_back(u, rms_scale(u), gain[...], total)
                target[there, :] = (base_s[here, :] + chosen * backward).astype(target.dtype)
                return unused

            lax.fori_loop(0, half // 64, part, 0)

        finish((1 - row) * half, sent)
        pieces = 4
        passing = [
            remote(
                sent.at[pl.ds(i * (half // pieces), half // pieces)],
                got.at[pl.ds(i * (half // pieces), half // pieces)], pass_sems, i, {"inner": 1 - row},
            )
            for i in range(pieces)
        ]
        finish(row * half, kept)
        keep = pltpu.make_async_copy(kept, kept_o, local_sems.at[2])
        keep.start()
        first_sum.phase(first_sum.phases - 1)
        store_first = both_copies(first_sum, early_o, local_sems, 3)
        for copy in store_first:
            copy.start()
        for number in range(2, last_sum.phases):
            last_sum.phase(number)
            if number - 2 < pieces:
                passing[number - 2].start()
        store_last = both_copies(last_sum, late_o, local_sems, 5)
        for copy in passing:
            copy.wait()
        store_got = pltpu.make_async_copy(got, got_o, local_sems.at[7])
        store_got.start()
        for copy in store_last:
            copy.start()
        for copy in store_first + store_last + [keep, store_got]:
            copy.wait()


def assemble_kernel(
    sizes, sel, kept, got, query_key, value, mixed, out, gate, conv, small, gains,
    results_o, in_o, out_o, query_o, key_o, value_o, mixed_o,
    state_o, step_o, decay_o, step_bias_o, skip_o, taps_o, conv_bias_o, gain_o, attn_gain_o,
):
    first = sel[1] == 0
    mine, other = kept[...], got[...].astype(F32)
    results_o[0, 0] = jnp.where(first, mine, other)
    results_o[0, 1] = jnp.where(first, other, mine)
    half = conv.shape[2]
    cut = query_key.shape[2] // 2
    for part in range(2):
        here = slice(part * cut, (part + 1) * cut)
        in_o[:, part * half : (part + 1) * half] = conv[part].astype(F32)
        in_o[:, (2 + part) * half : (3 + part) * half] = gate[part].astype(F32)
        query_o[:, here] = query_key[part, :, :cut].astype(F32)
        key_o[:, here] = query_key[part, :, cut:].astype(F32)
        value_o[0, :, here] = value[part, :, :cut].astype(F32)
        value_o[1, :, here] = value[part, :, cut:].astype(F32)
    out_o[...] = out[...].astype(F32)
    mixed_o[...] = mixed[...].astype(F32)
    both = jnp.concatenate([small[0].astype(F32), small[1].astype(F32)], axis=1)
    coefs, rank, states = sizes
    at = 0
    for target, size in (
        (state_o, coefs), (step_o, rank), (decay_o, states), (step_bias_o, 1), (skip_o, 1),
        (None, 6), (taps_o, 4), (conv_bias_o, 1),
    ):
        if target is not None:
            target[...] = both[at : at + size]
        at += size
    gain_o[...] = gains[0, 0:1].astype(F32) + gains[1, 0:1].astype(F32)
    attn_gain_o[...] = both[at + 1 : at + 2, :half]


def local(
    layer_input, output_grad, document_ids, mamba_gain, in_proj, conv_weight, conv_bias, state_proj,
    step_proj, step_bias, decay_log, skip_gain, out_proj, attn_gain, query_proj, key_proj, value_proj,
    mixed_proj,
):
    _, piece_len, width = layer_input.shape
    length = output_grad.shape[1]
    parts = lax.axis_size("kind")
    half = in_proj.shape[1] // (2 * parts)
    states = decay_log.shape[1]
    rank = step_proj.shape[0]
    coefs = state_proj.shape[1]
    head_cols = width // parts
    heads = head_cols // HEAD_DIM
    core = lax.axis_index("kind")
    row = lax.axis_index("inner")
    sel = jnp.stack([core, row]).astype(jnp.int32)
    steps = length // ROWS_STEP

    def swap(value, axis):
        return jax.tree.map(lambda v: lax.ppermute(v, axis, [(0, 1), (1, 0)]), value)

    ids = lax.dynamic_index_in_dim(document_ids, row, 0, keepdims=False)
    first = jnp.sum((ids[None, :] < ids[:, None]).astype(jnp.int32), axis=1)
    since = jnp.arange(length, dtype=jnp.int32) - first
    after = jnp.concatenate([since, jnp.zeros((4,), jnp.int32)])
    flags = jnp.stack(
        [since >= j for j in range(4)] + [after[j : j + length] >= max(j, 1) for j in range(4)],
        axis=1,
    ).astype(F32)
    first = first[None, :]
    taps = conv_weight.T
    state_t = state_proj.T
    decay_t = decay_log.T
    conv_b, step_b, skip = conv_bias[None, :], step_bias[None, :], skip_gain[None, :]
    gain_a, gain_b = mamba_gain[None, :], attn_gain[None, :]

    def rows(array):
        return (array, (ROWS_STEP, array.shape[1]), lambda i, sel: (i, 0))

    def rows_rev(array):
        return (array, (ROWS_STEP, array.shape[1]), lambda i, sel: (steps - 1 - i, 0))

    def cols(array):
        return (array, (array.shape[0], ROWS_STEP), lambda i, sel: (0, i))

    def cols_rev(array):
        return (array, (array.shape[0], ROWS_STEP), lambda i, sel: (0, steps - 1 - i))

    def full(array):
        return (array,) + whole(array.shape)

    def half_cols(array, size, shift=0):
        return (array, (array.shape[0], size), lambda i, sel: (0, sel[0] + shift))

    def half_rows(array, size):
        return (array, (size, array.shape[1]), lambda i, sel: (sel[0], 0))

    def out_rows(size, dtype):
        return ((length, size), dtype, (ROWS_STEP, size), lambda i, sel: (i, 0))

    def out_rows_rev(size, dtype):
        return ((length, size), dtype, (ROWS_STEP, size), lambda i, sel: (steps - 1 - i, 0))

    def out_whole(shape, dtype=F32):
        return (shape, dtype) + whole(shape)

    w_conv = half_cols(in_proj, half)
    w_gate = half_cols(in_proj, half, parts)
    taps_half = half_cols(taps, half)
    state_half = half_cols(state_t, half)
    step_half = half_cols(step_proj, half)
    decay_half = half_cols(decay_t, half)
    skip_half = half_cols(skip, half)
    out_half = half_rows(out_proj, half)

    small_rows = rank + states + 8
    block_f32 = pltpu.VMEM((half // 128, ROWS_STEP, 128), F32)
    plain_f32 = pltpu.VMEM((ROWS_STEP, half), F32)
    wide = CHUNK * states
    blocks = length // ROWS_STEP
    assert length // CHUNK * states == length
    row_outs = [
        (width, BF16), (width, BF16), (half, F32), (half, F32), (half, F32), None, (half, F32), (half, F32),
        (half, F32), (half, F32),
        (half, BF16), (half, F32), (width, BF16), (width, BF16),
    ]
    row_f32, row_low = pltpu.VMEM((length, half), F32), pltpu.VMEM((length, half), BF16)
    x_low = pltpu.VMEM((length, width), BF16)
    block_coef = (blocks, coefs, ROWS_STEP)
    front_weights = (in_proj, state_t, step_proj, decay_t, skip, taps, conv_b, step_b, out_proj)

    def pair_of_sems(count):
        return [pltpu.SemaphoreType.DMA((count,)), pltpu.SemaphoreType.DMA((count,))]

    (x, normed_a, conv_in, conv_pre, gate_z, coef, step_pre, step_size, conv_act, scan_out, gated, starts, branch,
     branch_other) = pl.pallas_call(
        front_kernel,
        in_specs=[pl.BlockSpec(memory_space=pltpu.VMEM)] * 2 + [pl.BlockSpec(memory_space=pl.ANY)]
        + [(pl.BlockSpec(memory_space=pl.ANY),) * len(front_weights)],
        out_specs=[pl.BlockSpec(memory_space=pl.ANY)] * len(row_outs),
        out_shape=[
            jax.ShapeDtypeStruct(block_coef, F32) if out is None
            else jax.ShapeDtypeStruct((length, out[0]), out[1])
            for out in row_outs
        ],
        scratch_shapes=[
            x_low, x_low, pltpu.VMEM((length + 8, half), F32), row_f32, row_f32,
            pltpu.VMEM(block_coef, F32), pltpu.VMEM(block_coef, F32), pltpu.VMEM(block_coef, F32),
            row_f32, row_f32, row_f32, row_f32, row_low, row_f32, x_low, x_low,
            [pltpu.VMEM((width, half), BF16), pltpu.VMEM((width, half), BF16)]
            + [pltpu.VMEM((array.shape[0], half), array.dtype)
               for array in (state_t, step_proj, decay_t, skip, taps, conv_b, step_b)]
            + [pltpu.VMEM((half, width), BF16)],
            [pltpu.VMEM((states, half), F32), block_f32, block_f32, plain_f32,
             pltpu.VMEM((ROWS_STEP, wide), BF16), pltpu.VMEM((STRETCH * wide, half), BF16)],
            pltpu.SemaphoreType.DMA((11,)), pair_of_sems(2), pair_of_sems(blocks), pair_of_sems(blocks),
            pltpu.SemaphoreType.DMA((11, blocks)), pltpu.SemaphoreType.DMA((3,)),
        ],
        compiler_params=pltpu.CompilerParams(
            vmem_limit_bytes=VMEM_BYTES, collective_id=2, has_side_effects=True
        ),
        cost_estimate=pl.CostEstimate(
            flops=2 * length * states * half * 1000, bytes_accessed=1 << 24, transcendentals=0
        ),
        name="front",
    )(flags, gain_a, layer_input, front_weights)

    vmem_spec = pl.BlockSpec(memory_space=pltpu.VMEM)
    any_spec = pl.BlockSpec(memory_space=pl.ANY)
    token_head = pltpu.VMEM((heads, length, HEAD_DIM), BF16)
    token_head_f32 = pltpu.VMEM((heads, length, HEAD_DIM), F32)
    head_token = pltpu.VMEM((head_cols, length), BF16)
    scores_f32 = pltpu.VMEM((length, QUERY_BLOCK), F32)
    scores_low = pltpu.VMEM((length, QUERY_BLOCK), BF16)
    tokens_low = pltpu.VMEM((length, width), BF16)
    tokens_f32 = pltpu.VMEM((length, width), F32)
    head_low = pltpu.VMEM((length, head_cols), BF16)
    square = pltpu.VMEM((width, head_cols), BF16)
    pack_rows = width + width // 2 + head_cols + half + width
    counts = [("inner", lax.axis_size("inner")), ("dp", lax.axis_size("dp"))]
    attn_rows = width + width // 2 + head_cols
    most = (pack_rows * 13 // 20 + 128) // 256 * 256
    plan, land = sum_plan(counts, [(0, most, 0), (1, pack_rows - most, 0)])
    base, scan_grad, gate_back, pack_early, g_attn_gain = pl.pallas_call(
        middle_kernel,
        in_specs=[vmem_spec] * 5 + [any_spec] * 5 + [(any_spec,) * 6],
        out_specs=[any_spec] * 4 + [vmem_spec],
        out_shape=[
            jax.ShapeDtypeStruct((length, width), F32),
            jax.ShapeDtypeStruct((length, half), F32),
            jax.ShapeDtypeStruct((length, width), F32),
            jax.ShapeDtypeStruct((pack_rows, width), BF16),
            jax.ShapeDtypeStruct((1, width), F32),
        ],
        scratch_shapes=[
            tokens_low, pltpu.VMEM((length, half), BF16), pltpu.VMEM((length, half), F32),
            pltpu.VMEM((length, half), F32), tokens_low, square, square, square,
            pltpu.VMEM((head_cols, width), BF16), pltpu.VMEM((half, width), BF16),
            pltpu.VMEM((width, half), BF16),
            tokens_low, head_token, token_head, token_head, token_head, head_token, head_token,
            token_head, head_token, head_token, token_head_f32, token_head_f32, token_head_f32,
            scores_f32, scores_f32, scores_f32, scores_low, scores_low,
            head_low, head_low, head_low, tokens_low, tokens_low, tokens_low, tokens_low, tokens_f32,
            pltpu.VMEM((length, half), F32), tokens_f32, pltpu.VMEM((half, width), F32),
            pltpu.VMEM((width, half), F32), pltpu.VMEM((pack_rows, width), BF16),
            pltpu.SemaphoreType.DMA((11,)),
            [pltpu.SemaphoreType.DMA((2 * blocks,)), pltpu.SemaphoreType.DMA((2 * blocks,))],
            pltpu.SemaphoreType.DMA((3, blocks)),
        ],
        compiler_params=pltpu.CompilerParams(
            vmem_limit_bytes=VMEM_BYTES, collective_id=3, has_side_effects=True
        ),
        cost_estimate=pl.CostEstimate(
            flops=2 * length * length * width * 10, bytes_accessed=1 << 24, transcendentals=0
        ),
        name="middle",
    )(x, branch, branch_other, first, gain_b, output_grad, gated, gate_z, scan_out, normed_a,
      (query_proj, key_proj, value_proj, mixed_proj, out_proj, in_proj))

    last_rows = width + 144
    plan_last, land_last = sum_plan(
        counts, [(0, width // 2, 0), (0, width // 2, 0), (1, 128, 0), (0, 16, -1)]
    )
    tile_f32 = pltpu.VMEM((2, half // 128, wide, 128), F32)
    tile_low = pltpu.VMEM((2, wide, half), BF16)
    own_f32 = pltpu.VMEM((ROWS_STEP, wide), F32)

    def now(i):
        return jnp.maximum(steps - 1 - i, 0)

    def late_at(i):
        return jnp.minimum(steps - i, steps - 1)

    def back_rows(array, at):
        return (array, (ROWS_STEP, array.shape[1]), lambda i: (at(i), 0))

    def fixed(array):
        return (array, array.shape, None)

    ins = [
        (coef, (None, coefs, ROWS_STEP), lambda i: (now(i), 0, 0)), back_rows(conv_act, now),
        back_rows(step_size, now), back_rows(step_pre, now),
        back_rows(scan_grad, now), back_rows(flags, now),
        (starts, (ROWS_STEP // CHUNK * states, half), lambda i: (now(i), 0)),
        back_rows(conv_pre, late_at), back_rows(conv_in, late_at), back_rows(normed_a, late_at),
        back_rows(flags, late_at), fixed(gain_a), fixed(g_attn_gain), fixed(pack_early),
    ]
    weights_all = (step_proj, decay_t, skip, state_t, taps, in_proj)
    specs = [
        pl.BlockSpec(block, lambda i: (0, 0), pipeline_mode=pl.Buffered(1)) if at is None
        else pl.BlockSpec(block, at)
        for _, block, at in ins
    ]
    early, late, kept, got = pl.pallas_call(
        functools.partial(back_kernel, plan, plan_last, steps),
        grid=(steps + 1,),
        in_specs=specs + [any_spec] * 3 + [(any_spec,) * len(weights_all)],
        out_specs=[any_spec] * 4,
        out_shape=[
            jax.ShapeDtypeStruct((parts,) + pack_early.shape, BF16),
            jax.ShapeDtypeStruct((parts, last_rows, width), BF16),
            jax.ShapeDtypeStruct((piece_len, width), F32),
            jax.ShapeDtypeStruct((piece_len, width), BF16),
        ],
        scratch_shapes=[pltpu.VMEM((array.shape[0], half), array.dtype) for array in weights_all] + [
            pltpu.SemaphoreType.DMA((len(weights_all),)),
            [pltpu.VMEM((states, half), F32), block_f32,
             block_f32, block_f32, block_f32, pltpu.VMEM((ROWS_STEP, wide), BF16), plain_f32,
             plain_f32, own_f32, own_f32, tile_f32, tile_f32, tile_low, tile_low, tile_low],
            pltpu.VMEM((small_rows, half), F32),
            pltpu.VMEM((2, ROWS_STEP, half), F32),
            pltpu.VMEM((steps, coefs, ROWS_STEP), F32),
            pltpu.VMEM((steps, coefs, ROWS_STEP), F32),
            pltpu.VMEM((ROWS_STEP + 8, half), F32),
            pltpu.VMEM((width, half), F32),
            pltpu.VMEM((128, half), F32),
            pltpu.VMEM((length, half), BF16),
            pltpu.VMEM((length, width), F32),
            pltpu.VMEM((length, width), BF16),
            pltpu.VMEM((length, width), BF16),
            pltpu.VMEM((length, width), BF16),
            pltpu.VMEM((length, width), F32),
            pltpu.VMEM((piece_len, width), F32),
            pltpu.VMEM((piece_len, width), BF16),
            pltpu.VMEM((piece_len, width), BF16),
            pltpu.VMEM((last_rows, width), BF16),
            sum_scratch(plan, pack_early.shape[0], land, width),
            sum_scratch(plan_last, last_rows, land_last, width),
            [pltpu.SemaphoreType.DMA((steps,)), pltpu.SemaphoreType.DMA((steps,))],
            [pltpu.SemaphoreType.DMA((steps,)), pltpu.SemaphoreType.DMA((steps,))],
            [pltpu.SemaphoreType.DMA((16,)), pltpu.SemaphoreType.DMA((16,))],
            pltpu.SemaphoreType.DMA((9,)),
        ],
        compiler_params=pltpu.CompilerParams(
            dimension_semantics=("arbitrary",), vmem_limit_bytes=VMEM_BYTES, collective_id=1,
            has_side_effects=True,
        ),
        cost_estimate=pl.CostEstimate(
            flops=2 * length * states * half * 3000, bytes_accessed=1 << 25, transcendentals=0
        ),
        name="back",
    )(*[a for a, _, _ in ins], x, base, gate_back, weights_all)
    cuts = 8
    quarter = width // cuts
    eighth = width // (2 * cuts)

    def from_sum(total, size, first_row):
        return (total, (parts, size, width), lambda i, sel: (0, first_row // size + i, 0))

    def out_parts(size):
        return ((parts, cuts * size, width), F32, (parts, size, width), lambda i, sel: (0, i, 0))

    results, t_in, t_out, t_query, t_key, t_value, t_mixed, *smalls = call(
        functools.partial(assemble_kernel, (coefs, rank, states)), sel, cuts,
        [(kept, (piece_len // cuts, width), lambda i, sel: (i, 0)),
         (got, (piece_len // cuts, width), lambda i, sel: (i, 0)),
         from_sum(early, quarter, 0), from_sum(early, eighth, width),
         from_sum(early, eighth, width + width // 2), from_sum(early, quarter, attn_rows),
         from_sum(early, quarter, attn_rows + half), from_sum(late, quarter, 0),
         (late, (parts, 128, width), lambda i, sel: (0, width // 128, 0)),
         (late, (parts, 16, width), lambda i, sel: (0, (width + 128) // 16, 0))],
        [((1, 2, piece_len, width), F32, (1, 2, piece_len // cuts, width), lambda i, sel: (0, 0, i, 0)),
         ((width, 4 * half), F32, (quarter, 4 * half), lambda i, sel: (i, 0)),
         out_parts(quarter), ((width, width), F32, (quarter, width), lambda i, sel: (i, 0)),
         ((width, width), F32, (quarter, width), lambda i, sel: (i, 0)), out_parts(eighth),
         out_parts(eighth)]
        + [out_whole((size, parts * half)) for size in (coefs, rank, states, 1, 1, 4, 1)]
        + [out_whole((1, width))] * 2,
        [], 0, "assemble",
    )
    t_state, t_step, t_decay, t_step_bias, t_skip, t_taps, t_conv_bias, t_gain, t_attn_gain = smalls
    return (
        results, t_gain[0], t_in, t_taps.T, t_conv_bias[0], t_state.T, t_step, t_step_bias[0],
        t_decay.T, t_skip[0], t_out.reshape(out_proj.shape), t_attn_gain[0], t_query, t_key,
        t_value.reshape(width, width), t_mixed.reshape(width, width),
    )


def solution(mesh):
    in_specs = (P("dp", "inner", None), P("dp", None, None), P("dp", None)) + (P(),) * 15
    out_specs = (P("kind", "dp", "inner", None),) + (P(),) * 15
    return jax.shard_map(local, mesh=mesh, in_specs=in_specs, out_specs=out_specs, check_vma=False)
```

```python
import functools

import jax
import jax.numpy as jnp
from jax import lax
from jax.experimental import pallas as pl
from jax.experimental.pallas import tpu as pltpu
from jax.sharding import PartitionSpec as P

HEAD_DIM = 64
EPS = 1e-05
NEG = -1e30
FAR = 1e30
CHUNK = 16
STRETCH = 8
ROWS_STEP = 256
QUERY_BLOCK = 256
KEY_TILE = 64
VMEM_BYTES = 58 * 1024 * 1024
F32 = jnp.float32
BF16 = jnp.bfloat16


def dot_nn(a, b):
    return lax.dot_general(a, b, (((1,), (0,)), ((), ())), preferred_element_type=F32)


def dot_nt(a, b):
    return lax.dot_general(a, b, (((1,), (1,)), ((), ())), preferred_element_type=F32)


def dot_tn(a, b):
    return lax.dot_general(a, b, (((0,), (0,)), ((), ())), preferred_element_type=F32)


def silu_slope(tensor):
    sigma = jax.nn.sigmoid(tensor)
    return sigma * (1.0 + tensor * (1.0 - sigma))


def rms_scale(tensor):
    return lax.rsqrt(jnp.mean(tensor * tensor, axis=-1, keepdims=True) + EPS)


def softplus(tensor):
    return jnp.maximum(tensor, 0.0) + jnp.log1p(jnp.exp(-jnp.abs(tensor)))


def rms_back(tensor, factor, gain_vec, gradient):
    weighted = gradient * gain_vec
    spread = jnp.mean(weighted * tensor, axis=-1, keepdims=True)
    return factor * weighted - tensor * (factor * factor * factor) * spread


def spread(ref, value):
    for c in range(ref.shape[0]):
        ref[c] = value[:, c * 128 : (c + 1) * 128]


def row_of(ref, c, row, states):
    part = ref[c, pl.ds(row, 8, stride=0), :]
    return jnp.concatenate([part] * (states // 8), axis=0)


def column_of(tile, at):
    return jnp.broadcast_to(tile[:, at : at + 1], tile.shape)


def own_token(chunk, states):
    at = lax.broadcasted_iota(jnp.int32, (chunk, chunk * states), 0)
    of = lax.broadcasted_iota(jnp.int32, (chunk, chunk * states), 1) // states
    return at == of


def state_picks(chunk, states):
    at = lax.broadcasted_iota(jnp.int32, (states, chunk * states), 0)
    of = lax.rem(lax.broadcasted_iota(jnp.int32, (states, chunk * states), 1), states)
    return (at == of).astype(F32).astype(BF16)


def remote(src, dst, sems, number, to):
    return pltpu.make_async_remote_copy(
        src_ref=src, dst_ref=dst, send_sem=sems[0].at[number], recv_sem=sems[1].at[number],
        device_id=to, device_id_type=pl.DeviceIdType.MESH,
    )


def call(body, sel, steps, ins, outs, scratch, flops, name):
    bytes_all = sum(a.size * a.dtype.itemsize for a, _, _ in ins)
    return pl.pallas_call(
        body,
        grid_spec=pltpu.PrefetchScalarGridSpec(
            num_scalar_prefetch=1,
            grid=(steps,),
            in_specs=[pl.BlockSpec(block, at) for _, block, at in ins],
            out_specs=[pl.BlockSpec(block, at) for _, _, block, at in outs],
            scratch_shapes=scratch,
        ),
        out_shape=[jax.ShapeDtypeStruct(shape, dtype) for shape, dtype, _, _ in outs],
        compiler_params=pltpu.CompilerParams(
            dimension_semantics=("arbitrary",), vmem_limit_bytes=VMEM_BYTES
        ),
        cost_estimate=pl.CostEstimate(flops=flops, bytes_accessed=bytes_all, transcendentals=0),
        name=name,
    )(sel, *[a for a, _, _ in ins])


def whole(shape):
    zeros = (0,) * len(shape)
    return (shape, lambda i, sel: zeros)


def scan_block(
    coef, pre, gate, flags, step_w, step_b, decay_t, skip, out_w,
    step_o, scan_o, gated_o, starts_o, branch_o, spare,
):
    state, stepd, drive, ys, blocked, h_low = spare
    block, width = pre.shape
    states = decay_t.shape[0]
    rank = step_w.shape[0]
    tiles = width // 128

    step_pre = dot_tn(coef[:rank, :].astype(BF16), step_w[...]) + step_b[...]
    step_o[...] = step_pre
    step = softplus(step_pre)
    act = pre[...] * jax.nn.sigmoid(pre[...])
    spread(drive, step * act)
    spread(stepd, jnp.where(flags[:, 1:2] > 0.0, step, FAR))
    neg = -jnp.exp(decay_t[...])
    neg_of = [neg[:, c * 128 : (c + 1) * 128] for c in range(tiles)]
    own_all = jnp.concatenate([own_token(CHUNK, states)] * (block // CHUNK), axis=0)
    blocked[...] = jnp.where(
        own_all, dot_tn(coef[rank + states :, :].astype(BF16), state_picks(CHUNK, states)), 0.0
    ).astype(BF16)

    def one_chunk(i, h, h_s):
        here = pl.ds(pl.multiple_of(i * CHUNK, CHUNK), CHUNK)
        tile = coef[rank : rank + states, pl.ds(pl.multiple_of((i // 8) * 128, 128), 128)]
        tile = pltpu.roll(tile, lax.rem(128 - lax.rem(i, 8) * CHUNK, 128), 1)
        for c in range(tiles):
            starts_o[here, c * 128 : (c + 1) * 128] = h[c]
        for at in range(CHUNK):
            row = i * CHUNK + at
            write = column_of(tile, at)
            for c in range(tiles):
                decay = jnp.exp(neg_of[c] * row_of(stepd, c, row, states))
                h[c] = decay * h[c] + row_of(drive, c, row, states) * write
                h_s[at * states : (at + 1) * states, c * 128 : (c + 1) * 128] = h[c].astype(BF16)
        return h

    def stretch(number, carried):
        def pair(step_no, carried):
            h = list(carried)
            for sub in range(2):
                at = 2 * step_no + sub
                spot = h_low.at[pl.ds(pl.multiple_of(at * CHUNK * states, CHUNK * states), CHUNK * states)]
                h = one_chunk(number * STRETCH + at, h, spot)
            return tuple(h)

        carried = lax.fori_loop(0, STRETCH // 2, pair, carried)
        for at in range(STRETCH):
            here = pl.ds(pl.multiple_of((number * STRETCH + at) * CHUNK, CHUNK), CHUNK)
            spot = slice(at * CHUNK * states, (at + 1) * CHUNK * states)
            ys[here, :] = dot_nn(blocked[here, :], h_low[spot, :])
        return carried

    begin = tuple(state[:, c * 128 : (c + 1) * 128] for c in range(tiles))
    for c, last in enumerate(lax.fori_loop(0, block // (STRETCH * CHUNK), stretch, begin)):
        state[:, c * 128 : (c + 1) * 128] = last
    scan_out = ys[...] + skip[...] * act
    scan_o[...] = scan_out
    z = gate[...]
    gated = (scan_out * (z * jax.nn.sigmoid(z))).astype(BF16)
    gated_o[...] = gated
    branch_o[...] = dot_nn(gated, out_w[...]).astype(BF16)


def front_kernel(
    flags, gain, layer_all, weights_all,
    x_o, normed_o, conv_o, pre_o, gate_o, coef_o, step_o, scan_o, gated_o, starts_o, branch_o, branch_other_o,
    x, normed, ext, pre, gate, coef, coef_got, coef_sum, step_pre, scan_out, gated, starts, branch,
    branch_got, weights, scan_spare, load_sems, x_sems, coef_sems, branch_sems, store_sems, late_sems,
):
    length, width = x.shape
    blocks = length // ROWS_STEP
    core, row = lax.axis_index("kind"), lax.axis_index("inner")
    other_core, other_row = {"kind": 1 - core}, {"inner": 1 - row}
    w_conv, w_gate, state_w, step_w, decay_t, skip, taps, conv_b, step_b, out_w = weights
    in_all, state_all, step_all, decay_all, skip_all, taps_all, conv_b_all, step_b_all, out_all = weights_all
    channels = w_conv.shape[1]

    def part_of(number):
        return pl.ds(pl.multiple_of(number * channels, 128), channels)

    def rows_at(b):
        return pl.ds(pl.multiple_of(b * ROWS_STEP, ROWS_STEP), ROWS_STEP)

    mine = part_of(core)
    loads = [
        pltpu.make_async_copy(source, target, load_sems.at[i])
        for i, (source, target) in enumerate((
            (layer_all.at[row], x.at[pl.ds(pl.multiple_of(row * (length // 2), 256), length // 2)]),
            (in_all.at[:, mine], w_conv), (in_all.at[:, part_of(2 + core)], w_gate),
            (state_all.at[:, mine], state_w), (step_all.at[:, mine], step_w),
            (decay_all.at[:, mine], decay_t), (skip_all.at[:, mine], skip), (taps_all.at[:, mine], taps),
            (conv_b_all.at[:, mine], conv_b), (step_b_all.at[:, mine], step_b), (out_all.at[mine], out_w),
        ))
    ]
    barrier = pltpu.get_barrier_semaphore()
    for device in (other_core, other_row):
        pl.semaphore_signal(barrier, inc=1, device_id=device, device_id_type=pl.DeviceIdType.MESH)
    pl.semaphore_wait(barrier, 2)
    sent = remote(
        layer_all.at[1 - row, rows_at(core)], x.at[rows_at(row * (blocks // 2) + core)], x_sems, 0, other_row
    )
    sent.start()
    for load in loads:
        load.start()
    for load in loads:
        load.wait()
    ext[0:8, :] = jnp.zeros((8, channels), F32)
    scan_spare[0][...] = jnp.zeros_like(scan_spare[0])

    results = (
        (x, x_o), (normed, normed_o), (gate, gate_o), (pre, pre_o), (step_pre, step_o),
        (scan_out, scan_o), (gated, gated_o), (starts, starts_o), (branch, branch_o),
    )

    def stores(b, numbers=range(len(results))):
        rows = rows_at(b)
        return [
            pltpu.make_async_copy(results[i][0].at[rows], results[i][1].at[rows], store_sems.at[i, b])
            for i in numbers
        ]

    def project(b):
        rows = rows_at(b)
        u = x[rows, :].astype(F32)
        low = (u * rms_scale(u) * gain[...]).astype(BF16)
        normed[rows, :] = low
        ext[pl.ds(pl.multiple_of(b * ROWS_STEP + 8, 8), ROWS_STEP), :] = dot_nn(low, w_conv[...])
        gate[rows, :] = dot_nn(low, w_gate[...])
        for store in stores(b, range(3)):
            store.start()

    first_other = (1 - row) * (blocks // 2)
    project(row * (blocks // 2))
    project(row * (blocks // 2) + 1)
    sent.wait()
    fetched = x.at[rows_at(first_other + core)]
    passed = remote(fetched, fetched, x_sems, 1, other_core)
    passed.start()
    project(first_other + core)
    passed.wait()
    project(first_other + 1 - core)
    store_conv = pltpu.make_async_copy(ext.at[pl.ds(8, length)], conv_o, late_sems.at[0])
    store_conv.start()

    def coef_copy(b):
        return remote(coef.at[b], coef_got.at[b], coef_sems, b, other_core)

    def branch_copy(b):
        rows = rows_at(b)
        return remote(branch.at[rows], branch_got.at[rows], branch_sems, b, other_core)

    for b in range(blocks):
        rows = slice(b * ROWS_STEP, (b + 1) * ROWS_STEP)
        total = conv_b[...] + taps[3:4, :] * ext[8 + b * ROWS_STEP : 8 + (b + 1) * ROWS_STEP, :]
        for j in range(1, 4):
            moved = ext[8 - j + b * ROWS_STEP : 8 - j + (b + 1) * ROWS_STEP, :]
            total = total + taps[3 - j : 4 - j, :] * jnp.where(flags[rows, j : j + 1] > 0.0, moved, 0.0)
        pre[rows, :] = total
        coef[b] = dot_nt(state_w[...], (total * jax.nn.sigmoid(total)).astype(BF16))
        coef_copy(b).start()
        stores(b, [3])[0].start()

    def scan(b, unused):
        rows = rows_at(b)
        coef_copy(b).wait()
        coef_sum[b] = coef[b] + coef_got[b]
        scan_block(
            coef_sum.at[b], pre.at[rows], gate.at[rows], flags.at[rows], step_w, step_b, decay_t, skip, out_w,
            step_pre.at[rows], scan_out.at[rows], gated.at[rows], starts.at[rows], branch.at[rows],
            scan_spare,
        )
        branch_copy(b).start()
        for store in stores(b, range(4, len(results))):
            store.start()
        return unused

    lax.fori_loop(0, blocks, scan, 0)
    store_coef = pltpu.make_async_copy(coef_sum, coef_o, late_sems.at[1])
    store_coef.start()
    for b in range(blocks):
        branch_copy(b).wait()
    store_other = pltpu.make_async_copy(branch_got, branch_other_o, late_sems.at[2])
    store_other.start()
    for copy in (store_conv, store_coef, store_other):
        copy.wait()
    for b in range(blocks):
        for store in stores(b):
            store.wait()


def middle_kernel(
    x, part_a, part_b, first, gain, grads, gated_all, gate_all, scan_all, normed_all, weights_all,
    base_o, scan_grad_o, back_o, pack_o, gain_grad_o,
    grad, gated, gate, scan_out, normed_a, wq, wk, wv, wm, out_w, w_gate,
    normed, q_t, q_n, k_n, v_n, k_t, v_t, g_n, g_t, o_t, dq_n, dk, dv, bias, expo, prob_grad, prob_low,
    score_low,
    dq_low, dk_low, dv_low, branch, branch_got, back, back_got, base, scan_grad, gate_back, gout, ggate,
    pack, load_sems, pass_sems, store_sems,
):
    length, width = x.shape
    core, row = lax.axis_index("kind"), lax.axis_index("inner")
    other_core = {"kind": 1 - core}
    head_cols, channels = wq.shape[1], out_w.shape[0]

    def part_of(size):
        return pl.ds(pl.multiple_of(core * size, 128), size)

    query_all, key_all, value_all, mixed_all, out_all, in_all = weights_all
    gate_cols = pl.ds(pl.multiple_of((2 + core) * channels, 128), channels)
    loads = [
        pltpu.make_async_copy(source, target, load_sems.at[i])
        for i, (source, target) in enumerate((
            (query_all.at[:, part_of(head_cols)], wq), (key_all.at[:, part_of(head_cols)], wk),
            (value_all.at[:, part_of(head_cols)], wv), (grads.at[row], grad),
            (mixed_all.at[part_of(head_cols)], wm), (gated_all, gated), (gate_all, gate),
            (scan_all, scan_out), (normed_all, normed_a), (out_all.at[part_of(channels)], out_w),
            (in_all.at[:, gate_cols], w_gate),
        ))
    ]
    for load in loads:
        load.start()
    barrier = pltpu.get_barrier_semaphore()
    pl.semaphore_signal(barrier, inc=1, device_id=other_core, device_id_type=pl.DeviceIdType.MESH)
    pl.semaphore_wait(barrier, 1)
    for load in loads[:5]:
        load.wait()

    heads = k_n.shape[0]
    scale = HEAD_DIM**-0.5
    for b in range(length // ROWS_STEP):
        rows = slice(b * ROWS_STEP, (b + 1) * ROWS_STEP)
        middle = x[rows, :].astype(F32) + (part_a[rows, :].astype(F32) + part_b[rows, :].astype(F32))
        normed_blk = (middle * rms_scale(middle) * gain[...]).astype(BF16)
        normed[rows, :] = normed_blk
        query = dot_nn(normed_blk, wq[...]).astype(BF16).astype(F32) * scale
        keys = dot_nn(normed_blk, wk[...]).astype(BF16).astype(F32)
        values = dot_nn(normed_blk, wv[...]).astype(BF16).astype(F32)
        out_grad = dot_nt(grad[rows, :], wm[...]).astype(BF16).astype(F32)
        q_t[:, rows] = query.T.astype(BF16)
        k_t[:, rows] = (keys.T * scale).astype(BF16)
        v_t[:, rows] = values.T.astype(BF16)
        g_t[:, rows] = out_grad.T.astype(BF16)
        for h in range(heads):
            cols = slice(h * HEAD_DIM, (h + 1) * HEAD_DIM)
            q_n[h, rows, :] = query[:, cols].astype(BF16)
            k_n[h, rows, :] = keys[:, cols].astype(BF16)
            v_n[h, rows, :] = values[:, cols].astype(BF16)
            g_n[h, rows, :] = out_grad[:, cols].astype(BF16)
    dk[...] = jnp.zeros_like(dk)
    dv[...] = jnp.zeros_like(dv)

    for block in range(length // QUERY_BLOCK):
        cols = slice(block * QUERY_BLOCK, (block + 1) * QUERY_BLOCK)
        reach = (block + 1) * QUERY_BLOCK
        key_at = lax.broadcasted_iota(jnp.int32, (reach, QUERY_BLOCK), 0)
        query_at = lax.broadcasted_iota(jnp.int32, (reach, QUERY_BLOCK), 1) + block * QUERY_BLOCK
        kept = (key_at >= first[:, cols]) & (key_at <= query_at)
        bias[0:reach, :] = jnp.where(kept, 0.0, NEG)

        def one_head(h, unused):
            dims = pl.ds(pl.multiple_of(h * HEAD_DIM, HEAD_DIM), HEAD_DIM)
            tiles = [slice(t * KEY_TILE, (t + 1) * KEY_TILE) for t in range(reach // KEY_TILE)]

            def by_eight(tile):
                return tile.reshape(KEY_TILE // 8, 8, QUERY_BLOCK)

            query, out_grad = q_t[dims, cols], g_t[dims, cols]
            most = jnp.full((8, QUERY_BLOCK), NEG, F32)
            for keys in tiles:
                scores = dot_nn(k_n[h, keys, :], query) + bias[keys, :]
                expo[keys, :] = scores
                most = jnp.maximum(most, jnp.max(by_eight(scores), axis=0))
            most = jnp.max(most, axis=0, keepdims=True)
            total = jnp.zeros((8, QUERY_BLOCK), F32)
            centre = jnp.zeros((8, QUERY_BLOCK), F32)
            for keys in tiles:
                exponent = jnp.exp(expo[keys, :] - most)
                grads = dot_nn(v_n[h, keys, :], out_grad)
                expo[keys, :] = exponent
                prob_grad[keys, :] = grads
                total = total + jnp.sum(by_eight(exponent), axis=0)
                centre = centre + jnp.sum(by_eight(exponent * grads), axis=0)
            scale_by = 1.0 / jnp.sum(total, axis=0, keepdims=True)
            centre = jnp.sum(centre, axis=0, keepdims=True) * scale_by
            for keys in tiles:
                prob = expo[keys, :] * scale_by
                prob_low[keys, :] = prob.astype(BF16)
                score_low[keys, :] = (prob * (prob_grad[keys, :] - centre)).astype(BF16)
            o_t[dims, cols] = dot_nn(v_t[dims, 0:reach], prob_low[0:reach, :]).astype(BF16)
            dq_n[h, cols, :] = dot_nn(k_t[dims, 0:reach], score_low[0:reach, :]).T
            dk[h, 0:reach, :] += dot_nn(score_low[0:reach, :], q_n[h, cols, :])
            dv[h, 0:reach, :] += dot_nn(prob_low[0:reach, :], g_n[h, cols, :])
            return unused

        lax.fori_loop(0, heads, one_head, 0)

    blocks = length // ROWS_STEP

    def rows_at(b):
        return pl.ds(pl.multiple_of(b * ROWS_STEP, ROWS_STEP), ROWS_STEP)

    def back_copy(b):
        return remote(back.at[rows_at(b)], back_got.at[rows_at(b)], pass_sems, b, other_core)

    def branch_copy(b):
        there = branch_got.at[rows_at(b)]
        return remote(branch.at[rows_at(b)], there, pass_sems, blocks + b, other_core)

    def partials(b, unused):
        rows = rows_at(b)
        for target, source in ((dq_low, dq_n), (dk_low, dk), (dv_low, dv)):
            joined = jnp.concatenate([source[h, rows, :] for h in range(heads)], axis=1)
            target[rows, :] = joined.astype(BF16)
        total = dot_nt(dq_low[rows, :], wq[...]) + dot_nt(dk_low[rows, :], wk[...])
        back[rows, :] = (total + dot_nt(dv_low[rows, :], wv[...])).astype(BF16)
        back_copy(b).start()
        branch[rows, :] = dot_tn(o_t[:, rows], wm[...]).astype(BF16)
        branch_copy(b).start()
        return unused

    lax.fori_loop(0, blocks, partials, 0)
    cut = width // 2
    attn_rows = width + cut + head_cols
    pack[0:width, 0:head_cols] = dot_tn(normed[...], dq_low[...]).astype(BF16)
    pack[0:width, head_cols:] = dot_tn(normed[...], dk_low[...]).astype(BF16)
    value_grad = dot_tn(normed[...], dv_low[...]).astype(BF16)
    pack[width : width + cut, 0:head_cols] = value_grad[:cut]
    pack[width : width + cut, head_cols:] = value_grad[cut:]
    pack[width + cut : attn_rows, :] = dot_nn(o_t[...], grad[...]).astype(BF16)
    for load in loads[5:]:
        load.wait()
    gout[...] = jnp.zeros_like(gout)
    ggate[...] = jnp.zeros_like(ggate)
    gain_grad_o[...] = jnp.zeros_like(gain_grad_o)

    def stores(b):
        rows = rows_at(b)
        return [
            pltpu.make_async_copy(source.at[rows], target.at[rows], store_sems.at[i, b])
            for i, (source, target) in enumerate(
                ((base, base_o), (scan_grad, scan_grad_o), (gate_back, back_o))
            )
        ]

    def gating(b, unused):
        rows = rows_at(b)
        back_copy(b).wait()
        branch_copy(b).wait()
        middle = x[rows, :].astype(F32) + (part_a[rows, :].astype(F32) + part_b[rows, :].astype(F32))
        total = back[rows, :].astype(F32) + back_got[rows, :].astype(F32)
        factor = rms_scale(middle)
        middle_grad = grad[rows, :].astype(F32) + rms_back(middle, factor, gain[...], total)
        gain_grad_o[...] += jnp.sum(total * middle * factor, axis=0, keepdims=True)
        layer_out = middle + (branch[rows, :].astype(F32) + branch_got[rows, :].astype(F32))
        chosen = (1 - core).astype(F32)
        base[rows, :] = chosen * middle_grad + (1.0 - chosen) * layer_out
        low = middle_grad.astype(BF16)
        gout[...] += dot_tn(gated[rows, :], low)
        gated_grad = dot_nt(low, out_w[...])
        z = gate[rows, :]
        sigma = jax.nn.sigmoid(z)
        scan_grad[rows, :] = gated_grad * (z * sigma)
        slope = sigma * (1.0 + z * (1.0 - sigma))
        gate_low = (gated_grad * scan_out[rows, :] * slope).astype(BF16)
        ggate[...] += dot_tn(normed_a[rows, :], gate_low)
        gate_back[rows, :] = dot_nt(gate_low, w_gate[...])
        for store in stores(b):
            store.start()
        return unused

    lax.fori_loop(0, blocks, gating, 0)
    pack[attn_rows : attn_rows + channels, :] = gout[...].astype(BF16)
    pack[attn_rows + channels :, :] = ggate[...].astype(BF16)
    last = pltpu.make_async_copy(pack, pack_o, load_sems.at[0])
    last.start()
    for b in range(blocks):
        for store in stores(b):
            store.wait()
    last.wait()


def scan_back_block(
    coef, pre, step_in, scan_grad, flags, starts, step_w, decay_t, skip,
    act_grad, coef_grad, small, spare, between,
):
    (state, steps, stepd, drive, reads, blocked, d_drive, d_expo, in_own, read_own,
     decays, decayed, h_low, sum_low, expo_low) = spare
    block, width = pre.shape
    states = decay_t.shape[0]
    rank = step_w.shape[0]
    tiles = width // 128
    wide = CHUNK * states

    step_pre = step_in[...]
    step = softplus(step_pre)
    act = pre[...] * jax.nn.sigmoid(pre[...])
    spread(steps, step)
    spread(drive, step * act)
    spread(stepd, jnp.where(flags[:, 1:2] > 0.0, step, FAR))
    spread(reads, scan_grad[...])
    neg = -jnp.exp(decay_t[...])
    neg_of = [neg[:, c * 128 : (c + 1) * 128] for c in range(tiles)]
    picks = state_picks(CHUNK, states)
    own = own_token(CHUNK, states)
    own_low = own.astype(F32).astype(BF16)
    own_all = jnp.concatenate([own] * (block // CHUNK), axis=0)
    blocked[...] = jnp.where(
        own_all, dot_tn(coef[rank : rank + states, :].astype(BF16), picks), 0.0
    ).astype(BF16)

    def one_chunk(i, backward, spare):
        decay_s, decayed_s, h_s, sum_s, expo_s = spare
        rows16 = pl.ds(pl.multiple_of(i * CHUNK, CHUNK), CHUNK)
        tile = coef[rank:, pl.ds(pl.multiple_of((i // 8) * 128, 128), 128)]
        tile = pltpu.roll(tile, lax.rem(128 - lax.rem(i, 8) * CHUNK, 128), 1)
        h = [starts[rows16, c * 128 : (c + 1) * 128] for c in range(tiles)]
        for at in range(CHUNK):
            row = i * CHUNK + at
            here = slice(at * states, (at + 1) * states)
            write = column_of(tile[:states], at)
            for c in range(tiles):
                cols = slice(c * 128, (c + 1) * 128)
                decay = jnp.exp(neg_of[c] * row_of(stepd, c, row, states))
                kept = decay * h[c]
                h[c] = kept + row_of(drive, c, row, states) * write
                decay_s[c, here, :] = decay
                decayed_s[c, here, :] = kept
                h_s[here, cols] = h[c].astype(BF16)
        total = [jnp.zeros((states, 128), F32)] * tiles
        for at in reversed(range(CHUNK)):
            row = i * CHUNK + at
            here = slice(at * states, (at + 1) * states)
            read = column_of(tile[states:], at)
            for c in range(tiles):
                cols = slice(c * 128, (c + 1) * 128)
                summed = read * row_of(reads, c, row, states) + backward[c]
                sum_s[here, cols] = summed.astype(BF16)
                expo = summed * decayed_s[c, here, :]
                expo_s[here, cols] = (expo * neg_of[c]).astype(BF16)
                total[c] = total[c] + expo * row_of(steps, c, row, states)
                backward[c] = decay_s[c, here, :] * summed
        for c in range(tiles):
            small[rank : rank + states, c * 128 : (c + 1) * 128] += total[c]

        def flat(ref):
            return jnp.concatenate([ref[c, rows16, :] for c in range(tiles)], axis=1).astype(BF16)

        d_drive[rows16, :] = dot_nn(blocked[rows16, :], sum_s[...])
        d_expo[rows16, :] = dot_nn(own_low, expo_s[...])
        in_own[rows16, :] = jnp.where(own, dot_nt(flat(drive), sum_s[...]), 0.0)
        read_own[rows16, :] = jnp.where(own, dot_nt(flat(reads), h_s[...]), 0.0)
        return backward

    def pair(step_no, carried):
        between(step_no)
        backward = list(carried)
        last = block // CHUNK - 1 - 2 * step_no
        for sub in range(2):
            spare = (decays.at[sub], decayed.at[sub], h_low.at[sub], sum_low.at[sub], expo_low.at[sub])
            backward = one_chunk(last - sub, backward, spare)
        return tuple(backward)

    begin = tuple(state[:, c * 128 : (c + 1) * 128] for c in range(tiles))
    for c, last in enumerate(lax.fori_loop(0, block // (2 * CHUNK), pair, begin)):
        state[:, c * 128 : (c + 1) * 128] = last

    def by_state(ref):
        high = ref[...].astype(BF16)
        rest = (ref[...] - high.astype(F32)).astype(BF16)
        return dot_nt(picks, high) + dot_nt(picks, rest)

    coef_grad[rank : rank + states, :] = by_state(in_own)
    coef_grad[rank + states :, :] = by_state(read_own)

    drive_grad = d_drive[...]
    pre_grad = (d_expo[...] + drive_grad * act) * jax.nn.sigmoid(step_pre)
    tail = rank + states
    small[tail : tail + 1, :] += jnp.sum(pre_grad, axis=0, keepdims=True)
    pre_low = pre_grad.astype(BF16)
    small[:rank, :] += dot_nn(coef[:rank, :].astype(BF16), pre_low)
    coef_grad[:rank, :] = dot_nt(step_w[...], pre_low)
    act_grad[...] = drive_grad * step + scan_grad[...] * skip[...]
    small[tail + 1 : tail + 2, :] += jnp.sum(scan_grad[...] * act, axis=0, keepdims=True)


def conv_back_block(
    coef_grad, pre, act_grad, conv_in, normed, x, gate_back, flags, state_w, taps, w_conv,
    ext, gconv, gsmall, taps_at,
):
    block = pre.shape[0]
    coefs = coef_grad.shape[0]
    v = pre[...]
    sigma = jax.nn.sigmoid(v)
    gsmall[0:coefs, :] += dot_nn(coef_grad, (v * sigma).astype(BF16))
    act_all = act_grad[...] + dot_tn(coef_grad, state_w[...])
    conv_grad = act_all * (sigma * (1.0 + v * (1.0 - sigma)))
    ext[0:block, :] = conv_grad
    conv_in_grad = taps[3:4, :] * conv_grad
    sums = [None] * 4
    sums[3] = jnp.sum(conv_grad * conv_in[...], axis=0, keepdims=True)
    for j in range(1, 4):
        moved = jnp.where(flags[:, 4 + j : 5 + j] > 0.0, ext[j : j + block, :], 0.0)
        sums[3 - j] = jnp.sum(moved * conv_in[...], axis=0, keepdims=True)
        conv_in_grad = conv_in_grad + taps[3 - j : 4 - j, :] * moved
    for j in range(4):
        gsmall[taps_at + j : taps_at + j + 1, :] += sums[j]
    gsmall[taps_at + 4 : taps_at + 5, :] += jnp.sum(conv_grad, axis=0, keepdims=True)
    low = conv_in_grad.astype(BF16)
    gconv[...] += dot_tn(normed[...], low)
    back = gate_back[...] + dot_nt(low, w_conv[...])
    u = x[...].astype(F32)
    gsmall[taps_at + 5 : taps_at + 6, :] += jnp.sum(back * u * rms_scale(u), axis=0, keepdims=True)
    ext[block:, :] = ext[0:8, :]
    return back


def sum_plan(rows, counts):
    bits = [(axis, 1 << i) for axis, size in counts for i in range(size.bit_length() - 1)]
    digits = [bits[i : i + 2] for i in range(0, len(bits), 2)]
    most = (rows * 13 // 20 + 128) // 256 * 256
    sizes = [(0, most), (1, rows - most)] if rows > 1024 else [(0, most // 2), (0, most // 2), (1, rows - most)]
    streams, at, land = [], 0, 0
    for number, size in sizes:
        turn = number % len(digits)
        steps, held = [], size
        for digit in digits[turn:] + digits[:turn]:
            radix = 1 << len(digit)
            split = held % (16 * radix) == 0
            held = held // radix if split else held
            steps.append((digit, split, held, land))
            land += held * (radix - 1)
        streams.append((at, size, steps))
        at += size
    return streams, land


class Summing:
    def __init__(self, plan, src, work, land, full, peer, send, recv):
        self.streams, self.src, self.work, self.land = plan, src, work, land
        self.full, self.peer = full, peer
        self.sems = (send, recv)
        self.turns = len(plan[0][2])
        self.phases = 2 * self.turns + 2
        self.start = []
        for first, _, steps in plan:
            at, spots = first, [first]
            for turn, (digit, split, kept, _) in enumerate(steps):
                at = at + self.index(digit, 0) * kept if split else at
                spots.append(at)
            self.start.append(spots)

    def index(self, digit, flipped):
        total = 0
        for i, (axis, weight) in enumerate(digit):
            place = lax.rem(lax.axis_index(axis) // weight, 2)
            total = total + (1 - place if flipped >> i & 1 else place) * (1 << i)
        return total

    def partner(self, digit, flipped):
        device = {}
        for i, (axis, weight) in enumerate(digit):
            if flipped >> i & 1:
                me = lax.axis_index(axis)
                device[axis] = device.get(axis, me) + weight * (1 - 2 * lax.rem(me // weight, 2))
        return device

    def other_core(self):
        return {"kind": 1 - lax.axis_index("kind")}

    def others(self, s, turn):
        return range(1, 1 << len(self.streams[s][2][turn][0]))

    def rows(self, ref, at, size):
        return ref.at[pl.ds(pl.multiple_of(at, 16), size)]

    def number(self, s, kind, turn, flipped):
        return ((s * 3 + kind) * (self.turns + 1) + turn) * 4 + flipped

    def piece(self, s, turn, flipped):
        digit, split, kept, _ = self.streams[s][2][turn]
        at = self.start[s][turn]
        return at + self.index(digit, flipped) * kept if split else at

    def halves(self, s, turn):
        digit, _, kept, land = self.streams[s][2][turn]
        source = self.src if turn == 0 else self.work
        return [
            remote(
                self.rows(source, self.piece(s, turn, q), kept),
                self.land.at[pl.ds(land + (q - 1) * kept, kept)],
                self.sems, self.number(s, 0, turn, q), self.partner(digit, q),
            )
            for q in self.others(s, turn)
        ]

    def add(self, s, turn):
        _, _, kept, land = self.streams[s][2][turn]
        at = self.start[s][turn + 1]
        source = self.src if turn == 0 else self.work
        target = self.full if turn == self.turns - 1 else self.work

        def step(i, unused):
            here = pl.ds(pl.multiple_of(at + i * 16, 16), 16)
            parts = [source[here, :].astype(F32)]
            for q in self.others(s, turn):
                there = pl.ds(pl.multiple_of(land + (q - 1) * kept + i * 16, 16), 16)
                parts.append(self.land[there, :].astype(F32))
            while len(parts) > 1:
                parts = [parts[i] + parts[i + 1] for i in range(0, len(parts), 2)]
            target[here, :] = parts[0].astype(BF16)
            return unused

        lax.fori_loop(0, kept // 16, step, 0)

    def spreads(self, s, turn):
        digit, split, kept, _ = self.streams[s][2][turn]
        if not split:
            return []
        here = self.rows(self.full, self.start[s][turn + 1], kept)
        return [
            remote(here, here, self.sems, self.number(s, 1, turn, q), self.partner(digit, q))
            for q in self.others(s, turn)
        ]

    def shares(self, s, turn):
        if turn == self.turns:
            found = [(0, self.start[s][turn], self.streams[s][2][-1][2])]
        else:
            _, split, kept, _ = self.streams[s][2][turn]
            found = [(q, self.piece(s, turn, q), kept) for q in self.others(s, turn)] if split else []
        return [
            remote(
                self.rows(self.full, at, size), self.rows(self.peer, at, size), self.sems,
                self.number(s, 2, turn, q), self.other_core(),
            )
            for q, at, size in found
        ]

    def slots(self, count):
        lengths = [2.5 + 14.0 * 0.5**turn for turn in range(self.turns)]
        found, at = [0], 0.0
        for length in lengths + lengths[::-1]:
            at += length * count / 42.0
            if at < count - 1:
                found.append(int(at))
        return found

    def greet(self):
        barrier = pltpu.get_barrier_semaphore()
        partners = [self.other_core()]
        for digit, _, _, _ in self.streams[0][2]:
            partners += [self.partner(digit, q) for q in range(1, 1 << len(digit))]
        for device in partners:
            pl.semaphore_signal(
                barrier, inc=1, device_id=device, device_id_type=pl.DeviceIdType.MESH
            )
        pl.semaphore_wait(barrier, len(partners))

    def begin(self, copies):
        for copy in copies:
            copy.start()

    def finish(self, copies):
        for copy in copies:
            copy.wait()

    def phase(self, number):
        for s in range(len(self.streams)):
            if number == 0:
                self.begin(self.halves(s, 0))
            elif number <= self.turns:
                self.finish(self.halves(s, number - 1))
                self.add(s, number - 1)
                if number < self.turns:
                    self.begin(self.halves(s, number))
                else:
                    self.begin(self.spreads(s, self.turns - 1))
                    self.begin(self.shares(s, self.turns))
            elif number <= 2 * self.turns:
                turn = 2 * self.turns - number
                self.finish(self.spreads(s, turn))
                if turn > 0:
                    self.begin(self.spreads(s, turn - 1))
                self.begin(self.shares(s, turn))
            else:
                for turn in range(self.turns + 1):
                    self.finish(self.shares(s, turn))


def sum_scratch(plan, rows, land, width):
    numbers = len(plan) * 3 * (len(plan[0][2]) + 1) * 4
    return [
        pltpu.VMEM((rows, width), BF16),
        pltpu.VMEM((land, width), BF16),
        pltpu.VMEM((rows, width), BF16),
        pltpu.VMEM((rows, width), BF16),
        pltpu.SemaphoreType.DMA((numbers,)),
        pltpu.SemaphoreType.DMA((numbers,)),
    ]


def both_copies(summing, out, sems, number):
    core = lax.axis_index("kind")
    return [
        pltpu.make_async_copy(summing.full, out.at[core], sems.at[number]),
        pltpu.make_async_copy(summing.peer, out.at[1 - core], sems.at[number + 1]),
    ]


def back_kernel(
    plan, plan_last, steps,
    coef, pre, step_in, scan_grad, flags, starts,
    pre_late, conv_in, normed, x, gate_back, flags_late,
    gain, gain_grad, pack, x_all, base_all, weights_all,
    early_o, late_o, kept_o, got_o,
    step_w, decay_t, skip, state_w, taps, w_conv, weight_sems,
    scan_spare, small, act_grads, coef_grads, coef_got, ext, gconv, gsmall, back, low, low_got,
    x_s, base_s, kept, sent, got, pack_last, sum_spare, sum_spare_last,
    coef_sems, low_sems, pass_sems, local_sems,
):
    pid = pl.program_id(0)
    states, rank, coefs = decay_t.shape[0], step_w.shape[0], state_w.shape[0]
    block = pre.shape[0]
    pairs = block // (2 * CHUNK)
    taps_at = coefs + small.shape[0]
    core, row = lax.axis_index("kind"), lax.axis_index("inner")
    other_core = {"kind": 1 - core}
    first_sum = Summing(plan, pack, *sum_spare)
    last_sum = Summing(plan_last, pack_last, *sum_spare_last)
    slots = first_sum.slots(pairs * steps)
    load_x = pltpu.make_async_copy(x_all, x_s, local_sems.at[0])
    load_base = pltpu.make_async_copy(base_all, base_s, local_sems.at[1])
    mine = pl.ds(pl.multiple_of(core * w_conv.shape[1], 128), w_conv.shape[1])
    load_weights = [
        pltpu.make_async_copy(source.at[:, mine], target, weight_sems.at[i])
        for i, (source, target) in enumerate(
            zip(weights_all, (step_w, decay_t, skip, state_w, taps, w_conv), strict=True)
        )
    ]

    def coef_copy(i):
        return remote(coef_grads.at[i], coef_got.at[i], coef_sems, i, other_core)

    def low_copy(i):
        here = pl.ds(pl.multiple_of((steps - 1 - i) * block, block), block)
        return remote(low.at[here], low_got.at[here], low_sems, i, other_core)

    def first_phase(number):
        first_sum.phase(number)

    @pl.when(pid == 0)
    def _():
        scan_spare[0][...] = jnp.zeros_like(scan_spare[0])
        small[...] = jnp.zeros_like(small)
        ext[block:, :] = jnp.zeros((8, ext.shape[1]), F32)
        gconv[...] = jnp.zeros_like(gconv)
        gsmall[...] = jnp.zeros_like(gsmall)
        for copy in load_weights:
            copy.start()
        first_sum.greet()
        load_x.start()
        load_base.start()
        for copy in load_weights:
            copy.wait()

    @pl.when(pid < steps)
    def _():
        def between(step_no):
            slot = pid * pairs + step_no
            for number, at in enumerate(slots):
                pl.when(slot == at)(functools.partial(first_phase, number))

        scan_back_block(
            coef, pre, step_in, scan_grad, flags, starts, step_w, decay_t, skip,
            act_grads.at[lax.rem(pid, 2)], coef_grads.at[pid], small, scan_spare, between,
        )
        coef_copy(pid).start()

    @pl.when(pid > 0)
    def _():
        late = pid - 1
        coef_copy(late).wait()
        coef_low = (coef_grads[late] + coef_got[late]).astype(BF16)
        here = pl.ds(pl.multiple_of((steps - 1 - late) * block, block), block)
        part = conv_back_block(
            coef_low, pre_late, act_grads.at[lax.rem(late, 2)], conv_in, normed, x, gate_back,
            flags_late, state_w, taps, w_conv, ext, gconv, gsmall, taps_at,
        )
        back[here, :] = part
        low[here, :] = part.astype(BF16)
        low_copy(late).start()

    @pl.when(pid == steps)
    def _():
        width = gconv.shape[0]
        small[rank : rank + states, :] = small[rank : rank + states, :] * -jnp.exp(decay_t[...])
        gsmall[coefs:taps_at, :] = small[...]
        gsmall[taps_at + 6 : taps_at + 7, :] = gain_grad[...]
        pack_last[0:width, :] = gconv[...].astype(BF16)
        pack_last[width:, :] = gsmall[...].astype(BF16)
        last_sum.phase(0)
        for i in range(steps):
            low_copy(i).wait()
        load_x.wait()
        load_base.wait()
        chosen = (1 - core).astype(F32)
        half = kept.shape[0]

        def finish(at, target):
            def part(i, unused):
                here = pl.ds(pl.multiple_of(at + i * 64, 64), 64)
                there = pl.ds(pl.multiple_of(i * 64, 64), 64)
                u = x_s[here, :].astype(F32)
                total = back[here, :] + low_got[here, :].astype(F32)
                backward = rms_back(u, rms_scale(u), gain[...], total)
                target[there, :] = (base_s[here, :] + chosen * backward).astype(target.dtype)
                return unused

            lax.fori_loop(0, half // 64, part, 0)

        finish((1 - row) * half, sent)
        pieces = last_sum.phases - 2
        passing = [
            remote(
                sent.at[pl.ds(i * (half // pieces), half // pieces)],
                got.at[pl.ds(i * (half // pieces), half // pieces)], pass_sems, i, {"inner": 1 - row},
            )
            for i in range(pieces)
        ]
        finish(row * half, kept)
        keep = pltpu.make_async_copy(kept, kept_o, local_sems.at[2])
        keep.start()
        for number in range(len(slots), first_sum.phases):
            first_sum.phase(number)
        store_first = both_copies(first_sum, early_o, local_sems, 3)
        for copy in store_first:
            copy.start()
        for number in range(1, last_sum.phases):
            last_sum.phase(number)
            if number <= pieces:
                passing[number - 1].start()
        store_last = both_copies(last_sum, late_o, local_sems, 5)
        for copy in passing:
            copy.wait()
        store_got = pltpu.make_async_copy(got, got_o, local_sems.at[7])
        store_got.start()
        for copy in store_last:
            copy.start()
        for copy in store_first + store_last + [keep, store_got]:
            copy.wait()


def assemble_kernel(
    sizes, sel, kept, got, query_key, value, mixed, out, gate, conv, small,
    results_o, in_o, out_o, query_o, key_o, value_o, mixed_o,
    state_o, step_o, decay_o, step_bias_o, skip_o, taps_o, conv_bias_o, gain_o, attn_gain_o,
):
    first = sel[1] == 0
    mine, other = kept[...], got[...].astype(F32)
    results_o[0, 0] = jnp.where(first, mine, other)
    results_o[0, 1] = jnp.where(first, other, mine)
    half = conv.shape[2]
    cut = query_key.shape[2] // 2
    for part in range(2):
        here = slice(part * cut, (part + 1) * cut)
        in_o[:, part * half : (part + 1) * half] = conv[part].astype(F32)
        in_o[:, (2 + part) * half : (3 + part) * half] = gate[part].astype(F32)
        query_o[:, here] = query_key[part, :, :cut].astype(F32)
        key_o[:, here] = query_key[part, :, cut:].astype(F32)
        value_o[0, :, here] = value[part, :, :cut].astype(F32)
        value_o[1, :, here] = value[part, :, cut:].astype(F32)
    out_o[...] = out[...].astype(F32)
    mixed_o[...] = mixed[...].astype(F32)
    both = jnp.concatenate([small[0].astype(F32), small[1].astype(F32)], axis=1)
    coefs, rank, states = sizes
    at = 0
    for target, size in (
        (state_o, coefs), (step_o, rank), (decay_o, states), (step_bias_o, 1), (skip_o, 1),
        (None, 6), (taps_o, 4), (conv_bias_o, 1),
    ):
        if target is not None:
            target[...] = both[at : at + size]
        at += size
    gain_o[...] = both[at : at + 1, :half] + both[at : at + 1, half:]
    attn_gain_o[...] = both[at + 1 : at + 2, :half]


def local(
    layer_input, output_grad, document_ids, mamba_gain, in_proj, conv_weight, conv_bias, state_proj,
    step_proj, step_bias, decay_log, skip_gain, out_proj, attn_gain, query_proj, key_proj, value_proj,
    mixed_proj,
):
    _, piece_len, width = layer_input.shape
    length = output_grad.shape[1]
    parts = lax.axis_size("kind")
    half = in_proj.shape[1] // (2 * parts)
    states = decay_log.shape[1]
    rank = step_proj.shape[0]
    coefs = state_proj.shape[1]
    head_cols = width // parts
    heads = head_cols // HEAD_DIM
    core = lax.axis_index("kind")
    row = lax.axis_index("inner")
    sel = jnp.stack([core, row]).astype(jnp.int32)
    steps = length // ROWS_STEP

    def swap(value, axis):
        return jax.tree.map(lambda v: lax.ppermute(v, axis, [(0, 1), (1, 0)]), value)

    ids = lax.dynamic_index_in_dim(document_ids, row, 0, keepdims=False)
    first = jnp.sum((ids[None, :] < ids[:, None]).astype(jnp.int32), axis=1)
    since = jnp.arange(length, dtype=jnp.int32) - first
    after = jnp.concatenate([since, jnp.zeros((4,), jnp.int32)])
    flags = jnp.stack(
        [since >= j for j in range(4)] + [after[j : j + length] >= max(j, 1) for j in range(4)],
        axis=1,
    ).astype(F32)
    first = first[None, :]
    taps = conv_weight.T
    state_t = state_proj.T
    decay_t = decay_log.T
    conv_b, step_b, skip = conv_bias[None, :], step_bias[None, :], skip_gain[None, :]
    gain_a, gain_b = mamba_gain[None, :], attn_gain[None, :]

    def rows(array):
        return (array, (ROWS_STEP, array.shape[1]), lambda i, sel: (i, 0))

    def rows_rev(array):
        return (array, (ROWS_STEP, array.shape[1]), lambda i, sel: (steps - 1 - i, 0))

    def cols(array):
        return (array, (array.shape[0], ROWS_STEP), lambda i, sel: (0, i))

    def cols_rev(array):
        return (array, (array.shape[0], ROWS_STEP), lambda i, sel: (0, steps - 1 - i))

    def full(array):
        return (array,) + whole(array.shape)

    def half_cols(array, size, shift=0):
        return (array, (array.shape[0], size), lambda i, sel: (0, sel[0] + shift))

    def half_rows(array, size):
        return (array, (size, array.shape[1]), lambda i, sel: (sel[0], 0))

    def out_rows(size, dtype):
        return ((length, size), dtype, (ROWS_STEP, size), lambda i, sel: (i, 0))

    def out_rows_rev(size, dtype):
        return ((length, size), dtype, (ROWS_STEP, size), lambda i, sel: (steps - 1 - i, 0))

    def out_whole(shape, dtype=F32):
        return (shape, dtype) + whole(shape)

    w_conv = half_cols(in_proj, half)
    w_gate = half_cols(in_proj, half, parts)
    taps_half = half_cols(taps, half)
    state_half = half_cols(state_t, half)
    step_half = half_cols(step_proj, half)
    decay_half = half_cols(decay_t, half)
    skip_half = half_cols(skip, half)
    out_half = half_rows(out_proj, half)

    small_rows = rank + states + 8
    block_f32 = pltpu.VMEM((half // 128, ROWS_STEP, 128), F32)
    plain_f32 = pltpu.VMEM((ROWS_STEP, half), F32)
    wide = CHUNK * states
    blocks = length // ROWS_STEP
    assert length // CHUNK * states == length
    row_outs = [
        (width, BF16), (width, BF16), (half, F32), (half, F32), (half, F32), None, (half, F32), (half, F32),
        (half, BF16), (half, F32), (width, BF16), (width, BF16),
    ]
    row_f32, row_low = pltpu.VMEM((length, half), F32), pltpu.VMEM((length, half), BF16)
    x_low = pltpu.VMEM((length, width), BF16)
    block_coef = (blocks, coefs, ROWS_STEP)
    front_weights = (in_proj, state_t, step_proj, decay_t, skip, taps, conv_b, step_b, out_proj)

    def pair_of_sems(count):
        return [pltpu.SemaphoreType.DMA((count,)), pltpu.SemaphoreType.DMA((count,))]

    (x, normed_a, conv_in, conv_pre, gate_z, coef, step_pre, scan_out, gated, starts, branch,
     branch_other) = pl.pallas_call(
        front_kernel,
        in_specs=[pl.BlockSpec(memory_space=pltpu.VMEM)] * 2 + [pl.BlockSpec(memory_space=pl.ANY)]
        + [(pl.BlockSpec(memory_space=pl.ANY),) * len(front_weights)],
        out_specs=[pl.BlockSpec(memory_space=pl.ANY)] * len(row_outs),
        out_shape=[
            jax.ShapeDtypeStruct(block_coef, F32) if out is None
            else jax.ShapeDtypeStruct((length, out[0]), out[1])
            for out in row_outs
        ],
        scratch_shapes=[
            x_low, x_low, pltpu.VMEM((length + 8, half), F32), row_f32, row_f32,
            pltpu.VMEM(block_coef, F32), pltpu.VMEM(block_coef, F32), pltpu.VMEM(block_coef, F32),
            row_f32, row_f32, row_low, row_f32, x_low, x_low,
            [pltpu.VMEM((width, half), BF16), pltpu.VMEM((width, half), BF16)]
            + [pltpu.VMEM((array.shape[0], half), array.dtype)
               for array in (state_t, step_proj, decay_t, skip, taps, conv_b, step_b)]
            + [pltpu.VMEM((half, width), BF16)],
            [pltpu.VMEM((states, half), F32), block_f32, block_f32, plain_f32,
             pltpu.VMEM((ROWS_STEP, wide), BF16), pltpu.VMEM((STRETCH * wide, half), BF16)],
            pltpu.SemaphoreType.DMA((11,)), pair_of_sems(2), pair_of_sems(blocks), pair_of_sems(blocks),
            pltpu.SemaphoreType.DMA((9, blocks)), pltpu.SemaphoreType.DMA((3,)),
        ],
        compiler_params=pltpu.CompilerParams(
            vmem_limit_bytes=VMEM_BYTES, collective_id=2, has_side_effects=True
        ),
        cost_estimate=pl.CostEstimate(
            flops=2 * length * states * half * 1000, bytes_accessed=1 << 24, transcendentals=0
        ),
        name="front",
    )(flags, gain_a, layer_input, front_weights)

    vmem_spec = pl.BlockSpec(memory_space=pltpu.VMEM)
    any_spec = pl.BlockSpec(memory_space=pl.ANY)
    token_head = pltpu.VMEM((heads, length, HEAD_DIM), BF16)
    token_head_f32 = pltpu.VMEM((heads, length, HEAD_DIM), F32)
    head_token = pltpu.VMEM((head_cols, length), BF16)
    scores_f32 = pltpu.VMEM((length, QUERY_BLOCK), F32)
    scores_low = pltpu.VMEM((length, QUERY_BLOCK), BF16)
    tokens_low = pltpu.VMEM((length, width), BF16)
    tokens_f32 = pltpu.VMEM((length, width), F32)
    head_low = pltpu.VMEM((length, head_cols), BF16)
    square = pltpu.VMEM((width, head_cols), BF16)
    pack_rows = width + width // 2 + head_cols + half + width
    base, scan_grad, gate_back, pack_early, g_attn_gain = pl.pallas_call(
        middle_kernel,
        in_specs=[vmem_spec] * 5 + [any_spec] * 5 + [(any_spec,) * 6],
        out_specs=[any_spec] * 4 + [vmem_spec],
        out_shape=[
            jax.ShapeDtypeStruct((length, width), F32),
            jax.ShapeDtypeStruct((length, half), F32),
            jax.ShapeDtypeStruct((length, width), F32),
            jax.ShapeDtypeStruct((pack_rows, width), BF16),
            jax.ShapeDtypeStruct((1, width), F32),
        ],
        scratch_shapes=[
            tokens_low, pltpu.VMEM((length, half), BF16), pltpu.VMEM((length, half), F32),
            pltpu.VMEM((length, half), F32), tokens_low, square, square, square,
            pltpu.VMEM((head_cols, width), BF16), pltpu.VMEM((half, width), BF16),
            pltpu.VMEM((width, half), BF16),
            tokens_low, head_token, token_head, token_head, token_head, head_token, head_token,
            token_head, head_token, head_token, token_head_f32, token_head_f32, token_head_f32,
            scores_f32, scores_f32, scores_f32, scores_low, scores_low,
            head_low, head_low, head_low, tokens_low, tokens_low, tokens_low, tokens_low, tokens_f32,
            pltpu.VMEM((length, half), F32), tokens_f32, pltpu.VMEM((half, width), F32),
            pltpu.VMEM((width, half), F32), pltpu.VMEM((pack_rows, width), BF16),
            pltpu.SemaphoreType.DMA((11,)),
            [pltpu.SemaphoreType.DMA((2 * blocks,)), pltpu.SemaphoreType.DMA((2 * blocks,))],
            pltpu.SemaphoreType.DMA((3, blocks)),
        ],
        compiler_params=pltpu.CompilerParams(
            vmem_limit_bytes=VMEM_BYTES, collective_id=3, has_side_effects=True
        ),
        cost_estimate=pl.CostEstimate(
            flops=2 * length * length * width * 10, bytes_accessed=1 << 24, transcendentals=0
        ),
        name="middle",
    )(x, branch, branch_other, first, gain_b, output_grad, gated, gate_z, scan_out, normed_a,
      (query_proj, key_proj, value_proj, mixed_proj, out_proj, in_proj))

    counts = [("inner", lax.axis_size("inner")), ("dp", lax.axis_size("dp"))]
    plan, land = sum_plan(pack_early.shape[0], counts)
    last_rows = width + 128
    plan_last, land_last = sum_plan(last_rows, counts)
    tile_f32 = pltpu.VMEM((2, half // 128, wide, 128), F32)
    tile_low = pltpu.VMEM((2, wide, half), BF16)
    own_f32 = pltpu.VMEM((ROWS_STEP, wide), F32)

    def now(i):
        return jnp.maximum(steps - 1 - i, 0)

    def late_at(i):
        return jnp.minimum(steps - i, steps - 1)

    def back_rows(array, at):
        return (array, (ROWS_STEP, array.shape[1]), lambda i: (at(i), 0))

    def fixed(array):
        return (array, array.shape, None)

    ins = [
        (coef, (None, coefs, ROWS_STEP), lambda i: (now(i), 0, 0)), back_rows(conv_pre, now), back_rows(step_pre, now),
        back_rows(scan_grad, now), back_rows(flags, now),
        (starts, (ROWS_STEP // CHUNK * states, half), lambda i: (now(i), 0)),
        back_rows(conv_pre, late_at), back_rows(conv_in, late_at), back_rows(normed_a, late_at),
        back_rows(x, late_at), back_rows(gate_back, late_at), back_rows(flags, late_at),
        fixed(gain_a), fixed(g_attn_gain), fixed(pack_early),
    ]
    weights_all = (step_proj, decay_t, skip, state_t, taps, in_proj)
    specs = [
        pl.BlockSpec(block, lambda i: (0, 0), pipeline_mode=pl.Buffered(1)) if at is None
        else pl.BlockSpec(block, at)
        for _, block, at in ins
    ]
    early, late, kept, got = pl.pallas_call(
        functools.partial(back_kernel, plan, plan_last, steps),
        grid=(steps + 1,),
        in_specs=specs + [any_spec] * 2 + [(any_spec,) * len(weights_all)],
        out_specs=[any_spec] * 4,
        out_shape=[
            jax.ShapeDtypeStruct((parts,) + pack_early.shape, BF16),
            jax.ShapeDtypeStruct((parts, last_rows, width), BF16),
            jax.ShapeDtypeStruct((piece_len, width), F32),
            jax.ShapeDtypeStruct((piece_len, width), BF16),
        ],
        scratch_shapes=[pltpu.VMEM((array.shape[0], half), array.dtype) for array in weights_all] + [
            pltpu.SemaphoreType.DMA((len(weights_all),)),
            [pltpu.VMEM((states, half), F32), block_f32,
             block_f32, block_f32, block_f32, pltpu.VMEM((ROWS_STEP, wide), BF16), plain_f32,
             plain_f32, own_f32, own_f32, tile_f32, tile_f32, tile_low, tile_low, tile_low],
            pltpu.VMEM((small_rows, half), F32),
            pltpu.VMEM((2, ROWS_STEP, half), F32),
            pltpu.VMEM((steps, coefs, ROWS_STEP), F32),
            pltpu.VMEM((steps, coefs, ROWS_STEP), F32),
            pltpu.VMEM((ROWS_STEP + 8, half), F32),
            pltpu.VMEM((width, half), F32),
            pltpu.VMEM((128, half), F32),
            pltpu.VMEM((length, width), F32),
            pltpu.VMEM((length, width), BF16),
            pltpu.VMEM((length, width), BF16),
            pltpu.VMEM((length, width), BF16),
            pltpu.VMEM((length, width), F32),
            pltpu.VMEM((piece_len, width), F32),
            pltpu.VMEM((piece_len, width), BF16),
            pltpu.VMEM((piece_len, width), BF16),
            pltpu.VMEM((last_rows, width), BF16),
            sum_scratch(plan, pack_early.shape[0], land, width),
            sum_scratch(plan_last, last_rows, land_last, width),
            [pltpu.SemaphoreType.DMA((steps,)), pltpu.SemaphoreType.DMA((steps,))],
            [pltpu.SemaphoreType.DMA((steps,)), pltpu.SemaphoreType.DMA((steps,))],
            [pltpu.SemaphoreType.DMA((16,)), pltpu.SemaphoreType.DMA((16,))],
            pltpu.SemaphoreType.DMA((8,)),
        ],
        compiler_params=pltpu.CompilerParams(
            dimension_semantics=("arbitrary",), vmem_limit_bytes=VMEM_BYTES, collective_id=1,
            has_side_effects=True,
        ),
        cost_estimate=pl.CostEstimate(
            flops=2 * length * states * half * 3000, bytes_accessed=1 << 25, transcendentals=0
        ),
        name="back",
    )(*[a for a, _, _ in ins], x, base, weights_all)
    quarter = width // 4
    eighth = width // 8

    def from_sum(total, size, first_row):
        return (total, (parts, size, width), lambda i, sel: (0, first_row // size + i, 0))

    def out_parts(size):
        return ((parts, 4 * size, width), F32, (parts, size, width), lambda i, sel: (0, i, 0))

    attn_rows = width + width // 2 + head_cols
    results, t_in, t_out, t_query, t_key, t_value, t_mixed, *smalls = call(
        functools.partial(assemble_kernel, (coefs, rank, states)), sel, 4,
        [(kept, (piece_len // 4, width), lambda i, sel: (i, 0)),
         (got, (piece_len // 4, width), lambda i, sel: (i, 0)),
         from_sum(early, quarter, 0), from_sum(early, eighth, width),
         from_sum(early, eighth, width + width // 2), from_sum(early, quarter, attn_rows),
         from_sum(early, quarter, attn_rows + half), from_sum(late, quarter, 0),
         (late, (parts, 128, width), lambda i, sel: (0, width // 128, 0))],
        [((1, 2, piece_len, width), F32, (1, 2, piece_len // 4, width), lambda i, sel: (0, 0, i, 0)),
         ((width, 4 * half), F32, (quarter, 4 * half), lambda i, sel: (i, 0)),
         out_parts(quarter), ((width, width), F32, (quarter, width), lambda i, sel: (i, 0)),
         ((width, width), F32, (quarter, width), lambda i, sel: (i, 0)), out_parts(eighth),
         out_parts(eighth)]
        + [out_whole((size, parts * half)) for size in (coefs, rank, states, 1, 1, 4, 1)]
        + [out_whole((1, width))] * 2,
        [], 0, "assemble",
    )
    t_state, t_step, t_decay, t_step_bias, t_skip, t_taps, t_conv_bias, t_gain, t_attn_gain = smalls
    return (
        results, t_gain[0], t_in, t_taps.T, t_conv_bias[0], t_state.T, t_step, t_step_bias[0],
        t_decay.T, t_skip[0], t_out.reshape(out_proj.shape), t_attn_gain[0], t_query, t_key,
        t_value.reshape(width, width), t_mixed.reshape(width, width),
    )


def solution(mesh):
    in_specs = (P("dp", "inner", None), P("dp", None, None), P("dp", None)) + (P(),) * 15
    out_specs = (P("kind", "dp", "inner", None),) + (P(),) * 15
    return jax.shard_map(local, mesh=mesh, in_specs=in_specs, out_specs=out_specs, check_vma=False)
```
